32 devices in a mesh: seq: 2 (over y), wide: 16 (over z, x, core).
Axes of the slice: x: 2, y: 2, z: 4, core: 2. Of those that a mesh axis runs over, the one named last changes fastest.
Arguments:
- tokens: bfloat16 [2, 4096, 2048], P(None, ('seq', 'wide')), may hold values from -6 to 6
- attention_weights: bfloat16 [5, 2048, 2048], P(None, 'wide'), may hold values from -0.125 to 0.125
- lowrank_down: bfloat16 [2048, 224], P('wide'), may hold values from -0.125 to 0.125
- lowrank_up: bfloat16 [224, 2048], P(None, 'wide'), may hold values from -0.75 to 0.75
- feedforward_key: bfloat16 [2048, 7168], P('wide'), may hold values from -0.125 to 0.125
- feedforward_value: bfloat16 [7168, 2048], P('wide'), may hold values from -0.0625 to 0.0625
- feedforward_receptance: bfloat16 [2048, 2048], P('wide'), may hold values from -0.125 to 0.125
- vectors: bfloat16 [16, 2048], P(None, 'wide'), may hold values from -11 to 1.61
- output_gradient: bfloat16 [2, 4096, 2048], P(None, ('seq', 'wide')), may hold values from -6 to 6
Outputs:
- block_out: bfloat16 [2, 4096, 2048], P(None, ('seq', 'wide'))
- input_grad: float32 [2, 4096, 2048], P(None, ('seq', 'wide'))
- att_weights_grad: float32 [5, 2048, 2048], P(None, 'wide')
- lora_down_grad: float32 [2048, 224], P('wide')
- lora_up_grad: float32 [224, 2048], P(None, 'wide')
- ffn_key_grad: float32 [2048, 7168], P('wide')
- ffn_value_grad: float32 [7168, 2048], P('wide')
- ffn_recept_grad: float32 [2048, 2048], P('wide')
- vectors_grad: float32 [16, 2048], P(None, 'wide')
The draws below stay inside these ranges and needn't reach their ends.
All inputs are finite; a program needn't handle non-finite values.
Results may differ from the reference program's by a relative error of at most 0.014.
Values may be sent and summed in bfloat16 or wider, within the bound.
No kernel may reach another device: no remote copies, remote signals or barrier semaphores. Data moves between devices by JAX's collectives and lax.ppermute only.
A program may use at most 768 MiB of HBM per device.

```python
import jax
import jax.numpy as jnp
from jax import lax

EMBED_BREADTH = 2048
CHANNEL_GROUPS = 32
GROUP_BREADTH = 64
FF = 7168
MIX_RANK = 32
LOWRANK_COLUMNS = 224
SEQS = 2
LEN = 4096


def draw_vectors(key, part):
    key = jax.random.fold_in(key, 11)
    divided_parts = jax.random.split(key, 7)
    gain_lo, gain_hi, bias_half, slow_share = (0.6, 1.4, 0.3, 0.5)
    scaling_coefficients = jax.random.uniform(divided_parts[0], (3, EMBED_BREADTH), jnp.float32, gain_lo, gain_hi)
    additive_shifts = jax.random.uniform(divided_parts[1], (3, EMBED_BREADTH), jnp.float32, -bias_half, bias_half)
    blend_coefficients = jax.random.uniform(divided_parts[2], (8, EMBED_BREADTH), jnp.float32, 0.0, 1.0)
    slow_heads = jax.random.uniform(divided_parts[3], (CHANNEL_GROUPS, 1), jnp.float32) < slow_share
    slow_rate = jax.random.uniform(divided_parts[4], (CHANNEL_GROUPS, GROUP_BREADTH), jnp.float32, -11.0, -9.5)
    fast_rate = jax.random.uniform(divided_parts[5], (CHANNEL_GROUPS, GROUP_BREADTH), jnp.float32, -4.5, -3.5)
    fading_entries = jnp.where(slow_heads, slow_rate, fast_rate).reshape(1, EMBED_BREADTH)
    first_reward_entries = jax.random.uniform(divided_parts[6], (1, EMBED_BREADTH), jnp.float32, -1.0, 1.0)
    return jnp.concatenate([scaling_coefficients[0:1], additive_shifts[0:1], blend_coefficients[0:6], fading_entries, first_reward_entries, scaling_coefficients[1:2], additive_shifts[1:2], scaling_coefficients[2:3], additive_shifts[2:3], blend_coefficients[6:8]], 0).astype(jnp.bfloat16)


def shard_levels(stream_key, shape, cuts, least, largest):
    gain = 1.0
    for position, blocks in cuts:
        draws = jax.random.uniform(jax.random.fold_in(jax.random.fold_in(stream_key, 6), position), (blocks,), jnp.float32, least / len(cuts), largest / len(cuts))
        gain = gain * jnp.repeat(jnp.exp(draws), shape[position] // blocks).reshape((-1,) + (1,) * (len(shape) - 1 - position))
    return gain


def centred(key, shape, scale, limit, shards=(), held_as=jnp.bfloat16):
    values = jax.random.normal(key, shape, jnp.float32) * scale
    if len(shards) > 0:
        values = shard_levels(key, shape, shards, -0.22, 0.18) * values
    return jnp.clip(values, min=-limit, max=limit).astype(held_as)


def setup_inputs(seed: int = 0) -> dict:
    arg_keys = jax.random.split(jax.random.key(seed), 10)
    tokens = centred(arg_keys[0], (SEQS, LEN, EMBED_BREADTH), 1.0, 6.0, ((1, 32),))
    attention_weights = centred(arg_keys[1], (5, EMBED_BREADTH, EMBED_BREADTH), EMBED_BREADTH ** -0.5, 0.125, ((1, 16),))
    lowrank_down = centred(arg_keys[2], (EMBED_BREADTH, LOWRANK_COLUMNS), EMBED_BREADTH ** -0.5, 0.125, ((0, 16),))
    lowrank_up = centred(arg_keys[3], (LOWRANK_COLUMNS, EMBED_BREADTH), 64 ** -0.5, 0.75, ((1, 16),))
    feedforward_key = centred(arg_keys[4], (EMBED_BREADTH, FF), EMBED_BREADTH ** -0.5, 0.125, ((0, 16),))
    feedforward_value = centred(arg_keys[5], (FF, EMBED_BREADTH), FF ** -0.5, 0.0625, ((0, 16),))
    feedforward_receptance = centred(arg_keys[6], (EMBED_BREADTH, EMBED_BREADTH), EMBED_BREADTH ** -0.5, 0.125, ((0, 16),))
    vectors = draw_vectors(jax.random.fold_in(arg_keys[9], 71), 0)
    output_gradient = centred(arg_keys[8], (SEQS, LEN, EMBED_BREADTH), 1.0, 6.0, ((1, 32),))
    return dict(tokens=tokens, attention_weights=attention_weights, lowrank_down=lowrank_down, lowrank_up=lowrank_up, feedforward_key=feedforward_key, feedforward_value=feedforward_value, feedforward_receptance=feedforward_receptance, vectors=vectors, output_gradient=output_gradient)


@jax.custom_vjp
def lowrank_hidden(v):
    return lax.optimization_barrier(v.astype(jnp.bfloat16)).astype(jnp.float32)

@jax.custom_vjp
def lowrank_backward(v):
    return v

def low_keep(v):
    return (lowrank_hidden(v), None)

def low_pass(kept, grad):
    return (grad,)

def back_keep(v):
    return (v, None)

def back_low(kept, grad):
    return (lowrank_hidden(grad),)
lowrank_hidden.defvjp(low_keep, low_pass)
lowrank_backward.defvjp(back_keep, back_low)
exact_arithmetic = lax.Precision.HIGHEST

def matrix_product(left, right):
    return jnp.dot(left, right, precision=exact_arithmetic, preferred_element_type=jnp.float32)

def layer_norm(values, gain_row, bias_row):
    mean_val = lax.optimization_barrier(jnp.mean(values, -1, keepdims=True))
    centered = values - mean_val
    spread = lax.optimization_barrier(jnp.mean(centered * centered, -1, keepdims=True))
    return centered * lax.rsqrt(spread + 1e-05) * gain_row + bias_row

def shifted(values):
    return jnp.concatenate([jnp.zeros_like(values[:1]), values[:-1]], 0)

def scaled_content_series(acceptor_entries, address_entries, content_entries, logarithmic_fading, first_reward_entries):
    length = acceptor_entries.shape[0]
    blocks = length // 64

    def token_step(memory_grid, inputs):
        acceptor_element, key_t, value_t, decay_t = inputs
        address_content_dyad = key_t[:, :, None] * value_t[:, None, :]
        layer_answer = jnp.einsum('ks,ksz->kz', acceptor_element, memory_grid + first_reward_entries[:, :, None] * address_content_dyad, precision=exact_arithmetic)
        return (jnp.exp(decay_t)[:, :, None] * memory_grid + address_content_dyad, layer_answer)

    def block_step(memory_grid, inputs):
        return lax.scan(token_step, memory_grid, inputs)
    shaped = tuple((array_in.reshape(blocks, 64, CHANNEL_GROUPS, GROUP_BREADTH) for array_in in (acceptor_entries, address_entries, content_entries, logarithmic_fading)))
    initial = jnp.zeros((CHANNEL_GROUPS, GROUP_BREADTH, GROUP_BREADTH), jnp.float32)
    final_state, outputs = lax.scan(jax.checkpoint(block_step), initial, shaped)
    return outputs.reshape(length, CHANNEL_GROUPS, GROUP_BREADTH)

def forward_block(tokens, attention_weights, lowrank_down, lowrank_up, feedforward_key, feedforward_value, feedforward_receptance, vectors):
    length = tokens.shape[0]
    mix_columns = 5 * MIX_RANK
    normed = layer_norm(tokens, vectors[0], vectors[1])
    delta_one = shifted(normed) - normed
    mix_input = lowrank_hidden(normed + delta_one * vectors[2])
    mix_hidden = lowrank_hidden(jnp.tanh(lowrank_backward(matrix_product(mix_input, lowrank_down[:, :mix_columns]))))
    mixed = []
    for position_index in range(5):
        shift_offset = lowrank_backward(matrix_product(mix_hidden[:, position_index * MIX_RANK:(position_index + 1) * MIX_RANK], lowrank_up[position_index * MIX_RANK:(position_index + 1) * MIX_RANK]))
        mixed.append(lowrank_hidden(normed + delta_one * (vectors[3 + position_index] + shift_offset)))
    decay_input, key_in, value_in, recept_in, gate_in = mixed
    acceptor_entries = lowrank_backward(matrix_product(recept_in, attention_weights[0]))
    address_entries = lowrank_backward(matrix_product(key_in, attention_weights[1]))
    content_entries = lowrank_backward(matrix_product(value_in, attention_weights[2]))
    gate_pre = lowrank_backward(matrix_product(gate_in, attention_weights[3]))
    decay_hidden = lowrank_hidden(jnp.tanh(lowrank_backward(matrix_product(decay_input, lowrank_down[:, mix_columns:]))))
    logarithmic_fading = -jnp.exp(vectors[8] + lowrank_backward(matrix_product(decay_hidden, lowrank_up[mix_columns:])))
    wkv_out = scaled_content_series(acceptor_entries.reshape(length, CHANNEL_GROUPS, GROUP_BREADTH), address_entries.reshape(length, CHANNEL_GROUPS, GROUP_BREADTH), content_entries.reshape(length, CHANNEL_GROUPS, GROUP_BREADTH), logarithmic_fading.reshape(length, CHANNEL_GROUPS, GROUP_BREADTH), vectors[9].reshape(CHANNEL_GROUPS, GROUP_BREADTH))
    mean_val = lax.optimization_barrier(jnp.mean(wkv_out, -1, keepdims=True))
    centered = wkv_out - mean_val
    spread = lax.optimization_barrier(jnp.mean(centered * centered, -1, keepdims=True))
    grouped = (centered * lax.rsqrt(spread + 0.00064)).reshape(length, -1) * vectors[10] + vectors[11]
    gated = lowrank_hidden(grouped * jax.nn.silu(gate_pre))
    first_sum = tokens + lowrank_backward(matrix_product(gated, attention_weights[4]))
    normed_two = layer_norm(first_sum, vectors[12], vectors[13])
    delta_two = shifted(normed_two) - normed_two
    key_mix = lowrank_hidden(normed_two + delta_two * vectors[14])
    recept_mix = lowrank_hidden(normed_two + delta_two * vectors[15])
    relu_part = jax.nn.relu(lowrank_backward(matrix_product(key_mix, feedforward_key)))
    squared = lowrank_hidden(relu_part * relu_part)
    value_out = lowrank_backward(matrix_product(squared, feedforward_value))
    recept_gate = jax.nn.sigmoid(lowrank_backward(matrix_product(recept_mix, feedforward_receptance)))
    return first_sum + recept_gate * value_out

def reference(tokens, attention_weights, lowrank_down, lowrank_up, feedforward_key, feedforward_value, feedforward_receptance, vectors, output_gradient):
    weight_list = (attention_weights.astype(jnp.float32), lowrank_down.astype(jnp.float32), lowrank_up.astype(jnp.float32), feedforward_key.astype(jnp.float32), feedforward_value.astype(jnp.float32), feedforward_receptance.astype(jnp.float32), vectors.astype(jnp.float32))

    def one_sequence(running, sequence_in):
        seq_tokens, seq_grad = sequence_in
        result, pullback = jax.vjp(forward_block, seq_tokens.astype(jnp.float32), weight_list[0], weight_list[1], weight_list[2], weight_list[3], weight_list[4], weight_list[5], weight_list[6])
        gradients = pullback(seq_grad.astype(jnp.float32))
        updated = tuple((before + increment for before, increment in zip(running, gradients[1:])))
        return (updated, (result.astype(jnp.bfloat16), gradients[0]))
    zero_sums = tuple((jnp.zeros_like(weight_arr) for weight_arr in weight_list))
    gradient_sums, outputs = lax.scan(one_sequence, zero_sums, (tokens, output_gradient))
    return (outputs[0], outputs[1], gradient_sums[0], gradient_sums[1], gradient_sums[2], gradient_sums[3], gradient_sums[4], gradient_sums[5], gradient_sums[6])
```

```python
import jax
import jax.numpy as jnp
from jax import lax
from jax.experimental import pallas as pl
from jax.experimental.pallas import tpu as pltpu
from jax.sharding import Mesh
from jax.sharding import PartitionSpec as P

HEADS = 32
HEAD = 64
RANK = 32
MIXCOLS = 5 * RANK
LANES = 128
F32, BF16 = jnp.float32, jnp.bfloat16
WIDE = ("z", "x", "core")
ALL = ("y", "z", "x", "core")
exact = lax.Precision.HIGHEST


def nn(a, b):
    return jnp.dot(a, b, preferred_element_type=F32)


def nt(a, b):
    return lax.dot_general(a, b, (((1,), (1,)), ((), ())), preferred_element_type=F32)


def tn(a, b):
    return lax.dot_general(a, b, (((0,), (0,)), ((), ())), preferred_element_type=F32)


def low(a):
    return a.astype(BF16)


def swap(value, axis):
    return lax.ppermute(value, axis, [(0, 1), (1, 0)])


def along(value, step):
    count = lax.axis_size(ALL)
    if step > 0:
        pairs = [(i, i + 1) for i in range(count - 1)]
    else:
        pairs = [(i + 1, i) for i in range(count - 1)]
    return lax.ppermute(value, ALL, pairs)


def piece(value, index, size, axis):
    start = [0] * value.ndim
    start[axis] = index * size
    shape = list(value.shape)
    shape[axis] = size
    return lax.dynamic_slice(value, start, shape)


def line_sum(block):
    count = lax.axis_size("z")
    place = lax.axis_index("z")

    def own(index):
        return lax.dynamic_index_in_dim(block, jnp.clip(index, 0, count - 1), 0, False).astype(F32)

    up = down = None
    for t in range(1, count):
        right = own(count - t + place)
        left = own(place + t - count)
        if up is not None:
            right = right + up.astype(F32)
            left = left + down.astype(F32)
        up = lax.ppermute(low(right), "z", [(i, i + 1) for i in range(count - 1) if i <= t - 1])
        down = lax.ppermute(
            low(left), "z", [(i, i - 1) for i in range(1, count) if count - 1 - i <= t - 1]
        )
    return own(place) + up.astype(F32) + down.astype(F32)


def x_halves(value):
    x = lax.axis_index("x")
    z = lax.axis_size("z")
    width = value.shape[1] // (2 * z)

    def take(which):
        return jnp.concatenate([piece(value, 2 * i + which, width, 1) for i in range(z)], 1)

    return take(1 - x), take(x)


def plane_sum(left_send, left_own, right):
    z = lax.axis_size("z")
    got = swap(low(tn(left_send, right)), "x")
    acc = low(tn(left_own, right) + got.astype(F32))
    return line_sum(acc.reshape(z, acc.shape[0] // z, acc.shape[1]))


def chip_grad(left, right):
    core = lax.axis_index("core")
    half = right.shape[1] // 2
    mine = piece(right, core, half, 1)
    theirs = piece(right, 1 - core, half, 1)
    left = jnp.concatenate([left, swap(left, "core")], 0)
    right = jnp.concatenate([mine, swap(theirs, "core")], 0)
    send, own = x_halves(left)
    part = plane_sum(send, own, right)
    part = part + swap(low(part), "y").astype(F32)
    rows = part.shape[0] // 2
    keep = piece(part, core, rows, 0)
    give = swap(piece(part, 1 - core, rows, 0), "core")
    first = core == 0
    return jnp.concatenate([jnp.where(first, keep, give), jnp.where(first, give, keep)], 1)


def group_rows(value):
    across = swap(value, "y")
    near = swap(value, "core")
    far = swap(across, "core")
    return jnp.concatenate([value, near, across, far], 0)


def group_sum(value):
    rows = value.shape[0] // 4
    own, near, across, far = [value[i * rows : (i + 1) * rows] for i in range(4)]
    across = across + swap(far, "core")
    got_y = swap(low(across), "y")
    own = own + swap(near, "core")
    return own + got_y.astype(F32)


def chain_kernel(decay_ref, state_ref, out_ref, *, reverse):
    count = state_ref.shape[0]

    def one(hop, held):
        b = count - 1 - hop if reverse else hop
        out_ref[b] = held
        return decay_ref[b] * held + state_ref[b]

    lax.fori_loop(0, count, one, jnp.zeros(state_ref.shape[1:], F32))


def chain(log_decay, state, reverse):
    count = lax.axis_size(ALL)
    rows = state.size // HEAD // count
    wide_rows = rows * HEAD // LANES
    pad = -rows % LANES
    logs = jnp.pad(log_decay.reshape(count, rows), ((0, 0), (0, pad))).reshape(count, -1, LANES)
    packed = jnp.concatenate([state.reshape(count, wide_rows, LANES), logs], 1)
    packed = lax.all_to_all(packed, ALL, 0, 0, tiled=True)
    logs = packed[:, wide_rows:].reshape(count, -1)[:, :rows]
    fade = jnp.repeat(jnp.exp(logs), HEAD, axis=1).reshape(count, wide_rows, LANES)
    spec = pl.BlockSpec(memory_space=pltpu.VMEM)
    entering = pl.pallas_call(
        lambda d, s, o: chain_kernel(d, s, o, reverse=reverse),
        out_shape=jax.ShapeDtypeStruct((count, wide_rows, LANES), F32),
        in_specs=[spec, spec],
        out_specs=spec,
        name="chain",
    )(fade, packed[:, :wide_rows])
    return lax.all_to_all(entering, ALL, 0, 0, tiled=True).reshape(state.shape)


def decay_sums(logs):
    inclusive = jnp.cumsum(logs, 1)
    return inclusive, inclusive - logs


def block_state(keys, values, logs):
    inclusive, _ = decay_sums(logs)
    final = inclusive[:, -1]
    weighted = keys * jnp.exp(final[:, None] - inclusive)
    return final, jnp.einsum("sthi,sthj->shij", weighted, values, precision=exact)


def wkv_local(recept, keys, values, logs, bonus, carried):
    length = recept.shape[1]
    inclusive, exclusive = decay_sums(logs)
    middle = inclusive[:, length // 2][:, None]
    query = recept * jnp.exp(exclusive - middle)
    key_side = keys * jnp.exp(middle - inclusive)
    scores = jnp.einsum("sthi,suhi->shtu", query, key_side, precision=exact)
    causal = jnp.arange(length)[:, None] > jnp.arange(length)[None, :]
    scores = jnp.where(causal, scores, 0.0)
    present = jnp.sum(recept * bonus * keys, -1)
    answer = (
        jnp.einsum("shtu,suhj->sthj", scores, values, precision=exact)
        + present[..., None] * values
    )
    answer = answer + jnp.einsum(
        "sthi,shij->sthj", recept * jnp.exp(exclusive), carried, precision=exact
    )
    final = inclusive[:, -1]
    state_out = jnp.exp(final)[..., None] * carried + jnp.einsum(
        "sthi,sthj->shij", keys * jnp.exp(final[:, None] - inclusive), values, precision=exact
    )
    return answer, state_out


def gate_norm(wkv, gate_pre, gain, bias):
    mean = jnp.mean(wkv, -1, keepdims=True)
    centered = wkv - mean
    spread = jnp.mean(centered * centered, -1, keepdims=True)
    grouped = (centered * lax.rsqrt(spread + 0.00064)).reshape(gate_pre.shape) * gain + bias
    return grouped * jax.nn.silu(gate_pre)


def norm_forward(values, gain, bias):
    mean = jnp.mean(values, -1, keepdims=True)
    centered = values - mean
    rstd = lax.rsqrt(jnp.mean(centered * centered, -1, keepdims=True) + 1e-05)
    hat = centered * rstd
    return hat * gain + bias, hat, rstd


def norm_backward(grad, hat, rstd, gain):
    d = grad * gain
    back = rstd * (
        d - jnp.mean(d, -1, keepdims=True) - hat * jnp.mean(d * hat, -1, keepdims=True)
    )
    return back, jnp.sum(grad * hat, 0), jnp.sum(grad, 0)


def prior_of(values, seqs):
    shaped = values.reshape(seqs, -1, values.shape[-1])
    incoming = along(shaped[:, -1], 1)
    return jnp.concatenate([incoming[:, None], shaped[:, :-1]], 1).reshape(values.shape)


def prior_back(grad, seqs):
    shaped = grad.reshape(seqs, -1, grad.shape[-1])
    incoming = along(shaped[:, 0], -1)
    return jnp.concatenate([shaped[:, 1:], incoming[:, None]], 1).reshape(grad.shape)


def row_gather(value):
    return lax.all_gather(value, WIDE, axis=0, tiled=True)


def body(tokens, att_w, down_w, up_w, key_w, value_w, rec_w, vectors, out_grad):
    seqs, length, width = tokens.shape
    total = seqs * length
    y, core = lax.axis_index("y"), lax.axis_index("core")
    zs = lax.axis_size("z")
    ff = key_w.shape[1]
    share = value_w.shape[0]
    half = share // 2
    quarter = ff // 4

    def heads(v):
        return v.reshape(seqs, length, HEADS, HEAD)

    def rows(v):
        return v.reshape(total, width)

    small = jnp.concatenate([up_w, down_w.T, vectors], 0)
    small = lax.all_gather(small, WIDE, axis=0)
    small = jnp.swapaxes(small, 0, 1).reshape(small.shape[1], width)
    cols = up_w.shape[0]
    up, down_t, vec = small[:cols], small[cols : 2 * cols], small[2 * cols :].astype(F32)
    w_key, w_value, w_rec, w_gate, w_out = [row_gather(att_w[i]) for i in (1, 2, 0, 3, 4)]
    key_sh = key_w.reshape(width // (4 * zs), zs, 2, 2, 2, half)
    key_sh = lax.dynamic_index_in_dim(key_sh, y, 4, False)
    key_sh = key_sh.transpose(0, 3, 2, 1, 4).reshape(-1, 2 * quarter)
    f_key = piece(row_gather(key_sh), core, quarter, 1)
    f_rec = row_gather(rec_w)
    value_sh = piece(value_w, y, half, 0)
    f_value = row_gather(value_sh).reshape(zs, 2, 2, half, width)
    f_value = lax.dynamic_index_in_dim(f_value, core, 2, False)
    f_value = jnp.swapaxes(f_value, 0, 1).reshape(quarter, width)

    x = rows(tokens.astype(F32))
    normed, hat, rstd = norm_forward(x, vec[0], vec[1])
    delta = prior_of(normed, seqs) - normed
    mix_low = low(normed + delta * vec[2])
    tanh_mix = jnp.tanh(nt(mix_low, down_t[:MIXCOLS]))
    hidden = low(tanh_mix)
    hid = [hidden[:, i * RANK : (i + 1) * RANK] for i in range(5)]
    ups = [up[i * RANK : (i + 1) * RANK] for i in range(5)]
    mixed = [low(normed + delta * (vec[3 + i] + nn(hid[i], ups[i]))) for i in range(5)]
    decay_in, key_in, value_in, rec_in, gate_in = mixed
    tanh_decay = jnp.tanh(nt(decay_in, down_t[MIXCOLS:]))
    hidden_decay = low(tanh_decay)
    logdecay = -jnp.exp(vec[8] + nn(hidden_decay, up[MIXCOLS:]))
    keys = nn(key_in, w_key)
    values = nn(value_in, w_value)
    final, state = block_state(heads(keys), heads(values), heads(logdecay))
    carried = chain(final, state, False)
    recept = nn(rec_in, w_rec)
    gate_pre = nn(gate_in, w_gate)
    wkv_pair, wkv_back = jax.vjp(
        wkv_local, heads(recept), heads(keys), heads(values), heads(logdecay),
        vec[9].reshape(HEADS, HEAD), carried,
    )
    gated, gate_back = jax.vjp(gate_norm, wkv_pair[0], gate_pre, vec[10], vec[11])
    gated = low(gated)
    first_sum = x + nn(gated, w_out)

    normed_two, hat_two, rstd_two = norm_forward(first_sum, vec[12], vec[13])
    delta_two = prior_of(normed_two, seqs) - normed_two
    key_mix = low(normed_two + delta_two * vec[14])
    rec_mix = low(normed_two + delta_two * vec[15])
    key_all = group_rows(key_mix)
    relu = jnp.maximum(nn(key_all, f_key), 0.0)
    squared = low(relu * relu)
    value_out = group_sum(nn(squared, f_value))
    rec_gate = jax.nn.sigmoid(nn(rec_mix, f_rec))
    block_out = low(first_sum + rec_gate * value_out).reshape(tokens.shape)

    g = rows(out_grad.astype(F32))
    grad_value = low(g * rec_gate)
    grad_gate_in = low(g * value_out * rec_gate * (1.0 - rec_gate))
    value_all = group_rows(grad_value)
    grad_key_pre = low(nt(value_all, f_value) * 2.0 * relu)
    g_key_mix = group_sum(nt(grad_key_pre, f_key))
    g_rec_mix = nt(grad_gate_in, f_rec)
    xi = lax.axis_index("x")
    value_part = low(
        plane_sum(piece(squared, 1 - xi, quarter // 2, 1), piece(squared, xi, quarter // 2, 1), value_all)
    )
    other = swap(value_part, "y")
    first = y == 0
    value_share = jnp.concatenate(
        [jnp.where(first, value_part, other), jnp.where(first, other, value_part)], 0
    ).astype(F32)
    send, own = x_halves(key_all)
    part = low(plane_sum(send, own, grad_key_pre))
    n = part.shape[0] // 2
    keep = piece(part, core, n, 0)
    give = swap(piece(part, 1 - core, n, 0), "core")
    first_c = core == 0
    key_part = jnp.stack([jnp.where(first_c, keep, give), jnp.where(first_c, give, keep)], 0)
    other = swap(key_part, "y")
    key_share = jnp.stack([jnp.where(first, key_part, other), jnp.where(first, other, key_part)], 0)
    key_share = key_share.reshape(2, 2, n, 2, zs, half).transpose(2, 4, 3, 1, 0, 5)
    key_share = key_share.reshape(n, ff).astype(F32)
    rec_share = chip_grad(rec_mix, grad_gate_in)

    g_prior = prior_back(g_key_mix * vec[14] + g_rec_mix * vec[15], seqs)
    g_normed_two = g_key_mix * (1.0 - vec[14]) + g_rec_mix * (1.0 - vec[15]) + g_prior
    g_maa_key = jnp.sum(g_key_mix * delta_two, 0)
    g_maa_rec = jnp.sum(g_rec_mix * delta_two, 0)
    back_two, g_gain_two, g_bias_two = norm_backward(g_normed_two, hat_two, rstd_two, vec[12])
    grad_first = g + back_two

    grad_att = low(grad_first)
    out_share = chip_grad(gated, grad_att)
    g_wkv, g_gate_pre, g_gain_x, g_bias_x = gate_back(nt(grad_att, w_out))
    exclusive = decay_sums(heads(logdecay))[1]
    state_grad = jnp.einsum(
        "sthi,sthj->shij", heads(recept) * jnp.exp(exclusive), g_wkv, precision=exact
    )
    g_state_out = chain(final, state_grad, True)
    g_rec, g_key, g_val, g_log, g_bonus, _ = wkv_back((g_wkv, g_state_out))
    g_decay = rows(g_log) * logdecay
    g_decay_low = low(g_decay)
    projs = [low(rows(g_rec)), low(rows(g_key)), low(rows(g_val)), low(g_gate_pre)]
    shares = [chip_grad(a, b) for a, b in zip((rec_in, key_in, value_in, gate_in), projs)]
    att_share = jnp.stack(shares + [out_share], 0)

    decay_up_grad = tn(hidden_decay, g_decay_low)
    g_pre_decay = low(nt(g_decay_low, up[MIXCOLS:]) * (1.0 - tanh_decay * tanh_decay))
    decay_down_grad = tn(g_pre_decay, decay_in)
    g_mixed = [
        nn(g_pre_decay, down_t[MIXCOLS:]),
        nt(projs[1], w_key),
        nt(projs[2], w_value),
        nt(projs[0], w_rec),
        nt(projs[3], w_gate),
    ]
    g_normed = g_prior_sum = None
    maa_rows, up_grads, hid_grads = [], [], []
    for i in range(5):
        offset = vec[3 + i] + nn(hid[i], ups[i])
        g_off = g_mixed[i] * delta
        maa_rows.append(jnp.sum(g_off, 0))
        off_low = low(g_off)
        up_grads.append(tn(hid[i], off_low))
        hid_grads.append(nt(off_low, ups[i]))
        here = g_mixed[i] * (1.0 - offset)
        back = g_mixed[i] * offset
        g_normed = here if g_normed is None else g_normed + here
        g_prior_sum = back if g_prior_sum is None else g_prior_sum + back
    g_pre_mix = low(jnp.concatenate(hid_grads, 1) * (1.0 - tanh_mix * tanh_mix))
    mix_down_grad = tn(g_pre_mix, mix_low)
    g_first_mix = nn(g_pre_mix, down_t[:MIXCOLS])
    maa_first = jnp.sum(g_first_mix * delta, 0)
    g_prior_sum = g_prior_sum + g_first_mix * vec[2]
    g_normed = g_normed + g_first_mix * (1.0 - vec[2]) + prior_back(g_prior_sum, seqs)
    back_one, g_gain, g_bias = norm_backward(g_normed, hat, rstd, vec[0])
    input_grad = (grad_first + back_one).reshape(tokens.shape)

    vec_rows = jnp.stack(
        [g_gain, g_bias, maa_first] + maa_rows
        + [jnp.sum(g_decay, 0), g_bonus.reshape(-1), g_gain_x, g_bias_x, g_gain_two, g_bias_two,
           g_maa_key, g_maa_rec], 0,
    )
    packed = jnp.concatenate(up_grads + [decay_up_grad, mix_down_grad, decay_down_grad, vec_rows], 0)
    packed = lax.psum_scatter(packed, WIDE, scatter_dimension=1, tiled=True)
    packed = packed + swap(packed, "y")
    return (
        block_out, input_grad, att_share, packed[cols : 2 * cols].T, packed[:cols],
        key_share, value_share, rec_share, packed[2 * cols :],
    )


def solution(mesh):
    seq, wide = mesh.devices.shape
    fine = Mesh(mesh.devices.reshape(seq, wide // 4, 2, 2), ALL)
    token = P(None, ALL, None)
    by_row, by_col, stacked = P(WIDE, None), P(None, WIDE), P(None, WIDE, None)
    return jax.shard_map(
        body,
        mesh=fine,
        in_specs=(token, stacked, by_row, by_col, by_row, by_row, by_row, by_col, token),
        out_specs=(token, token, stacked, by_row, by_col, by_row, by_row, by_row, by_col),
        check_vma=False,
    )
```

```python
import jax
import jax.numpy as jnp
from jax import lax
from jax.experimental import pallas as pl
from jax.experimental.pallas import tpu as pltpu
from jax.sharding import Mesh
from jax.sharding import PartitionSpec as P

HEAD = 64
RANK = 32
MIXCOLS = 5 * RANK
LANES = 128
F32, BF16 = jnp.float32, jnp.bfloat16
WIDE = ("z", "x", "core")
ALL = ("y", "z", "x", "core")


def nn(a, b):
    return jnp.dot(a, b, preferred_element_type=F32)


def nt(a, b):
    return lax.dot_general(a, b, (((1,), (1,)), ((), ())), preferred_element_type=F32)


def tn(a, b):
    return lax.dot_general(a, b, (((0,), (0,)), ((), ())), preferred_element_type=F32)


def low(a):
    return a.astype(BF16)


def swap(value, axis):
    return lax.ppermute(value, axis, [(0, 1), (1, 0)])


def along(value, step):
    count = lax.axis_size(ALL)
    if step > 0:
        pairs = [(i, i + 1) for i in range(count - 1)]
    else:
        pairs = [(i + 1, i) for i in range(count - 1)]
    return lax.ppermute(value, ALL, pairs)


def piece(value, index, size, axis):
    start = [0] * value.ndim
    start[axis] = index * size
    shape = list(value.shape)
    shape[axis] = size
    return lax.dynamic_slice(value, start, shape)


def line_sum(block):
    count = lax.axis_size("z")
    place = lax.axis_index("z")

    def own(index):
        return lax.dynamic_index_in_dim(block, jnp.clip(index, 0, count - 1), 0, False).astype(F32)

    up = down = None
    for t in range(1, count):
        right = own(count - t + place)
        left = own(place + t - count)
        if up is not None:
            right = right + up.astype(F32)
            left = left + down.astype(F32)
        up = lax.ppermute(low(right), "z", [(i, i + 1) for i in range(count - 1) if i <= t - 1])
        down = lax.ppermute(
            low(left), "z", [(i, i - 1) for i in range(1, count) if count - 1 - i <= t - 1]
        )
    return own(place) + up.astype(F32) + down.astype(F32)


def small_sum(value):
    z, rows = lax.axis_size("z"), value.shape[0]
    for axis in ("core", "x"):
        place = lax.axis_index(axis)
        parts = value.reshape(rows, z, 2, -1) if axis == "x" else value.reshape(rows, 2 * z, 2, -1)
        give = lax.dynamic_index_in_dim(parts, 1 - place, 2, False).reshape(rows, -1)
        keep = lax.dynamic_index_in_dim(parts, place, 2, False).reshape(rows, -1)
        value = keep + swap(give if axis == "core" else low(give), axis).astype(F32)
    value = line_sum(jnp.swapaxes(value.reshape(rows, z, -1), 0, 1))
    return value + swap(value, "y")


def quarter_cols(right):
    y, core = lax.axis_index("y"), lax.axis_index("core")
    half = right.shape[2] // 2
    near = piece(right, y, half, 2)
    across = swap(piece(right, 1 - y, half, 2), "y")
    both = jnp.concatenate([near, across], 0)
    mine = piece(both, core, half // 2, 2)
    other = swap(piece(both, 1 - core, half // 2, 2), "core")
    rows = right.shape[0]
    return jnp.concatenate([mine[:rows], other[:rows], mine[rows:], other[rows:]], 0)


def spread_cols(part):
    y, core = lax.axis_index("y"), lax.axis_index("core")
    rows = part.shape[0] // 2
    keep = piece(part, core, rows, 0)
    give = swap(piece(part, 1 - core, rows, 0), "core")
    first = core == 0
    part = jnp.stack([jnp.where(first, keep, give), jnp.where(first, give, keep)], 0)
    other = swap(part, "y")
    first = y == 0
    part = jnp.stack([jnp.where(first, part, other), jnp.where(first, other, part)], 0)
    part = part.transpose(3, 2, 0, 1, 4)
    return part.reshape(part.shape[0], rows, -1).astype(F32)


def quad_grads(lefts, rights):
    right = quarter_cols(jnp.stack(rights, 1))
    quarter = right.shape[2]
    parts = [low(tn(a, right[:, i])) for i, a in enumerate(lefts)]
    part = jnp.concatenate(parts, 1)
    part = lax.psum_scatter(part, ("z", "x"), scatter_dimension=0, tiled=True)
    return spread_cols(part.reshape(part.shape[0], len(lefts), quarter))


def group_many(values):
    value = jnp.stack(values, 0)
    near = swap(value, "core")
    across = swap(value, "y")
    far = swap(across, "core")
    return [jnp.concatenate([v[i] for v in (value, near, across, far)], 0) for i in range(len(values))]


def group_sum(value):
    rows = value.shape[0] // 4
    pair = value.reshape(2, 2, rows, -1)
    got = swap(pair[:, 1], "core")
    across = swap(low(pair[1, 0].astype(F32) + got[1].astype(F32)), "y")
    return pair[0, 0].astype(F32) + got[0].astype(F32) + across.astype(F32)


SPAN = 256
GROUP = SPAN // HEAD
SUB = 32


def lane_head(shape, dim):
    return lax.broadcasted_iota(jnp.int32, shape, dim) // HEAD


def head_block(rows, cols):
    shape = (rows, cols)
    return jnp.where(lane_head(shape, 0) == lane_head(shape, 1), 1.0, 0.0).astype(BF16)


def head_sum(value):
    coarse = low(value)
    fine = low(value - coarse.astype(F32))
    ones = head_block(SPAN, SPAN)
    return nn(coarse, ones) + nn(fine, ones)


def exact_product(left, value):
    coarse = low(value)
    rest = value - coarse.astype(F32)
    fine = low(rest)
    last = low(rest - fine.astype(F32))
    return nn(left, coarse) + (nn(left, fine) + nn(left, last))


def triangle(length, keep):
    shape = (length, length)
    row = lax.broadcasted_iota(jnp.int32, shape, 0)
    col = lax.broadcasted_iota(jnp.int32, shape, 1)
    return jnp.where(keep(row, col), 1.0, 0.0).astype(BF16)


def spread_heads(value):
    lane = lane_head(value.shape, 1)
    return jnp.concatenate([low(jnp.where(lane == h, value, 0.0)) for h in range(GROUP)], 0)


def pick_heads(value):
    rows = value.shape[0] // GROUP
    lane = lane_head((rows, SPAN), 1)
    out = value[:rows]
    for h in range(1, GROUP):
        out = jnp.where(lane == h, value[h * rows : (h + 1) * rows], out)
    return out


def widen_state(ref):
    state = jnp.concatenate([ref[0, 0], ref[0, 1]], 1)
    return jnp.concatenate(
        [jnp.where(lane_head(state.shape, 1) == h, state, jnp.zeros_like(state)) for h in range(GROUP)], 0
    )


def store_state(ref, value):
    state = low(pick_heads(value))
    ref[0, 0] = state[:, :LANES]
    ref[0, 1] = state[:, LANES:]


def exclusive_of(inclusive):
    return jnp.concatenate([jnp.zeros_like(inclusive[:1]), inclusive[:-1]], 0)


def cap(value):
    return jnp.exp(jnp.minimum(value, 80.0))


def state_kernel(key_ref, value_ref, log_ref, inc_ref, state_ref, final_ref):
    length = log_ref.shape[0]
    inclusive = exact_product(triangle(length, lambda r, c: r >= c), log_ref[...])
    inc_ref[...] = inclusive
    final = inclusive[length - 1 :]
    weighted = low(key_ref[...] * jnp.exp(final - inclusive))
    store_state(state_ref, tn(weighted, low(value_ref[...])))
    coarse = low(final)
    fine = low(final - coarse.astype(F32))
    rows = jnp.concatenate([coarse, fine, jnp.zeros((14, SPAN), BF16)], 0)
    final_ref[0, 0] = rows[:, :LANES]
    final_ref[0, 1] = rows[:, LANES:]


def sub_block(q, inclusive, exclusive, length):
    start, stop = q * SUB, (q + 1) * SUB
    middle = inclusive[start + SUB // 2 - 1 : start + SUB // 2]
    query = cap(exclusive[start:stop] - middle)
    key = cap(middle - inclusive[:stop])
    shape = (GROUP * SUB, stop)
    row = lax.rem(lax.broadcasted_iota(jnp.int32, shape, 0), SUB) + start
    mask = row > lax.broadcasted_iota(jnp.int32, shape, 1)
    return start, stop, query, key, mask


def wkv_kernel(rec_ref, key_ref, value_ref, inc_ref, state_ref, gate_ref, row_ref, wkv_ref, gated_ref):
    length = rec_ref.shape[0]
    inclusive = inc_ref[...]
    exclusive = exclusive_of(inclusive)
    rec, key, value = rec_ref[...], key_ref[...], value_ref[...]
    value_low = low(value)
    bonus, gain, bias = row_ref[9:10], row_ref[10:11], row_ref[11:12]
    answer = nn(low(rec * jnp.exp(exclusive)), widen_state(state_ref))
    answer = answer + head_sum(rec * bonus * key) * value
    parts = []
    for q in range(length // SUB):
        start, stop, query, fade, mask = sub_block(q, inclusive, exclusive, length)
        left = spread_heads(rec[start:stop] * query)
        scores = nt(left, low(key[:stop] * fade))
        scores = low(jnp.where(mask, scores, 0.0))
        parts.append(pick_heads(nn(scores, value_low[:stop])))
    answer = answer + jnp.concatenate(parts, 0)
    wkv_ref[...] = answer
    centered = answer - head_sum(answer) * (1.0 / HEAD)
    spread = head_sum(centered * centered) * (1.0 / HEAD)
    grouped = centered * lax.rsqrt(spread + 0.00064) * gain + bias
    gate = gate_ref[...]
    gated_ref[...] = low(grouped * gate / (1.0 + jnp.exp(-gate)))


def gate_back_kernel(grad_ref, wkv_ref, gate_ref, rec_ref, inc_ref, row_ref, gwkv_ref, ggate_ref, state_ref, sum_ref):
    gain, bias = row_ref[10:11], row_ref[11:12]
    answer, gate, grad = wkv_ref[...], gate_ref[...], grad_ref[...]
    centered = answer - head_sum(answer) * (1.0 / HEAD)
    rstd = lax.rsqrt(head_sum(centered * centered) * (1.0 / HEAD) + 0.00064)
    hat = centered * rstd
    grouped = hat * gain + bias
    sig = 1.0 / (1.0 + jnp.exp(-gate))
    g_grouped = grad * gate * sig
    ggate_ref[...] = low(grad * grouped * sig * (1.0 + gate * (1.0 - sig)))
    g_gain = jnp.sum(g_grouped * hat, 0, keepdims=True)
    g_bias = jnp.sum(g_grouped, 0, keepdims=True)
    sum_ref[0] = jnp.concatenate([g_gain, g_bias, jnp.zeros((6, SPAN), F32)], 0)
    g_hat = g_grouped * gain
    back = rstd * (
        g_hat - head_sum(g_hat) * (1.0 / HEAD) - hat * (head_sum(g_hat * hat) * (1.0 / HEAD))
    )
    back = low(back)
    gwkv_ref[...] = back
    query = low(rec_ref[...] * jnp.exp(exclusive_of(inc_ref[...])))
    store_state(state_ref, tn(query, back))


def wkv_back_kernel(
    rec_ref, key_ref, value_ref, inc_ref, log_ref, state_ref, gstate_ref, gwkv_ref, row_ref,
    grec_ref, gkey_ref, gvalue_ref, gdecay_ref, sum_ref, key_acc, value_acc, pair_acc,
):
    length = rec_ref.shape[0]
    inclusive = inc_ref[...]
    exclusive = exclusive_of(inclusive)
    final = inclusive[length - 1 :]
    rec, key, value = rec_ref[...], key_ref[...], value_ref[...]
    value_low = low(value)
    grad_low = gwkv_ref[...]
    grad = grad_low.astype(F32)
    bonus = row_ref[9:10]
    state, gstate = widen_state(state_ref), widen_state(gstate_ref)
    pair = head_sum(grad * value)
    shared = pair * bonus
    g_key = shared * rec
    g_value = head_sum(rec * bonus * key) * grad
    g_bonus = jnp.sum(rec * key * pair, 0, keepdims=True)
    fade = jnp.exp(exclusive)
    back = nt(grad_low, state)
    from_state = low(rec * fade).astype(F32) * back
    g_rec = shared * key + fade * back
    fade = jnp.exp(final - inclusive)
    weighted = low(key * fade)
    back = nt(value_low, gstate)
    to_state = weighted.astype(F32) * back
    key_acc[...] = g_key + fade * back
    value_acc[...] = g_value + nn(weighted, gstate)
    pair_acc[...] = jnp.zeros_like(pair_acc)
    rec_parts, own_parts = [], []
    for q in range(length // SUB):
        start, stop, query, fade, mask = sub_block(q, inclusive, exclusive, length)
        left = rec[start:stop] * query
        spread = spread_heads(left)
        right = low(key[:stop] * fade)
        gspread = spread_heads(grad[start:stop])
        scores = low(jnp.where(mask, nt(spread, right), 0.0))
        weight = low(jnp.where(mask, nt(gspread, value_low[:stop]), 0.0))
        back = pick_heads(nn(weight, right))
        rec_parts.append(g_rec[start:stop] + query * back)
        own_parts.append(low(left).astype(F32) * back)
        back = tn(weight, spread)
        key_acc[:stop] += fade * back
        pair_acc[:stop] += right.astype(F32) * back
        value_acc[:stop] += tn(scores, gspread)
    grec_ref[...] = low(jnp.concatenate(rec_parts, 0))
    gkey_ref[...] = low(key_acc[...])
    gvalue_ref[...] = low(value_acc[...])
    inner, pairs = jnp.concatenate(own_parts, 0), pair_acc[...]
    both = head_sum(
        jnp.concatenate([state_ref[0, 0], state_ref[0, 1]], 1).astype(F32)
        * jnp.concatenate([gstate_ref[0, 0], gstate_ref[0, 1]], 1).astype(F32)
    )
    shape = both.shape
    here = lax.rem(lax.broadcasted_iota(jnp.int32, shape, 1), HEAD) == lax.broadcasted_iota(
        jnp.int32, shape, 0
    )
    through = jnp.exp(final) * jnp.sum(jnp.where(here, both, 0.0), 0, keepdims=True)
    later = exact_product(triangle(length, lambda r, c: r < c), inner + from_state - pairs)
    earlier = exact_product(triangle(length, lambda r, c: r > c), to_state)
    g_log = later - pairs + earlier + through
    g_decay = g_log * log_ref[...]
    gdecay_ref[...] = low(g_decay)
    sum_ref[0] = jnp.concatenate(
        [g_bonus, jnp.sum(g_decay, 0, keepdims=True), jnp.zeros((6, SPAN), F32)], 0
    )


def wkv_call(kernel, seqs, ins, outs, name, flops, scratch=()):
    width = ins[0].shape[1]
    length = ins[0].shape[0] // seqs

    def spec(a):
        if len(a.shape) == 4:
            return pl.BlockSpec((1, 2, a.shape[2], LANES), lambda s, g: (s, g, 0, 0))
        if len(a.shape) == 3:
            return pl.BlockSpec((1, 8, SPAN), lambda s, g: (s, 0, g))
        if a.shape[0] == 16:
            return pl.BlockSpec((16, SPAN), lambda s, g: (0, g))
        return pl.BlockSpec((length, SPAN), lambda s, g: (s, g))

    moved = sum(a.size * a.dtype.itemsize for a in ins + outs)
    return pl.pallas_call(
        kernel,
        grid=(seqs, width // SPAN),
        in_specs=[spec(a) for a in ins],
        out_specs=[spec(a) for a in outs],
        out_shape=outs,
        scratch_shapes=scratch,
        compiler_params=pltpu.CompilerParams(vmem_limit_bytes=40 << 20),
        cost_estimate=pl.CostEstimate(flops=flops, transcendentals=0, bytes_accessed=moved),
        name=name,
    )(*ins)


def chain_kernel(first_ref, packed_ref, out_ref, held_fade, *, rows, reverse):
    count = packed_ref.shape[0]
    logs = packed_ref[:, rows : rows + 1], packed_ref[:, rows + 1 : rows + 2]
    shape = (count, rows, LANES)
    lane = lax.rem(lax.broadcasted_iota(jnp.int32, shape, 2), HEAD)
    here = lane == lax.broadcasted_iota(jnp.int32, shape, 1) + first_ref[0]
    ones = head_block(LANES, LANES)
    total = None
    for part in logs:
        part = jnp.where(here, part.astype(F32), 0.0)
        part = nn(low(part.reshape(count * rows, LANES)), ones)
        total = part if total is None else total + part
    held_fade[...] = jnp.exp(total).reshape(shape)

    def one(hop, held):
        b = count - 1 - hop if reverse else hop
        out_ref[b] = low(held)
        return held_fade[b] * held + packed_ref[b, :rows].astype(F32)

    lax.fori_loop(0, count, one, jnp.zeros((rows, LANES), F32))


def chain(state, finals, reverse):
    count = lax.axis_size(ALL)
    pairs = state.shape[0] * state.shape[1]
    split = count // pairs
    rows = state.shape[2] // split
    logs = finals.reshape(pairs, finals.shape[2], LANES)
    if split > 1:
        logs = jnp.repeat(logs, split, axis=0)
    packed = jnp.concatenate([state.reshape(count, rows, LANES), logs], 1)
    packed = lax.all_to_all(packed, ALL, 0, 0, tiled=True)
    first = lax.rem(lax.axis_index(ALL), split) * rows
    entering = pl.pallas_call(
        lambda *refs: chain_kernel(*refs, rows=rows, reverse=reverse),
        grid_spec=pltpu.PrefetchScalarGridSpec(
            num_scalar_prefetch=1,
            grid=(1,),
            in_specs=[pl.BlockSpec(packed.shape, lambda i, c: (0, 0, 0))],
            out_specs=pl.BlockSpec((count, rows, LANES), lambda i, c: (0, 0, 0)),
            scratch_shapes=[pltpu.VMEM((count, rows, LANES), F32)],
        ),
        out_shape=jax.ShapeDtypeStruct((count, rows, LANES), BF16),
        compiler_params=pltpu.CompilerParams(vmem_limit_bytes=40 << 20),
        name="chain",
    )(first.astype(jnp.int32).reshape(1), packed)
    return lax.all_to_all(entering, ALL, 0, 0, tiled=True).reshape(state.shape)


def norm_forward(values, gain, bias):
    mean = jnp.mean(values, -1, keepdims=True)
    centered = values - mean
    rstd = lax.rsqrt(jnp.mean(centered * centered, -1, keepdims=True) + 1e-05)
    hat = centered * rstd
    return hat * gain + bias, hat, rstd


def norm_backward(grad, hat, rstd, gain):
    d = grad * gain
    back = rstd * (
        d - jnp.mean(d, -1, keepdims=True) - hat * jnp.mean(d * hat, -1, keepdims=True)
    )
    return back, jnp.sum(grad * hat, 0), jnp.sum(grad, 0)


def prior_of(values, seqs):
    shaped = values.reshape(seqs, -1, values.shape[-1])
    incoming = along(shaped[:, -1], 1)
    return jnp.concatenate([incoming[:, None], shaped[:, :-1]], 1).reshape(values.shape)


def prior_back(grad, seqs):
    shaped = grad.reshape(seqs, -1, grad.shape[-1])
    incoming = along(shaped[:, 0], -1)
    return jnp.concatenate([shaped[:, 1:], incoming[:, None]], 1).reshape(grad.shape)


def stack_nn(value, shards, which, tile=512):
    devices, _, rows, cols = shards.shape

    def kernel(a_ref, w_ref, o_ref):
        w = w_ref[...].reshape(devices * rows, tile)
        o_ref[...] = jnp.dot(a_ref[...], w, preferred_element_type=F32)

    return pl.pallas_call(
        kernel,
        grid=(cols // tile,),
        out_shape=jax.ShapeDtypeStruct((value.shape[0], cols), F32),
        in_specs=[
            pl.BlockSpec(value.shape, lambda j: (0, 0)),
            pl.BlockSpec((devices, 1, rows, tile), lambda j: (0, which, 0, j)),
        ],
        out_specs=pl.BlockSpec((value.shape[0], tile), lambda j: (0, j)),
        compiler_params=pltpu.CompilerParams(vmem_limit_bytes=40 << 20),
        cost_estimate=pl.CostEstimate(
            flops=2 * value.size * cols, transcendentals=0,
            bytes_accessed=2 * value.size + 2 * devices * rows * cols + 4 * value.shape[0] * cols,
        ),
        name="stack_nn",
    )(value, shards)


def stack_nt(value, shards, which, tile=512):
    devices, _, rows, cols = shards.shape
    group = tile // rows

    def kernel(a_ref, w_ref, o_ref):
        w = w_ref[...].reshape(tile, cols)
        o_ref[...] = lax.dot_general(
            a_ref[...], w, (((1,), (1,)), ((), ())), preferred_element_type=F32
        )

    return pl.pallas_call(
        kernel,
        grid=(devices // group,),
        out_shape=jax.ShapeDtypeStruct((value.shape[0], devices * rows), F32),
        in_specs=[
            pl.BlockSpec(value.shape, lambda j: (0, 0)),
            pl.BlockSpec((group, 1, rows, cols), lambda j: (j, which, 0, 0)),
        ],
        out_specs=pl.BlockSpec((value.shape[0], tile), lambda j: (0, j)),
        compiler_params=pltpu.CompilerParams(vmem_limit_bytes=40 << 20),
        cost_estimate=pl.CostEstimate(
            flops=2 * value.size * devices * rows, transcendentals=0,
            bytes_accessed=2 * value.size + 2 * devices * rows * cols
            + 4 * value.shape[0] * devices * rows,
        ),
        name="stack_nt",
    )(value, shards)


TILE = 256


def pack_blocks(shard):
    rows, cols = shard.shape
    return jnp.swapaxes(shard.reshape(rows, cols // TILE, TILE), 0, 1).reshape(-1, TILE)


def ffn_call(kernel, core, grid, ins, specs, outs, out_specs, flops, scratch=(), name=None):
    moved = sum(a.size * a.dtype.itemsize for a in ins[:1] + outs) + flops // 1024
    return pl.pallas_call(
        kernel,
        grid_spec=pltpu.PrefetchScalarGridSpec(
            num_scalar_prefetch=1, grid=grid, in_specs=specs, out_specs=out_specs, scratch_shapes=scratch
        ),
        out_shape=outs,
        compiler_params=pltpu.CompilerParams(vmem_limit_bytes=56 << 20),
        cost_estimate=pl.CostEstimate(flops=flops, transcendentals=0, bytes_accessed=moved),
        name=name,
    )(core.reshape(1), *ins)


class PackedWeights:
    def __init__(self, packed, core, ff, width, half, chips):
        self.packed, self.core = packed, core
        self.devices = packed.shape[0]
        self.rows = width // self.devices
        self.quarter, self.width, self.half, self.chips = ff // 4, width, half, chips
        self.blocks = self.quarter // TILE
        self.fast = half % 16 == 0 and self.rows % 16 == 0 and self.rows == 128

    def _plain(self, start, rows, count):
        part = self.packed[:, start : start + rows * count]
        return part.reshape(-1, count, rows, TILE)

    def plain_key(self):
        start = self.half * (self.width // TILE)
        part = self._plain(start, self.rows, 2 * self.blocks)
        part = piece(part, self.core, self.blocks, 1)
        return jnp.swapaxes(part, 1, 2).reshape(self.width, self.quarter)

    def plain_value(self):
        part = self._plain(0, self.half, self.width // TILE)
        part = lax.dynamic_index_in_dim(
            part.reshape(self.chips, 2, *part.shape[1:]), self.core, 1, False
        )
        return jnp.swapaxes(part, 1, 2).reshape(self.quarter, self.width)

    def plain_rec(self):
        start = self.half * (self.width // TILE) + self.rows * 2 * self.blocks
        part = self._plain(start, self.rows, self.width // TILE)
        return jnp.swapaxes(part, 1, 2).reshape(self.width, self.width)

    def key_forward(self, mix):
        if not self.fast:
            relu = low(jnp.maximum(nn(mix, self.plain_key()), 0.0))
            return relu, low(relu.astype(F32) * relu.astype(F32))
        tokens = mix.shape[0]
        first = self.half * (self.width // TILE) // self.rows

        def kernel(c_ref, a_ref, w_ref, relu_ref, sq_ref):
            w = w_ref[...].reshape(self.width, TILE)
            relu = jnp.maximum(jnp.dot(a_ref[...], w, preferred_element_type=F32), 0.0)
            relu_ref[...] = low(relu)
            sq_ref[...] = low(relu * relu)

        out = jax.ShapeDtypeStruct((tokens, self.quarter), BF16)
        spec = pl.BlockSpec((tokens, TILE), lambda n, c: (0, n))
        return ffn_call(
            kernel, self.core, (self.blocks,), [mix, self.packed],
            [pl.BlockSpec(mix.shape, lambda n, c: (0, 0)),
             pl.BlockSpec((self.devices, self.rows, TILE),
                          lambda n, c: (0, first + c[0] * self.blocks + n, 0))],
            [out, out], [spec, spec], 2 * mix.size * self.quarter, name="key_forward",
        )

    def value_forward(self, squared):
        if not self.fast:
            return low(nn(squared, self.plain_value()))
        tokens = squared.shape[0]
        view = self.packed.reshape(self.chips, 2, *self.packed.shape[1:])

        def kernel(c_ref, a_ref, w_ref, o_ref):
            w = w_ref[...].reshape(self.quarter, TILE)
            o_ref[...] = low(jnp.dot(a_ref[...], w, preferred_element_type=F32))

        return ffn_call(
            kernel, self.core, (self.width // TILE,), [squared, view],
            [pl.BlockSpec(squared.shape, lambda m, c: (0, 0)),
             pl.BlockSpec((self.chips, 1, self.half, TILE), lambda m, c: (0, c[0], m, 0))],
            [jax.ShapeDtypeStruct((tokens, self.width), BF16)],
            [pl.BlockSpec((tokens, TILE), lambda m, c: (0, m))],
            2 * squared.size * self.width, name="value_forward",
        )[0]

    def rec_forward(self, mix):
        if not self.fast:
            return jax.nn.sigmoid(nn(mix, self.plain_rec()))
        tokens = mix.shape[0]
        first = self.packed.shape[1] // self.rows - self.width // TILE

        def kernel(c_ref, a_ref, w_ref, o_ref):
            w = w_ref[...].reshape(self.width, TILE)
            o_ref[...] = jax.nn.sigmoid(jnp.dot(a_ref[...], w, preferred_element_type=F32))

        return ffn_call(
            kernel, self.core, (self.width // TILE,), [mix, self.packed],
            [pl.BlockSpec(mix.shape, lambda m, c: (0, 0)),
             pl.BlockSpec((self.devices, self.rows, TILE), lambda m, c: (0, first + m, 0))],
            [jax.ShapeDtypeStruct((tokens, self.width), F32)],
            [pl.BlockSpec((tokens, TILE), lambda m, c: (0, m))],
            2 * mix.size * self.width, name="rec_forward",
        )[0]

    def value_backward(self, grad, relu):
        if not self.fast:
            return low(nt(grad, self.plain_value()) * 2.0 * relu.astype(F32))
        tokens = grad.shape[0]
        view = self.packed.reshape(self.chips, 2, *self.packed.shape[1:])
        count = self.width // TILE
        part = self.chips // 2

        def kernel(c_ref, a_ref, r_ref, w_ref, o_ref, flat):
            w = w_ref[...].reshape(part, count, self.half, TILE)
            for m in range(count):
                flat[:, m * TILE : (m + 1) * TILE] = w[:, m].reshape(part * self.half, TILE)
            back = lax.dot_general(
                a_ref[...], flat[...], (((1,), (1,)), ((), ())), preferred_element_type=F32
            )
            o_ref[...] = low(back * 2.0 * r_ref[...].astype(F32))

        wide = part * self.half
        return ffn_call(
            kernel, self.core, (2,), [grad, relu, view],
            [pl.BlockSpec(grad.shape, lambda i, c: (0, 0)),
             pl.BlockSpec((tokens, wide), lambda i, c: (0, i)),
             pl.BlockSpec((part, 1, count * self.half, TILE), lambda i, c: (i, c[0], 0, 0))],
            [jax.ShapeDtypeStruct((tokens, self.quarter), BF16)],
            [pl.BlockSpec((tokens, wide), lambda i, c: (0, i))],
            2 * grad.size * self.quarter,
            scratch=(pltpu.VMEM((wide, self.width), BF16),), name="value_backward",
        )[0]

    def key_backward(self, grad):
        if not self.fast:
            return low(nt(grad, self.plain_key()))
        tokens = grad.shape[0]
        part = 4
        rows = self.blocks * self.rows
        first = self.half * (self.width // TILE) // rows

        def kernel(c_ref, a_ref, w_ref, o_ref, flat):
            w = w_ref[...].reshape(part, self.blocks, self.rows, TILE)
            for n in range(self.blocks):
                flat[:, n * TILE : (n + 1) * TILE] = w[:, n].reshape(part * self.rows, TILE)
            o_ref[...] = low(lax.dot_general(
                a_ref[...], flat[...], (((1,), (1,)), ((), ())), preferred_element_type=F32
            ))

        wide = part * self.rows
        return ffn_call(
            kernel, self.core, (self.devices // part,), [grad, self.packed],
            [pl.BlockSpec(grad.shape, lambda i, c: (0, 0)),
             pl.BlockSpec((part, rows, TILE), lambda i, c: (i, first + c[0], 0))],
            [jax.ShapeDtypeStruct((tokens, self.width), BF16)],
            [pl.BlockSpec((tokens, wide), lambda i, c: (0, i))],
            2 * grad.size * self.width,
            scratch=(pltpu.VMEM((wide, self.quarter), BF16),), name="key_backward",
        )[0]

    def rec_backward(self, grad):
        if not self.fast:
            return nt(grad, self.plain_rec())
        tokens = grad.shape[0]
        part, count = 4, self.width // TILE
        rows = count * self.rows // 2
        first = self.packed.shape[1] // rows - 2

        def kernel(c_ref, a_ref, w_ref, v_ref, o_ref, flat):
            for k, ref in enumerate((w_ref, v_ref)):
                w = ref[...].reshape(part, count // 2, self.rows, TILE)
                for n in range(count // 2):
                    m = k * (count // 2) + n
                    flat[:, m * TILE : (m + 1) * TILE] = w[:, n].reshape(part * self.rows, TILE)
            o_ref[...] = lax.dot_general(
                a_ref[...], flat[...], (((1,), (1,)), ((), ())), preferred_element_type=F32
            )

        wide = part * self.rows
        return ffn_call(
            kernel, self.core, (self.devices // part,), [grad, self.packed, self.packed],
            [pl.BlockSpec(grad.shape, lambda i, c: (0, 0)),
             pl.BlockSpec((part, rows, TILE), lambda i, c: (i, first, 0)),
             pl.BlockSpec((part, rows, TILE), lambda i, c: (i, first + 1, 0))],
            [jax.ShapeDtypeStruct((tokens, self.width), F32)],
            [pl.BlockSpec((tokens, wide), lambda i, c: (0, i))],
            2 * grad.size * self.width,
            scratch=(pltpu.VMEM((wide, self.width), BF16),), name="rec_backward",
        )[0]


def body(tokens, att_w, down_w, up_w, key_w, value_w, rec_w, vectors, out_grad):
    seqs, length, width = tokens.shape
    total = seqs * length
    y, core = lax.axis_index("y"), lax.axis_index("core")
    zs = lax.axis_size("z")
    ff = key_w.shape[1]
    share = value_w.shape[0]
    half = share // 2
    quarter = ff // 4

    def rows(v):
        return v.reshape(total, width)

    def columns(shard):
        gathered = lax.all_gather(shard, WIDE, axis=0)
        return jnp.swapaxes(gathered, 0, 1).reshape(shard.shape[0], width)

    cols = up_w.shape[0]
    up_vec = columns(jnp.concatenate([vectors, up_w], 0))
    vec, up = up_vec[:16].astype(F32), up_vec[16:]
    down_t = columns(down_w.T)
    w_rkv = lax.all_gather(att_w[:3], WIDE, axis=0)
    w_go = lax.all_gather(att_w[3:], WIDE, axis=0)
    key_sh = key_w.reshape(-1, zs, 2, 2, 2, half)
    key_sh = lax.dynamic_index_in_dim(key_sh, y, 4, False)
    key_sh = key_sh.transpose(0, 3, 1, 2, 4).reshape(-1, 2 * quarter)
    packed = jnp.concatenate(
        [pack_blocks(piece(value_w, y, half, 0)), pack_blocks(key_sh), pack_blocks(rec_w)], 0
    )
    packed = lax.all_gather(packed, WIDE, axis=0)

    x = rows(tokens.astype(F32))
    normed, hat, rstd = norm_forward(x, vec[0], vec[1])
    delta = prior_of(normed, seqs) - normed
    mix_low = low(normed + delta * vec[2])
    tanh_mix = jnp.tanh(nt(mix_low, down_t[:MIXCOLS]))
    hidden = low(tanh_mix)
    hid = [hidden[:, i * RANK : (i + 1) * RANK] for i in range(5)]
    ups = [up[i * RANK : (i + 1) * RANK] for i in range(5)]
    mixed = [low(normed + delta * (vec[3 + i] + nn(hid[i], ups[i]))) for i in range(5)]
    decay_in, key_in, value_in, rec_in, gate_in = mixed
    tanh_decay = jnp.tanh(nt(decay_in, down_t[MIXCOLS:]))
    hidden_decay = low(tanh_decay)
    logdecay = -jnp.exp(vec[8] + nn(hidden_decay, up[MIXCOLS:]))
    keys = stack_nn(key_in, w_rkv, 1)
    values = stack_nn(value_in, w_rkv, 2)
    shaped = jax.ShapeDtypeStruct
    flat, flat_low = shaped((total, width), F32), shaped((total, width), BF16)
    states = shaped((seqs, width // LANES, HEAD, LANES), BF16)
    finals = shaped((seqs, width // LANES, 16, LANES), BF16)
    sums = shaped((seqs, 8, width), F32)
    unit = 2 * total * width
    inclusive, state, final = wkv_call(
        state_kernel, seqs, [keys, values, logdecay], [flat, states, finals], "wkv_state", unit * 512
    )
    carried = chain(state, final, False)
    recept = stack_nn(rec_in, w_rkv, 0)
    gate_pre = stack_nn(gate_in, w_go, 0)
    wkv, gated = wkv_call(
        wkv_kernel, seqs, [recept, keys, values, inclusive, carried, gate_pre, vec], [flat, flat_low],
        "wkv_forward", unit * 1536,
    )
    first_sum = x + stack_nn(gated, w_go, 1)

    normed_two, hat_two, rstd_two = norm_forward(first_sum, vec[12], vec[13])
    delta_two = prior_of(normed_two, seqs) - normed_two
    key_mix = low(normed_two + delta_two * vec[14])
    rec_mix = low(normed_two + delta_two * vec[15])
    key_all, rec_all = group_many([key_mix, rec_mix])
    gated_all = group_many([gated])[0]
    mix_all = group_many([rec_in, key_in, value_in, gate_in])
    packed, key_all, rec_all, gated_all, mix_all = lax.optimization_barrier(
        (packed, key_all, rec_all, gated_all, mix_all)
    )
    ffn = PackedWeights(packed, core, ff, width, half, 2 * zs)
    relu, squared = ffn.key_forward(key_all)
    value_out = group_sum(ffn.value_forward(squared))
    rec_gate = ffn.rec_forward(rec_mix)
    block_out = low(first_sum + rec_gate * value_out).reshape(tokens.shape)

    g = rows(out_grad.astype(F32))
    grad_value = low(g * rec_gate)
    grad_gate_in = low(g * value_out * rec_gate * (1.0 - rec_gate))
    value_all = group_many([grad_value])[0]
    grad_key_pre = ffn.value_backward(value_all, relu)
    g_key_mix = group_sum(ffn.key_backward(grad_key_pre))
    g_rec_mix = ffn.rec_backward(grad_gate_in)
    value_part = low(tn(squared, value_all)).reshape(-1, half, width)
    value_part = lax.psum_scatter(value_part, ("z", "x"), scatter_dimension=0, tiled=True)[0]
    other = swap(value_part, "y")
    first = y == 0
    value_share = jnp.concatenate(
        [jnp.where(first, value_part, other), jnp.where(first, other, value_part)], 0
    ).astype(F32)
    part = low(tn(key_all, grad_key_pre))
    part = lax.psum_scatter(part, ("z", "x"), scatter_dimension=0, tiled=True)
    key_share = spread_cols(part[:, None])[0].reshape(-1, 2, 2, zs, 2, half)
    key_share = key_share.transpose(0, 3, 4, 2, 1, 5).reshape(-1, ff)

    g_prior = prior_back(g_key_mix * vec[14] + g_rec_mix * vec[15], seqs)
    g_normed_two = g_key_mix * (1.0 - vec[14]) + g_rec_mix * (1.0 - vec[15]) + g_prior
    g_maa_key = jnp.sum(g_key_mix * delta_two, 0)
    g_maa_rec = jnp.sum(g_rec_mix * delta_two, 0)
    back_two, g_gain_two, g_bias_two = norm_backward(g_normed_two, hat_two, rstd_two, vec[12])
    grad_first = g + back_two

    grad_att = low(grad_first)
    g_wkv, g_gate_low, g_state, gate_sums = wkv_call(
        gate_back_kernel, seqs,
        [stack_nt(grad_att, w_go, 1), wkv, gate_pre, recept, inclusive, vec],
        [flat_low, flat_low, states, sums], "gate_backward", unit * 1536,
    )
    g_state_out = chain(g_state, final, True)
    g_rec, g_key, g_val, g_decay_low, wkv_sums = wkv_call(
        wkv_back_kernel, seqs,
        [recept, keys, values, inclusive, logdecay, carried, g_state_out, g_wkv, vec],
        [flat_low, flat_low, flat_low, flat_low, sums], "wkv_backward", unit * 4096,
        scratch=[pltpu.VMEM((length, SPAN), F32)] * 3,
    )
    gate_sums, wkv_sums = jnp.sum(gate_sums, 0), jnp.sum(wkv_sums, 0)
    projs = [g_rec, g_key, g_val, g_gate_low]
    early = quad_grads([rec_all, gated_all, mix_all[3]], [grad_gate_in, grad_att, projs[3]])
    late = quad_grads(mix_all[:3], projs[:3])
    rec_share = early[0]
    att_share = jnp.concatenate([late, early[2:], early[1:2]], 0)

    decay_up_grad = tn(hidden_decay, g_decay_low)
    g_pre_decay = low(nt(g_decay_low, up[MIXCOLS:]) * (1.0 - tanh_decay * tanh_decay))
    decay_down_grad = tn(g_pre_decay, decay_in)
    g_mixed = [
        nn(g_pre_decay, down_t[MIXCOLS:]),
        stack_nt(projs[1], w_rkv, 1),
        stack_nt(projs[2], w_rkv, 2),
        stack_nt(projs[0], w_rkv, 0),
        stack_nt(projs[3], w_go, 0),
    ]
    g_normed = g_prior_sum = None
    maa_rows, up_grads, hid_grads = [], [], []
    for i in range(5):
        offset = vec[3 + i] + nn(hid[i], ups[i])
        g_off = g_mixed[i] * delta
        maa_rows.append(jnp.sum(g_off, 0))
        off_low = low(g_off)
        up_grads.append(tn(hid[i], off_low))
        hid_grads.append(nt(off_low, ups[i]))
        here = g_mixed[i] * (1.0 - offset)
        back = g_mixed[i] * offset
        g_normed = here if g_normed is None else g_normed + here
        g_prior_sum = back if g_prior_sum is None else g_prior_sum + back
    g_pre_mix = low(jnp.concatenate(hid_grads, 1) * (1.0 - tanh_mix * tanh_mix))
    mix_down_grad = tn(g_pre_mix, mix_low)
    g_first_mix = nn(g_pre_mix, down_t[:MIXCOLS])
    maa_first = jnp.sum(g_first_mix * delta, 0)
    g_prior_sum = g_prior_sum + g_first_mix * vec[2]
    g_normed = g_normed + g_first_mix * (1.0 - vec[2]) + prior_back(g_prior_sum, seqs)
    back_one, g_gain, g_bias = norm_backward(g_normed, hat, rstd, vec[0])
    input_grad = (grad_first + back_one).reshape(tokens.shape)

    vec_rows = jnp.stack(
        [g_gain, g_bias, maa_first] + maa_rows
        + [wkv_sums[1], wkv_sums[0], gate_sums[0], gate_sums[1], g_gain_two, g_bias_two,
           g_maa_key, g_maa_rec], 0,
    )
    packed = jnp.concatenate(up_grads + [decay_up_grad, mix_down_grad, decay_down_grad, vec_rows], 0)
    packed = small_sum(packed)
    return (
        block_out, input_grad, att_share, packed[cols : 2 * cols].T, packed[:cols],
        key_share, value_share, rec_share, packed[2 * cols :],
    )


def solution(mesh):
    seq, wide = mesh.devices.shape
    fine = Mesh(mesh.devices.reshape(seq, wide // 4, 2, 2), ALL)
    token = P(None, ALL, None)
    by_row, by_col, stacked = P(WIDE, None), P(None, WIDE), P(None, WIDE, None)
    return jax.shard_map(
        body,
        mesh=fine,
        in_specs=(token, stacked, by_row, by_col, by_row, by_row, by_row, by_col, token),
        out_specs=(token, token, stacked, by_row, by_col, by_row, by_row, by_row, by_col),
        check_vma=False,
    )
```

```python
import jax
import jax.numpy as jnp
from jax import lax
from jax.experimental import pallas as pl
from jax.experimental.pallas import tpu as pltpu
from jax.sharding import Mesh
from jax.sharding import PartitionSpec as P

HEAD = 64
RANK = 32
MIXCOLS = 5 * RANK
LANES = 128
F32, BF16 = jnp.float32, jnp.bfloat16
WIDE = ("z", "x", "core")
ALL = ("y", "z", "x", "core")


def nn(a, b):
    return jnp.dot(a, b, preferred_element_type=F32)


def nt(a, b):
    return lax.dot_general(a, b, (((1,), (1,)), ((), ())), preferred_element_type=F32)


def tn(a, b):
    return lax.dot_general(a, b, (((0,), (0,)), ((), ())), preferred_element_type=F32)


def low(a):
    return a.astype(BF16)


def swap(value, axis):
    return lax.ppermute(value, axis, [(0, 1), (1, 0)])


def along(value, step):
    count = lax.axis_size(ALL)
    if step > 0:
        pairs = [(i, i + 1) for i in range(count - 1)]
    else:
        pairs = [(i + 1, i) for i in range(count - 1)]
    return lax.ppermute(value, ALL, pairs)


def piece(value, index, size, axis):
    start = [0] * value.ndim
    start[axis] = index * size
    shape = list(value.shape)
    shape[axis] = size
    return lax.dynamic_slice(value, start, shape)


def line_own(block, index):
    count = lax.axis_size("z")
    return lax.dynamic_index_in_dim(block, jnp.clip(index, 0, count - 1), 0, False).astype(F32)


def line_step(block, t, moving):
    count, place = lax.axis_size("z"), lax.axis_index("z")
    right = line_own(block, count - t + place)
    left = line_own(block, place + t - count)
    if moving is not None:
        right, left = right + moving[0].astype(F32), left + moving[1].astype(F32)
    up = lax.ppermute(low(right), "z", [(i, i + 1) for i in range(count - 1) if i <= t - 1])
    down = lax.ppermute(
        low(left), "z", [(i, i - 1) for i in range(1, count) if count - 1 - i <= t - 1]
    )
    return up, down


def line_end(block, moving):
    own = line_own(block, lax.axis_index("z"))
    return own + moving[0].astype(F32) + moving[1].astype(F32)


def line_sum(block):
    moving = None
    for t in range(1, lax.axis_size("z")):
        moving = line_step(block, t, moving)
    return line_end(block, moving)


def pack_columns(parts):
    width = parts[0].shape[1]
    counts = [p.shape[0] for p in parts]
    rows = sum(counts)
    block = LANES

    def kernel(*refs):
        out = refs[-1]
        start = 0
        while start < len(counts):
            take, n = [], 0
            while n == 0 or n % 8:
                take.append(refs[start][...])
                n += counts[start]
                start += 1
            first = sum(counts[: start - len(take)])
            out[0, first : first + n] = take[0] if len(take) == 1 else jnp.concatenate(take, 0)

    return pl.pallas_call(
        kernel,
        grid=(width // block,),
        in_specs=[pl.BlockSpec((c, block), lambda j: (0, j)) for c in counts],
        out_specs=pl.BlockSpec((1, rows, block), lambda j: (j, 0, 0)),
        out_shape=jax.ShapeDtypeStruct((width // block, rows, block), F32),
        name="pack_columns",
    )(*parts)


def small_core(value):
    z, rows = lax.axis_size("z"), value.shape[1]
    share = 16 * LANES // (4 * z)
    if share != LANES:
        value = value.reshape(16, rows, LANES // share, share).swapaxes(1, 2).reshape(-1, rows, share)
    core = lax.axis_index("core")
    value = value.reshape(2 * z, 2, rows, share)
    give = low(lax.dynamic_index_in_dim(value, 1 - core, 1, False))
    value = lax.dynamic_index_in_dim(value, core, 1, False) + swap(give, "core").astype(F32)
    return value.reshape(z, 2, rows, share)


def small_sum(value):
    x = lax.axis_index("x")
    give = low(lax.dynamic_index_in_dim(value, 1 - x, 1, False))
    value = line_sum(lax.dynamic_index_in_dim(value, x, 1, False) + swap(give, "x").astype(F32))
    return value + swap(value, "y")


def tie(*values):
    return lax.optimization_barrier(values)


def half_cols(right):
    y = lax.axis_index("y")
    half = right.shape[2] // 2
    return piece(right, y, half, 2), swap(piece(right, 1 - y, half, 2), "y")


def quarter_cols(near, across):
    core = lax.axis_index("core")
    both = jnp.stack([near, across], 1)
    quarter = near.shape[2] // 2
    mine = piece(both, core, quarter, 3)
    other = swap(piece(both, 1 - core, quarter, 3), "core")
    both = jnp.stack([mine, other], 2)
    return both.reshape(near.shape[0], -1, quarter)


def spread_cols(part):
    y, core = lax.axis_index("y"), lax.axis_index("core")
    rows = part.shape[0] // 2
    keep = piece(part, core, rows, 0)
    give = piece(part, 1 - core, rows, 0)
    near, across = swap(give, "core"), swap(keep, "y")
    far = lax.ppermute(give, ("y", "core"), [(0, 3), (1, 2), (2, 1), (3, 0)])
    quarters = []
    for q in range(4):
        this, that = jnp.where(core == q % 2, keep, near), jnp.where(core == q % 2, across, far)
        quarters.append(jnp.where(y == q // 2, this, that))
    outs = [
        jnp.concatenate([a[:, i].astype(F32) for a in quarters], 1) for i in range(part.shape[1])
    ]
    return outs


def x_parts(part):
    x, z = lax.axis_index("x"), lax.axis_size("z")
    view = part.reshape(z, 2, -1, part.shape[1])
    give = lax.dynamic_index_in_dim(view, 1 - x, 1, False)
    keep = lax.dynamic_index_in_dim(view, x, 1, False)
    return give.reshape(-1, part.shape[1]), keep.reshape(-1, part.shape[1])


def z_sum(keep, got):
    part = low(keep.astype(F32) + got.astype(F32))
    return lax.psum_scatter(part, "z", scatter_dimension=0, tiled=True)


def grad_call(lefts, rights, block, count, place):
    total, tokens, q = rights.shape
    bounds = [0]
    for _, _, many in lefts:
        bounds.append(bounds[-1] + many)

    def left_spec(k):
        low_end, high_end, first = bounds[k], bounds[k + 1], lefts[k][1]

        def index(i, j, x):
            inside = jnp.logical_and(i >= low_end, i < high_end)
            which = jnp.clip(i, low_end, high_end - 1) - low_end + first
            at = jnp.where(inside, place(j, x[0]), place(jnp.where(i < low_end, 0, count - 1), x[0]))
            return which, 0, at

        return pl.BlockSpec((1, tokens, block), index)

    def kernel(x_ref, *refs):
        *a_refs, b_ref, o_ref = refs
        i = pl.program_id(0)
        for k, a_ref in enumerate(a_refs):

            @pl.when(jnp.logical_and(i >= bounds[k], i < bounds[k + 1]))
            def _(a_ref=a_ref):
                o_ref[...] = low(tn(a_ref[0], b_ref[0]))

    return pl.pallas_call(
        kernel,
        grid_spec=pltpu.PrefetchScalarGridSpec(
            num_scalar_prefetch=1,
            grid=(total, count),
            in_specs=[left_spec(k) for k in range(len(lefts))]
            + [pl.BlockSpec((1, tokens, q), lambda i, j, x: (i, 0, 0))],
            out_specs=pl.BlockSpec((block, q), lambda i, j, x: (j, i)),
        ),
        out_shape=jax.ShapeDtypeStruct((count * block, total * q), BF16),
        compiler_params=pltpu.CompilerParams(vmem_limit_bytes=40 << 20),
        cost_estimate=pl.CostEstimate(
            flops=2 * rights.size * count * block, transcendentals=0,
            bytes_accessed=2 * (tokens * total * count * block + rights.size + count * block * total * q),
        ),
        name="weight_grad",
    )(lax.axis_index("x").astype(jnp.int32).reshape(1), *[a for a, _, _ in lefts], rights)


def all_rows(lefts, rights):
    return grad_call(lefts, rights, 512, lefts[0][0].shape[2] // 512, lambda j, x: j)


def x_rows(lefts, rights):
    z = lax.axis_size("z")
    block = lefts[0][0].shape[2] // (2 * z)
    if block % LANES:
        return x_parts(all_rows(lefts, rights))
    give = grad_call(lefts, rights, block, z, lambda j, x: 2 * j + 1 - x)
    return give, grad_call(lefts, rights, block, z, lambda j, x: 2 * j + x)


def group_pieces(values):
    value = jnp.stack(values, 0)
    near = swap(value, "core")
    across = swap(value, "y")
    far = swap(across, "core")
    return value, near, across, far


def group_many(values):
    return jnp.concatenate(group_pieces(values), 1)


def group_sum(value):
    rows = value.shape[0] // 4
    pair = value.reshape(2, 2, rows, -1)
    got = swap(pair[:, 1], "core")
    across = swap(low(pair[1, 0].astype(F32) + got[1].astype(F32)), "y")
    return pair[0, 0].astype(F32) + got[0].astype(F32) + across.astype(F32)


SPAN = 256
GROUP = SPAN // HEAD
SUB = 32


def lane_head(shape, dim):
    return lax.broadcasted_iota(jnp.int32, shape, dim) // HEAD


def head_block(rows, cols):
    shape = (rows, cols)
    return jnp.where(lane_head(shape, 0) == lane_head(shape, 1), 1.0, 0.0).astype(BF16)


def head_sum(value):
    coarse = low(value)
    fine = low(value - coarse.astype(F32))
    ones = head_block(SPAN, SPAN)
    return nn(coarse, ones) + nn(fine, ones)


def exact_product(left, value):
    coarse = low(value)
    rest = value - coarse.astype(F32)
    fine = low(rest)
    last = low(rest - fine.astype(F32))
    return nn(left, coarse) + (nn(left, fine) + nn(left, last))


def triangle(length, keep):
    shape = (length, length)
    row = lax.broadcasted_iota(jnp.int32, shape, 0)
    col = lax.broadcasted_iota(jnp.int32, shape, 1)
    return jnp.where(keep(row, col), 1.0, 0.0).astype(BF16)


def spread_heads(value):
    lane = lane_head(value.shape, 1)
    return jnp.concatenate([low(jnp.where(lane == h, value, 0.0)) for h in range(GROUP)], 0)


def pick_heads(value):
    rows = value.shape[0] // GROUP
    lane = lane_head((rows, SPAN), 1)
    out = value[:rows]
    for h in range(1, GROUP):
        out = jnp.where(lane == h, value[h * rows : (h + 1) * rows], out)
    return out


def widen_state(ref):
    state = jnp.concatenate([ref[0, 0], ref[0, 1]], 1)
    return jnp.concatenate(
        [jnp.where(lane_head(state.shape, 1) == h, state, jnp.zeros_like(state)) for h in range(GROUP)], 0
    )


def store_state(ref, value):
    state = low(pick_heads(value))
    ref[0, 0] = state[:, :LANES]
    ref[0, 1] = state[:, LANES:]


def exclusive_of(inclusive):
    return jnp.concatenate([jnp.zeros_like(inclusive[:1]), inclusive[:-1]], 0)


def cap(value):
    return jnp.exp(jnp.minimum(value, 80.0))


def state_kernel(key_ref, value_ref, log_ref, inc_ref, state_ref, final_ref):
    length = log_ref.shape[0]
    inclusive = exact_product(triangle(length, lambda r, c: r >= c), log_ref[...])
    inc_ref[...] = inclusive
    final = inclusive[length - 1 :]
    weighted = low(key_ref[...] * jnp.exp(final - inclusive))
    store_state(state_ref, tn(weighted, low(value_ref[...])))
    coarse = low(final)
    fine = low(final - coarse.astype(F32))
    rows = jnp.concatenate([coarse, fine, jnp.zeros((14, SPAN), BF16)], 0)
    final_ref[0, 0] = rows[:, :LANES]
    final_ref[0, 1] = rows[:, LANES:]


def sub_block(q, inclusive, exclusive, length):
    start, stop = q * SUB, (q + 1) * SUB
    middle = inclusive[start + SUB // 2 - 1 : start + SUB // 2]
    query = cap(exclusive[start:stop] - middle)
    key = cap(middle - inclusive[:stop])
    shape = (GROUP * SUB, stop)
    row = lax.rem(lax.broadcasted_iota(jnp.int32, shape, 0), SUB) + start
    mask = row > lax.broadcasted_iota(jnp.int32, shape, 1)
    return start, stop, query, key, mask


def wkv_kernel(rec_ref, key_ref, value_ref, inc_ref, state_ref, gate_ref, row_ref, wkv_ref, gated_ref):
    length = rec_ref.shape[0]
    inclusive = inc_ref[...]
    exclusive = exclusive_of(inclusive)
    rec, key, value = rec_ref[...], key_ref[...], value_ref[...]
    value_low = low(value)
    bonus, gain, bias = row_ref[9:10], row_ref[10:11], row_ref[11:12]
    answer = nn(low(rec * jnp.exp(exclusive)), widen_state(state_ref))
    answer = answer + head_sum(rec * bonus * key) * value
    parts = []
    for q in range(length // SUB):
        start, stop, query, fade, mask = sub_block(q, inclusive, exclusive, length)
        left = spread_heads(rec[start:stop] * query)
        scores = nt(left, low(key[:stop] * fade))
        scores = low(jnp.where(mask, scores, 0.0))
        parts.append(pick_heads(nn(scores, value_low[:stop])))
    answer = answer + jnp.concatenate(parts, 0)
    wkv_ref[...] = answer
    centered = answer - head_sum(answer) * (1.0 / HEAD)
    spread = head_sum(centered * centered) * (1.0 / HEAD)
    grouped = centered * lax.rsqrt(spread + 0.00064) * gain + bias
    gate = gate_ref[...]
    gated_ref[...] = low(grouped * gate / (1.0 + jnp.exp(-gate)))


def gate_back_kernel(grad_ref, wkv_ref, gate_ref, rec_ref, inc_ref, row_ref, gwkv_ref, ggate_ref, state_ref, sum_ref):
    gain, bias = row_ref[10:11], row_ref[11:12]
    answer, gate, grad = wkv_ref[...], gate_ref[...], grad_ref[...]
    centered = answer - head_sum(answer) * (1.0 / HEAD)
    rstd = lax.rsqrt(head_sum(centered * centered) * (1.0 / HEAD) + 0.00064)
    hat = centered * rstd
    grouped = hat * gain + bias
    sig = 1.0 / (1.0 + jnp.exp(-gate))
    g_grouped = grad * gate * sig
    ggate_ref[...] = low(grad * grouped * sig * (1.0 + gate * (1.0 - sig)))
    g_gain = jnp.sum(g_grouped * hat, 0, keepdims=True)
    g_bias = jnp.sum(g_grouped, 0, keepdims=True)
    sum_ref[0] = jnp.concatenate([g_gain, g_bias, jnp.zeros((6, SPAN), F32)], 0)
    g_hat = g_grouped * gain
    back = rstd * (
        g_hat - head_sum(g_hat) * (1.0 / HEAD) - hat * (head_sum(g_hat * hat) * (1.0 / HEAD))
    )
    back = low(back)
    gwkv_ref[...] = back
    query = low(rec_ref[...] * jnp.exp(exclusive_of(inc_ref[...])))
    store_state(state_ref, tn(query, back))


def wkv_back_kernel(
    rec_ref, key_ref, value_ref, inc_ref, log_ref, state_ref, gstate_ref, gwkv_ref, row_ref,
    grec_ref, gkey_ref, gvalue_ref, gdecay_ref, sum_ref, key_acc, value_acc, pair_acc,
):
    length = rec_ref.shape[0]
    inclusive = inc_ref[...]
    exclusive = exclusive_of(inclusive)
    final = inclusive[length - 1 :]
    rec, key, value = rec_ref[...], key_ref[...], value_ref[...]
    value_low = low(value)
    grad_low = gwkv_ref[...]
    grad = grad_low.astype(F32)
    bonus = row_ref[9:10]
    state, gstate = widen_state(state_ref), widen_state(gstate_ref)
    pair = head_sum(grad * value)
    shared = pair * bonus
    g_key = shared * rec
    g_value = head_sum(rec * bonus * key) * grad
    g_bonus = jnp.sum(rec * key * pair, 0, keepdims=True)
    fade = jnp.exp(exclusive)
    back = nt(grad_low, state)
    from_state = low(rec * fade).astype(F32) * back
    g_rec = shared * key + fade * back
    fade = jnp.exp(final - inclusive)
    weighted = low(key * fade)
    back = nt(value_low, gstate)
    to_state = weighted.astype(F32) * back
    key_acc[...] = g_key + fade * back
    value_acc[...] = g_value + nn(weighted, gstate)
    pair_acc[...] = jnp.zeros_like(pair_acc)
    rec_parts, own_parts = [], []
    for q in range(length // SUB):
        start, stop, query, fade, mask = sub_block(q, inclusive, exclusive, length)
        left = rec[start:stop] * query
        spread = spread_heads(left)
        right = low(key[:stop] * fade)
        gspread = spread_heads(grad[start:stop])
        scores = low(jnp.where(mask, nt(spread, right), 0.0))
        weight = low(jnp.where(mask, nt(gspread, value_low[:stop]), 0.0))
        back = pick_heads(nn(weight, right))
        rec_parts.append(g_rec[start:stop] + query * back)
        own_parts.append(low(left).astype(F32) * back)
        back = tn(weight, spread)
        key_acc[:stop] += fade * back
        pair_acc[:stop] += right.astype(F32) * back
        value_acc[:stop] += tn(scores, gspread)
    grec_ref[...] = low(jnp.concatenate(rec_parts, 0))
    gkey_ref[...] = low(key_acc[...])
    gvalue_ref[...] = low(value_acc[...])
    inner, pairs = jnp.concatenate(own_parts, 0), pair_acc[...]
    both = head_sum(
        jnp.concatenate([state_ref[0, 0], state_ref[0, 1]], 1).astype(F32)
        * jnp.concatenate([gstate_ref[0, 0], gstate_ref[0, 1]], 1).astype(F32)
    )
    shape = both.shape
    here = lax.rem(lax.broadcasted_iota(jnp.int32, shape, 1), HEAD) == lax.broadcasted_iota(
        jnp.int32, shape, 0
    )
    through = jnp.exp(final) * jnp.sum(jnp.where(here, both, 0.0), 0, keepdims=True)
    later = exact_product(triangle(length, lambda r, c: r < c), inner + from_state - pairs)
    earlier = exact_product(triangle(length, lambda r, c: r > c), to_state)
    g_log = later - pairs + earlier + through
    g_decay = g_log * log_ref[...]
    gdecay_ref[...] = low(g_decay)
    sum_ref[0] = jnp.concatenate(
        [g_bonus, jnp.sum(g_decay, 0, keepdims=True), jnp.zeros((6, SPAN), F32)], 0
    )


def wkv_call(kernel, seqs, ins, outs, name, flops, scratch=()):
    width = ins[0].shape[1]
    length = ins[0].shape[0] // seqs

    def spec(a):
        if len(a.shape) == 4:
            return pl.BlockSpec((1, 2, a.shape[2], LANES), lambda s, g: (s, g, 0, 0))
        if len(a.shape) == 3:
            return pl.BlockSpec((1, 8, SPAN), lambda s, g: (s, 0, g))
        if a.shape[0] == 16:
            return pl.BlockSpec((16, SPAN), lambda s, g: (0, g))
        return pl.BlockSpec((length, SPAN), lambda s, g: (s, g))

    moved = sum(a.size * a.dtype.itemsize for a in ins + outs)
    return pl.pallas_call(
        kernel,
        grid=(seqs, width // SPAN),
        in_specs=[spec(a) for a in ins],
        out_specs=[spec(a) for a in outs],
        out_shape=outs,
        scratch_shapes=scratch,
        compiler_params=pltpu.CompilerParams(vmem_limit_bytes=40 << 20),
        cost_estimate=pl.CostEstimate(flops=flops, transcendentals=0, bytes_accessed=moved),
        name=name,
    )(*ins)


def chain_kernel(first_ref, packed_ref, out_ref, held_fade, *, rows, reverse):
    count = packed_ref.shape[0]
    logs = packed_ref[:, rows : rows + 1], packed_ref[:, rows + 1 : rows + 2]
    shape = (count, rows, LANES)
    lane = lax.rem(lax.broadcasted_iota(jnp.int32, shape, 2), HEAD)
    here = lane == lax.broadcasted_iota(jnp.int32, shape, 1) + first_ref[0]
    ones = head_block(LANES, LANES)
    total = None
    for part in logs:
        part = jnp.where(here, part.astype(F32), 0.0)
        part = nn(low(part.reshape(count * rows, LANES)), ones)
        total = part if total is None else total + part
    held_fade[...] = jnp.exp(total).reshape(shape)

    def one(hop, held):
        b = count - 1 - hop if reverse else hop
        out_ref[b] = low(held)
        return held_fade[b] * held + packed_ref[b, :rows].astype(F32)

    lax.fori_loop(0, count, one, jnp.zeros((rows, LANES), F32))


def chain(state, finals, reverse):
    count = lax.axis_size(ALL)
    pairs = state.shape[0] * state.shape[1]
    split = count // pairs
    rows = state.shape[2] // split
    logs = finals.reshape(pairs, finals.shape[2], LANES)
    if split > 1:
        logs = jnp.repeat(logs, split, axis=0)
    packed = jnp.concatenate([state.reshape(count, rows, LANES), logs], 1)
    packed = lax.all_to_all(packed, ALL, 0, 0, tiled=True)
    first = lax.rem(lax.axis_index(ALL), split) * rows
    entering = pl.pallas_call(
        lambda *refs: chain_kernel(*refs, rows=rows, reverse=reverse),
        grid_spec=pltpu.PrefetchScalarGridSpec(
            num_scalar_prefetch=1,
            grid=(1,),
            in_specs=[pl.BlockSpec(packed.shape, lambda i, c: (0, 0, 0))],
            out_specs=pl.BlockSpec((count, rows, LANES), lambda i, c: (0, 0, 0)),
            scratch_shapes=[pltpu.VMEM((count, rows, LANES), F32)],
        ),
        out_shape=jax.ShapeDtypeStruct((count, rows, LANES), BF16),
        compiler_params=pltpu.CompilerParams(vmem_limit_bytes=40 << 20),
        name="chain",
    )(first.astype(jnp.int32).reshape(1), packed)
    return lax.all_to_all(entering, ALL, 0, 0, tiled=True).reshape(state.shape)


def norm_forward(values, gain, bias):
    mean = jnp.mean(values, -1, keepdims=True)
    centered = values - mean
    rstd = lax.rsqrt(jnp.mean(centered * centered, -1, keepdims=True) + 1e-05)
    hat = centered * rstd
    return hat * gain + bias, hat, rstd


def norm_backward(grad, hat, rstd, gain):
    d = grad * gain
    back = rstd * (
        d - jnp.mean(d, -1, keepdims=True) - hat * jnp.mean(d * hat, -1, keepdims=True)
    )
    return back, jnp.sum(grad * hat, 0, keepdims=True), jnp.sum(grad, 0, keepdims=True)


def prior_of(values, seqs):
    shaped = values.reshape(seqs, -1, values.shape[-1])
    incoming = along(shaped[:, -1], 1)
    return jnp.concatenate([incoming[:, None], shaped[:, :-1]], 1).reshape(values.shape)


def prior_back(grad, seqs):
    shaped = grad.reshape(seqs, -1, grad.shape[-1])
    incoming = along(shaped[:, 0], -1)
    return jnp.concatenate([shaped[:, 1:], incoming[:, None]], 1).reshape(grad.shape)


def stack_nn(value, shards, which, tile=512):
    devices, _, rows, cols = shards.shape

    def kernel(a_ref, w_ref, o_ref):
        w = w_ref[...].reshape(devices * rows, tile)
        o_ref[...] = jnp.dot(a_ref[...], w, preferred_element_type=F32)

    return pl.pallas_call(
        kernel,
        grid=(cols // tile,),
        out_shape=jax.ShapeDtypeStruct((value.shape[0], cols), F32),
        in_specs=[
            pl.BlockSpec(value.shape, lambda j: (0, 0)),
            pl.BlockSpec((devices, 1, rows, tile), lambda j: (0, which, 0, j)),
        ],
        out_specs=pl.BlockSpec((value.shape[0], tile), lambda j: (0, j)),
        compiler_params=pltpu.CompilerParams(vmem_limit_bytes=40 << 20),
        cost_estimate=pl.CostEstimate(
            flops=2 * value.size * cols, transcendentals=0,
            bytes_accessed=2 * value.size + 2 * devices * rows * cols + 4 * value.shape[0] * cols,
        ),
        name="stack_nn",
    )(value, shards)


def stack_nt(value, shards, which, tile=512):
    devices, _, rows, cols = shards.shape
    group = tile // rows

    def kernel(a_ref, w_ref, o_ref):
        w = w_ref[...].reshape(tile, cols)
        o_ref[...] = lax.dot_general(
            a_ref[...], w, (((1,), (1,)), ((), ())), preferred_element_type=F32
        )

    return pl.pallas_call(
        kernel,
        grid=(devices // group,),
        out_shape=jax.ShapeDtypeStruct((value.shape[0], devices * rows), F32),
        in_specs=[
            pl.BlockSpec(value.shape, lambda j: (0, 0)),
            pl.BlockSpec((group, 1, rows, cols), lambda j: (j, which, 0, 0)),
        ],
        out_specs=pl.BlockSpec((value.shape[0], tile), lambda j: (0, j)),
        compiler_params=pltpu.CompilerParams(vmem_limit_bytes=40 << 20),
        cost_estimate=pl.CostEstimate(
            flops=2 * value.size * devices * rows, transcendentals=0,
            bytes_accessed=2 * value.size + 2 * devices * rows * cols
            + 4 * value.shape[0] * devices * rows,
        ),
        name="stack_nt",
    )(value, shards)


TILE = 256


def pack_blocks(shard):
    rows, cols = shard.shape
    return jnp.swapaxes(shard.reshape(rows, cols // TILE, TILE), 0, 1).reshape(-1, TILE)


def ffn_call(kernel, core, grid, ins, specs, outs, out_specs, flops, scratch=(), name=None):
    moved = sum(a.size * a.dtype.itemsize for a in ins[:1] + outs) + flops // 1024
    return pl.pallas_call(
        kernel,
        grid_spec=pltpu.PrefetchScalarGridSpec(
            num_scalar_prefetch=1, grid=grid, in_specs=specs, out_specs=out_specs, scratch_shapes=scratch
        ),
        out_shape=outs,
        compiler_params=pltpu.CompilerParams(vmem_limit_bytes=56 << 20),
        cost_estimate=pl.CostEstimate(flops=flops, transcendentals=0, bytes_accessed=moved),
        name=name,
    )(core.reshape(1), *ins)


class PackedWeights:
    def __init__(self, packed, core, ff, width, half, chips):
        self.packed, self.core = packed, core
        self.devices = packed.shape[0]
        self.rows = width // self.devices
        self.quarter, self.width, self.half, self.chips = ff // 4, width, half, chips
        self.blocks = self.quarter // TILE
        self.fast = half % 16 == 0 and self.rows % 16 == 0 and self.rows == 128

    def _plain(self, start, rows, count):
        part = self.packed[:, start : start + rows * count]
        return part.reshape(-1, count, rows, TILE)

    def plain_key(self):
        start = self.half * (self.width // TILE)
        part = self._plain(start, self.rows, 2 * self.blocks)
        part = piece(part, self.core, self.blocks, 1)
        return jnp.swapaxes(part, 1, 2).reshape(self.width, self.quarter)

    def plain_value(self):
        part = self._plain(0, self.half, self.width // TILE)
        part = lax.dynamic_index_in_dim(
            part.reshape(self.chips, 2, *part.shape[1:]), self.core, 1, False
        )
        return jnp.swapaxes(part, 1, 2).reshape(self.quarter, self.width)

    def plain_rec(self):
        start = self.half * (self.width // TILE) + self.rows * 2 * self.blocks
        part = self._plain(start, self.rows, self.width // TILE)
        return jnp.swapaxes(part, 1, 2).reshape(self.width, self.width)

    def key_forward(self, mix):
        if not self.fast:
            relu = low(jnp.maximum(nn(mix, self.plain_key()), 0.0))
            return relu, low(relu.astype(F32) * relu.astype(F32))
        tokens = mix.shape[0]
        first = self.half * (self.width // TILE) // self.rows

        def kernel(c_ref, a_ref, w_ref, relu_ref, sq_ref):
            w = w_ref[...].reshape(self.width, TILE)
            relu = jnp.maximum(jnp.dot(a_ref[...], w, preferred_element_type=F32), 0.0)
            relu_ref[...] = low(relu)
            sq_ref[...] = low(relu * relu)

        out = jax.ShapeDtypeStruct((tokens, self.quarter), BF16)
        spec = pl.BlockSpec((tokens, TILE), lambda n, c: (0, n))
        return ffn_call(
            kernel, self.core, (self.blocks,), [mix, self.packed],
            [pl.BlockSpec(mix.shape, lambda n, c: (0, 0)),
             pl.BlockSpec((self.devices, self.rows, TILE),
                          lambda n, c: (0, first + c[0] * self.blocks + n, 0))],
            [out, out], [spec, spec], 2 * mix.size * self.quarter, name="key_forward",
        )

    def value_forward(self, squared):
        if not self.fast:
            return low(nn(squared, self.plain_value()))
        tokens = squared.shape[0]
        view = self.packed.reshape(self.chips, 2, *self.packed.shape[1:])

        def kernel(c_ref, a_ref, w_ref, o_ref):
            w = w_ref[...].reshape(self.quarter, TILE)
            o_ref[...] = low(jnp.dot(a_ref[...], w, preferred_element_type=F32))

        return ffn_call(
            kernel, self.core, (self.width // TILE,), [squared, view],
            [pl.BlockSpec(squared.shape, lambda m, c: (0, 0)),
             pl.BlockSpec((self.chips, 1, self.half, TILE), lambda m, c: (0, c[0], m, 0))],
            [jax.ShapeDtypeStruct((tokens, self.width), BF16)],
            [pl.BlockSpec((tokens, TILE), lambda m, c: (0, m))],
            2 * squared.size * self.width, name="value_forward",
        )[0]

    def rec_forward(self, mix):
        if not self.fast:
            return jax.nn.sigmoid(nn(mix, self.plain_rec()))
        tokens = mix.shape[0]
        first = self.packed.shape[1] // self.rows - self.width // TILE

        def kernel(c_ref, a_ref, w_ref, o_ref):
            w = w_ref[...].reshape(self.width, TILE)
            o_ref[...] = jax.nn.sigmoid(jnp.dot(a_ref[...], w, preferred_element_type=F32))

        return ffn_call(
            kernel, self.core, (self.width // TILE,), [mix, self.packed],
            [pl.BlockSpec(mix.shape, lambda m, c: (0, 0)),
             pl.BlockSpec((self.devices, self.rows, TILE), lambda m, c: (0, first + m, 0))],
            [jax.ShapeDtypeStruct((tokens, self.width), F32)],
            [pl.BlockSpec((tokens, TILE), lambda m, c: (0, m))],
            2 * mix.size * self.width, name="rec_forward",
        )[0]

    def value_backward(self, grad, relu):
        if not self.fast:
            return low(nt(grad, self.plain_value()) * 2.0 * relu.astype(F32))
        tokens = grad.shape[0]
        view = self.packed.reshape(self.chips, 2, *self.packed.shape[1:])
        count = self.width // TILE
        part = self.chips // 2

        def kernel(c_ref, a_ref, r_ref, w_ref, o_ref, flat):
            w = w_ref[...].reshape(part, count, self.half, TILE)
            for m in range(count):
                flat[:, m * TILE : (m + 1) * TILE] = w[:, m].reshape(part * self.half, TILE)
            back = lax.dot_general(
                a_ref[...], flat[...], (((1,), (1,)), ((), ())), preferred_element_type=F32
            )
            o_ref[...] = low(back * 2.0 * r_ref[...].astype(F32))

        wide = part * self.half
        return ffn_call(
            kernel, self.core, (2,), [grad, relu, view],
            [pl.BlockSpec(grad.shape, lambda i, c: (0, 0)),
             pl.BlockSpec((tokens, wide), lambda i, c: (0, i)),
             pl.BlockSpec((part, 1, count * self.half, TILE), lambda i, c: (i, c[0], 0, 0))],
            [jax.ShapeDtypeStruct((tokens, self.quarter), BF16)],
            [pl.BlockSpec((tokens, wide), lambda i, c: (0, i))],
            2 * grad.size * self.quarter,
            scratch=(pltpu.VMEM((wide, self.width), BF16),), name="value_backward",
        )[0]

    def key_backward(self, grad):
        if not self.fast:
            return low(nt(grad, self.plain_key()))
        tokens = grad.shape[0]
        part = 4
        rows = self.blocks * self.rows
        first = self.half * (self.width // TILE) // rows

        def kernel(c_ref, a_ref, w_ref, o_ref, flat):
            w = w_ref[...].reshape(part, self.blocks, self.rows, TILE)
            for n in range(self.blocks):
                flat[:, n * TILE : (n + 1) * TILE] = w[:, n].reshape(part * self.rows, TILE)
            o_ref[...] = low(lax.dot_general(
                a_ref[...], flat[...], (((1,), (1,)), ((), ())), preferred_element_type=F32
            ))

        wide = part * self.rows
        return ffn_call(
            kernel, self.core, (self.devices // part,), [grad, self.packed],
            [pl.BlockSpec(grad.shape, lambda i, c: (0, 0)),
             pl.BlockSpec((part, rows, TILE), lambda i, c: (i, first + c[0], 0))],
            [jax.ShapeDtypeStruct((tokens, self.width), BF16)],
            [pl.BlockSpec((tokens, wide), lambda i, c: (0, i))],
            2 * grad.size * self.width,
            scratch=(pltpu.VMEM((wide, self.quarter), BF16),), name="key_backward",
        )[0]

    def rec_backward(self, grad):
        if not self.fast:
            return nt(grad, self.plain_rec())
        tokens = grad.shape[0]
        part, count = 4, self.width // TILE
        rows = count * self.rows // 2
        first = self.packed.shape[1] // rows - 2

        def kernel(c_ref, a_ref, w_ref, v_ref, o_ref, flat):
            for k, ref in enumerate((w_ref, v_ref)):
                w = ref[...].reshape(part, count // 2, self.rows, TILE)
                for n in range(count // 2):
                    m = k * (count // 2) + n
                    flat[:, m * TILE : (m + 1) * TILE] = w[:, n].reshape(part * self.rows, TILE)
            o_ref[...] = lax.dot_general(
                a_ref[...], flat[...], (((1,), (1,)), ((), ())), preferred_element_type=F32
            )

        wide = part * self.rows
        return ffn_call(
            kernel, self.core, (self.devices // part,), [grad, self.packed, self.packed],
            [pl.BlockSpec(grad.shape, lambda i, c: (0, 0)),
             pl.BlockSpec((part, rows, TILE), lambda i, c: (i, first, 0)),
             pl.BlockSpec((part, rows, TILE), lambda i, c: (i, first + 1, 0))],
            [jax.ShapeDtypeStruct((tokens, self.width), F32)],
            [pl.BlockSpec((tokens, wide), lambda i, c: (0, i))],
            2 * grad.size * self.width,
            scratch=(pltpu.VMEM((wide, self.width), BF16),), name="rec_backward",
        )[0]


def body(tokens, att_w, down_w, up_w, key_w, value_w, rec_w, vectors, out_grad):
    seqs, length, width = tokens.shape
    total = seqs * length
    y, core = lax.axis_index("y"), lax.axis_index("core")
    zs = lax.axis_size("z")
    ff = key_w.shape[1]
    share = value_w.shape[0]
    half = share // 2
    quarter = ff // 4

    def rows(v):
        return v.reshape(total, width)

    def columns(shard):
        gathered = lax.all_gather(shard, WIDE, axis=0)
        return jnp.swapaxes(gathered, 0, 1).reshape(shard.shape[0], width)

    cols = up_w.shape[0]
    up_vec = columns(jnp.concatenate([vectors, up_w], 0))
    vec, up = up_vec[:16].astype(F32), up_vec[16:]
    down_t = columns(down_w.T)
    w_att = lax.all_gather(att_w, WIDE, axis=0)
    key_sh = key_w.reshape(-1, zs, 2, 2, 2, half)
    key_sh = lax.dynamic_index_in_dim(key_sh, y, 4, False)
    key_sh = key_sh.transpose(0, 3, 1, 2, 4).reshape(-1, 2 * quarter)
    packed = jnp.concatenate(
        [pack_blocks(piece(value_w, y, half, 0)), pack_blocks(key_sh), pack_blocks(rec_w)], 0
    )
    packed = lax.all_gather(packed, WIDE, axis=0)

    x = rows(tokens.astype(F32))
    normed, hat, rstd = norm_forward(x, vec[0], vec[1])
    delta = prior_of(normed, seqs) - normed
    mix_low = low(normed + delta * vec[2])
    tanh_mix = jnp.tanh(nt(mix_low, down_t[:MIXCOLS]))
    hidden = low(tanh_mix)
    hid = [hidden[:, i * RANK : (i + 1) * RANK] for i in range(5)]
    ups = [up[i * RANK : (i + 1) * RANK] for i in range(5)]
    mixed = [low(normed + delta * (vec[3 + i] + nn(hid[i], ups[i]))) for i in range(5)]
    decay_in, key_in, value_in, rec_in, gate_in = mixed
    tanh_decay = jnp.tanh(nt(decay_in, down_t[MIXCOLS:]))
    hidden_decay = low(tanh_decay)
    logdecay = -jnp.exp(vec[8] + nn(hidden_decay, up[MIXCOLS:]))
    mix_all = group_many([gate_in, rec_in, key_in, value_in])
    w_att, mix_all = tie(w_att, mix_all)
    keys = stack_nn(key_in, w_att, 1)
    values = stack_nn(value_in, w_att, 2)
    shaped = jax.ShapeDtypeStruct
    flat, flat_low = shaped((total, width), F32), shaped((total, width), BF16)
    states = shaped((seqs, width // LANES, HEAD, LANES), BF16)
    finals = shaped((seqs, width // LANES, 16, LANES), BF16)
    sums = shaped((seqs, 8, width), F32)
    unit = 2 * total * width
    inclusive, state, final = wkv_call(
        state_kernel, seqs, [keys, values, logdecay], [flat, states, finals], "wkv_state", unit * 512
    )
    carried = chain(state, final, False)
    recept = stack_nn(rec_in, w_att, 0)
    gate_pre = stack_nn(gate_in, w_att, 3)
    wkv, gated = wkv_call(
        wkv_kernel, seqs, [recept, keys, values, inclusive, carried, gate_pre, vec], [flat, flat_low],
        "wkv_forward", unit * 1536,
    )
    first_sum = x + stack_nn(gated, w_att, 4)

    normed_two, hat_two, rstd_two = norm_forward(first_sum, vec[12], vec[13])
    delta_two = prior_of(normed_two, seqs) - normed_two
    key_mix = low(normed_two + delta_two * vec[14])
    rec_mix = low(normed_two + delta_two * vec[15])
    key_all = group_many([key_mix])[0]
    key_all, rec_low, gated_low = tie(key_all, rec_mix, gated)
    side_all = group_pieces([rec_low, gated_low])
    ffn = PackedWeights(packed, core, ff, width, half, 2 * zs)
    relu, squared = ffn.key_forward(key_all)
    squared, side_all = tie(squared, side_all)
    value_out = group_sum(ffn.value_forward(squared))
    rec_gate = ffn.rec_forward(rec_mix)
    block_out = low(first_sum + rec_gate * value_out).reshape(tokens.shape)

    g = rows(out_grad.astype(F32))
    grad_value = low(g * rec_gate)
    grad_gate_in = low(g * value_out * rec_gate * (1.0 - rec_gate))
    value_all = group_many([grad_value])[0]
    value_part = low(tn(squared, value_all)).reshape(-1, half, width)
    value_part, value_all = tie(value_part, value_all)
    value_part = lax.psum_scatter(value_part, ("z", "x"), scatter_dimension=0, tiled=True)[0]
    grad_key_pre = ffn.value_backward(value_all, relu)
    g_key_mix = ffn.key_backward(grad_key_pre)
    grad_key_pre, g_key_mix = tie(grad_key_pre, g_key_mix)
    key_part = low(tn(key_all, grad_key_pre))
    key_part = lax.psum_scatter(key_part, ("z", "x"), scatter_dimension=0, tiled=True)
    g_key_mix = group_sum(g_key_mix)
    g_rec_mix = ffn.rec_backward(grad_gate_in)

    g_prior = prior_back(g_key_mix * vec[14] + g_rec_mix * vec[15], seqs)
    g_normed_two = g_key_mix * (1.0 - vec[14]) + g_rec_mix * (1.0 - vec[15]) + g_prior
    g_maa_key = jnp.sum(g_key_mix * delta_two, 0, keepdims=True)
    g_maa_rec = jnp.sum(g_rec_mix * delta_two, 0, keepdims=True)
    back_two, g_gain_two, g_bias_two = norm_backward(g_normed_two, hat_two, rstd_two, vec[12])
    grad_first = g + back_two

    grad_att = low(grad_first)
    g_wkv, g_gate_low, g_state, gate_sums = wkv_call(
        gate_back_kernel, seqs,
        [stack_nt(grad_att, w_att, 4), wkv, gate_pre, recept, inclusive, vec],
        [flat_low, flat_low, states, sums], "gate_backward", unit * 1536,
    )
    g_state_out = chain(g_state, final, True)
    g_state_out, grad_gate_in, grad_att, g_gate_low, value_part = tie(
        g_state_out, grad_gate_in, grad_att, g_gate_low, value_part
    )
    side_near, side_across = half_cols(jnp.stack([grad_gate_in, grad_att, g_gate_low], 0))
    g_rec, g_key, g_val, g_decay_low, wkv_sums = wkv_call(
        wkv_back_kernel, seqs,
        [recept, keys, values, inclusive, logdecay, carried, g_state_out, g_wkv, vec],
        [flat_low, flat_low, flat_low, flat_low, sums], "wkv_backward", unit * 4096,
        scratch=[pltpu.VMEM((length, SPAN), F32)] * 3,
    )
    gate_sums, wkv_sums = jnp.sum(gate_sums, 0), jnp.sum(wkv_sums, 0)
    projs = [g_rec, g_key, g_val, g_gate_low]
    main_near, main_across = half_cols(jnp.stack([g_rec, g_key, g_val], 0))
    main_near, side_across = tie(main_near, side_across)
    side_lefts = [(jnp.concatenate(side_all, 1), 0, 2), (mix_all, 0, 1)]
    side_give, side_keep = x_rows(side_lefts, quarter_cols(side_near, side_across))
    side_got = swap(side_give, "x")
    main_across, side_keep = tie(main_across, side_keep)
    main = all_rows([(mix_all, 1, 3)], quarter_cols(main_near, main_across))
    main, g_rec, g_key, g_val, g_gate_low, g_decay_low, key_part = tie(
        main, g_rec, g_key, g_val, g_gate_low, g_decay_low, key_part
    )
    main = lax.psum_scatter(main, ("z", "x"), scatter_dimension=0, tiled=True)
    projs = [g_rec, g_key, g_val, g_gate_low]

    decay_up_grad = tn(hidden_decay, g_decay_low)
    g_pre_decay = low(nt(g_decay_low, up[MIXCOLS:]) * (1.0 - tanh_decay * tanh_decay))
    decay_down_grad = tn(g_pre_decay, decay_in)
    g_mixed = [
        nn(g_pre_decay, down_t[MIXCOLS:]),
        stack_nt(projs[1], w_att, 1),
        stack_nt(projs[2], w_att, 2),
        stack_nt(projs[0], w_att, 0),
        stack_nt(projs[3], w_att, 3),
    ]
    g_normed = g_prior_sum = None
    maa_rows, up_grads, hid_grads = [], [], []
    for i in range(5):
        offset = vec[3 + i] + nn(hid[i], ups[i])
        g_off = g_mixed[i] * delta
        maa_rows.append(jnp.sum(g_off, 0, keepdims=True))
        off_low = low(g_off)
        up_grads.append(tn(hid[i], off_low))
        hid_grads.append(nt(off_low, ups[i]))
        here = g_mixed[i] * (1.0 - offset)
        back = g_mixed[i] * offset
        g_normed = here if g_normed is None else g_normed + here
        g_prior_sum = back if g_prior_sum is None else g_prior_sum + back
    g_pre_mix = low(jnp.concatenate(hid_grads, 1) * (1.0 - tanh_mix * tanh_mix))
    g_pre_mix, value_part, key_part, side_got = tie(g_pre_mix, value_part, key_part, side_got)
    side = low(side_keep.astype(F32) + side_got.astype(F32))
    side = side.reshape(zs, -1, side.shape[1])
    moving = line_step(side, 1, None)
    mix_down_grad = tn(g_pre_mix, mix_low)
    g_first_mix = nn(g_pre_mix, down_t[:MIXCOLS])
    maa_first = jnp.sum(g_first_mix * delta, 0, keepdims=True)
    g_prior_sum = g_prior_sum + g_first_mix * vec[2]
    g_normed = g_normed + g_first_mix * (1.0 - vec[2]) + prior_back(g_prior_sum, seqs)
    back_one, g_gain, g_bias = norm_backward(g_normed, hat, rstd, vec[0])
    input_grad = (grad_first + back_one).reshape(tokens.shape)

    vec_rows = (
        [g_gain, g_bias, maa_first] + maa_rows
        + [wkv_sums[1:2], wkv_sums[0:1], gate_sums[0:1], gate_sums[1:2], g_gain_two, g_bias_two,
           g_maa_key, g_maa_rec]
    )
    packed = pack_columns(up_grads + [decay_up_grad, mix_down_grad, decay_down_grad] + vec_rows)
    first = y == 0
    other = swap(value_part, "y")
    value_share = jnp.concatenate(
        [jnp.where(first, value_part, other), jnp.where(first, other, value_part)], 0
    ).astype(F32)
    key_share = spread_cols(key_part[:, None])[0].reshape(-1, 2, 2, zs, 2, half)
    key_share = key_share.transpose(0, 3, 4, 2, 1, 5).reshape(-1, ff)
    packed, key_share, value_share, moving = tie(packed, key_share, value_share, moving)
    for t in range(2, zs - 1):
        moving = line_step(side, t, moving)
    packed, main, moving = tie(small_core(packed), main, moving)
    side = low(line_end(side, line_step(side, zs - 1, moving)))
    late = spread_cols(main.reshape(main.shape[0], 3, -1))
    early = spread_cols(side.reshape(side.shape[0], 3, -1))
    packed = small_sum(packed)
    rec_share = early[0]
    att_share = jnp.stack(late + [early[2], early[1]], 0)
    return (
        block_out, input_grad, att_share, packed[cols : 2 * cols].T, packed[:cols],
        key_share, value_share, rec_share, packed[2 * cols :],
    )


def solution(mesh):
    seq, wide = mesh.devices.shape
    fine = Mesh(mesh.devices.reshape(seq, wide // 4, 2, 2), ALL)
    token = P(None, ALL, None)
    by_row, by_col, stacked = P(WIDE, None), P(None, WIDE), P(None, WIDE, None)
    return jax.shard_map(
        body,
        mesh=fine,
        in_specs=(token, stacked, by_row, by_col, by_row, by_row, by_row, by_col, token),
        out_specs=(token, token, stacked, by_row, by_col, by_row, by_row, by_row, by_col),
        check_vma=False,
    )
```

```python
import jax
import jax.numpy as jnp
from jax import lax
from jax.experimental import pallas as pl
from jax.experimental.pallas import tpu as pltpu
from jax.sharding import Mesh
from jax.sharding import PartitionSpec as P

HEAD = 64
RANK = 32
MIXCOLS = 5 * RANK
LANES = 128
F32, BF16 = jnp.float32, jnp.bfloat16
WIDE = ("z", "x", "core")
ALL = ("y", "z", "x", "core")


def nn(a, b):
    return jnp.dot(a, b, preferred_element_type=F32)


def nt(a, b):
    return lax.dot_general(a, b, (((1,), (1,)), ((), ())), preferred_element_type=F32)


def tn(a, b):
    return lax.dot_general(a, b, (((0,), (0,)), ((), ())), preferred_element_type=F32)


def low(a):
    return a.astype(BF16)


def swap(value, axis):
    return lax.ppermute(value, axis, [(0, 1), (1, 0)])


def along(value, step):
    count = lax.axis_size(ALL)
    if step > 0:
        pairs = [(i, i + 1) for i in range(count - 1)]
    else:
        pairs = [(i + 1, i) for i in range(count - 1)]
    return lax.ppermute(value, ALL, pairs)


def piece(value, index, size, axis):
    start = [0] * value.ndim
    start[axis] = index * size
    shape = list(value.shape)
    shape[axis] = size
    return lax.dynamic_slice(value, start, shape)


def line_own(block, index):
    count = lax.axis_size("z")
    return lax.dynamic_index_in_dim(block, jnp.clip(index, 0, count - 1), 0, False).astype(F32)


def line_step(block, t, moving):
    count, place = lax.axis_size("z"), lax.axis_index("z")
    right = line_own(block, count - t + place)
    left = line_own(block, place + t - count)
    if moving is not None:
        right, left = right + moving[0].astype(F32), left + moving[1].astype(F32)
    up = lax.ppermute(low(right), "z", [(i, i + 1) for i in range(count - 1) if i <= t - 1])
    down = lax.ppermute(
        low(left), "z", [(i, i - 1) for i in range(1, count) if count - 1 - i <= t - 1]
    )
    return up, down


def line_end(block, moving):
    own = line_own(block, lax.axis_index("z"))
    return own + moving[0].astype(F32) + moving[1].astype(F32)


def line_sum(block):
    moving = None
    for t in range(1, lax.axis_size("z")):
        moving = line_step(block, t, moving)
    return line_end(block, moving)


def pack_columns(parts):
    width = parts[0].shape[1]
    counts = [p.shape[0] for p in parts]
    rows = sum(counts)
    block = LANES

    def kernel(*refs):
        out = refs[-1]
        start = 0
        while start < len(counts):
            take, n = [], 0
            while n == 0 or n % 8:
                take.append(refs[start][...])
                n += counts[start]
                start += 1
            first = sum(counts[: start - len(take)])
            out[0, first : first + n] = take[0] if len(take) == 1 else jnp.concatenate(take, 0)

    return pl.pallas_call(
        kernel,
        grid=(width // block,),
        in_specs=[pl.BlockSpec((c, block), lambda j: (0, j)) for c in counts],
        out_specs=pl.BlockSpec((1, rows, block), lambda j: (j, 0, 0)),
        out_shape=jax.ShapeDtypeStruct((width // block, rows, block), F32),
        name="pack_columns",
    )(*parts)


def small_core(value):
    z, rows = lax.axis_size("z"), value.shape[1]
    share = 16 * LANES // (4 * z)
    if share != LANES:
        value = value.reshape(16, rows, LANES // share, share).swapaxes(1, 2).reshape(-1, rows, share)
    core = lax.axis_index("core")
    value = value.reshape(2 * z, 2, rows, share)
    give = low(lax.dynamic_index_in_dim(value, 1 - core, 1, False))
    value = lax.dynamic_index_in_dim(value, core, 1, False) + swap(give, "core").astype(F32)
    return value.reshape(z, 2, rows, share)


def small_cross(value):
    x = lax.axis_index("x")
    give = low(lax.dynamic_index_in_dim(value, 1 - x, 1, False))
    return lax.dynamic_index_in_dim(value, x, 1, False) + swap(give, "x").astype(F32)


def small_sum(value):
    value = line_sum(value)
    return value + swap(value, "y")


def tie(*values):
    return lax.optimization_barrier(values)


def half_cols(right):
    y = lax.axis_index("y")
    half = right.shape[2] // 2
    return piece(right, y, half, 2), swap(piece(right, 1 - y, half, 2), "y")


def quarter_cols(near, across):
    core = lax.axis_index("core")
    both = jnp.stack([near, across], 1)
    quarter = near.shape[2] // 2
    mine = piece(both, core, quarter, 3)
    other = swap(piece(both, 1 - core, quarter, 3), "core")
    both = jnp.stack([mine, other], 2)
    return both.reshape(near.shape[0], -1, quarter)


def spread_cols(part):
    y, core = lax.axis_index("y"), lax.axis_index("core")
    rows = part.shape[0] // 2
    keep = piece(part, core, rows, 0)
    give = piece(part, 1 - core, rows, 0)
    near, across = swap(give, "core"), swap(keep, "y")
    far = lax.ppermute(give, ("y", "core"), [(0, 3), (1, 2), (2, 1), (3, 0)])
    quarters = []
    for q in range(4):
        this, that = jnp.where(core == q % 2, keep, near), jnp.where(core == q % 2, across, far)
        quarters.append(jnp.where(y == q // 2, this, that))
    outs = [
        jnp.concatenate([a[:, i].astype(F32) for a in quarters], 1) for i in range(part.shape[1])
    ]
    return outs


def x_parts(part):
    x, z = lax.axis_index("x"), lax.axis_size("z")
    view = part.reshape(z, 2, -1, part.shape[1])
    give = lax.dynamic_index_in_dim(view, 1 - x, 1, False)
    keep = lax.dynamic_index_in_dim(view, x, 1, False)
    return give.reshape(-1, part.shape[1]), keep.reshape(-1, part.shape[1])


def z_sum(keep, got):
    part = low(keep.astype(F32) + got.astype(F32))
    return lax.psum_scatter(part, "z", scatter_dimension=0, tiled=True)


def grad_call(lefts, rights, block, count, place):
    total, tokens, q = rights.shape
    bounds, arrays, specs = [0], [], []

    def left_spec(low_end, high_end, first, rows):
        def index(i, j, x):
            inside = jnp.logical_and(i >= low_end, i < high_end)
            which = jnp.clip(i, low_end, high_end - 1) - low_end + first
            at = jnp.where(inside, place(j, x[0]), place(jnp.where(i < low_end, 0, count - 1), x[0]))
            return which, 0, at

        return pl.BlockSpec((1, rows, block), index)

    for pieces, first, many in lefts:
        bounds.append(bounds[-1] + many)
        arrays.extend(pieces)
        specs.extend(left_spec(bounds[-2], bounds[-1], first, p.shape[1]) for p in pieces)

    def kernel(x_ref, *refs):
        *a_refs, b_ref, o_ref = refs
        i = pl.program_id(0)
        parts = len(lefts[0][0])
        for k in range(len(lefts)):

            @pl.when(jnp.logical_and(i >= bounds[k], i < bounds[k + 1]))
            def _(mine=a_refs[k * parts : (k + 1) * parts]):
                left = jnp.concatenate([a[0] for a in mine], 0)
                o_ref[...] = low(tn(left, b_ref[0]))

    return pl.pallas_call(
        kernel,
        grid_spec=pltpu.PrefetchScalarGridSpec(
            num_scalar_prefetch=1,
            grid=(total, count),
            in_specs=specs + [pl.BlockSpec((1, tokens, q), lambda i, j, x: (i, 0, 0))],
            out_specs=pl.BlockSpec((block, q), lambda i, j, x: (j, i)),
        ),
        out_shape=jax.ShapeDtypeStruct((count * block, total * q), BF16),
        compiler_params=pltpu.CompilerParams(vmem_limit_bytes=40 << 20),
        cost_estimate=pl.CostEstimate(
            flops=2 * rights.size * count * block, transcendentals=0,
            bytes_accessed=2 * (tokens * total * count * block + rights.size + count * block * total * q),
        ),
        name="weight_grad",
    )(lax.axis_index("x").astype(jnp.int32).reshape(1), *arrays, rights)


def all_rows(lefts, rights):
    return grad_call(lefts, rights, 512, lefts[0][0][0].shape[2] // 512, lambda j, x: j)


def x_rows(lefts, rights):
    z = lax.axis_size("z")
    block = lefts[0][0][0].shape[2] // (2 * z)
    if block % LANES:
        return x_parts(all_rows(lefts, rights))
    give = grad_call(lefts, rights, block, z, lambda j, x: 2 * j + 1 - x)
    return give, grad_call(lefts, rights, block, z, lambda j, x: 2 * j + x)


def group_pieces(values):
    value = jnp.stack(values, 0)
    near = swap(value, "core")
    across = swap(value, "y")
    far = swap(across, "core")
    return value, near, across, far


def group_many(values):
    return jnp.concatenate(group_pieces(values), 1)


def group_sum(value):
    rows = value.shape[0] // 4
    pair = value.reshape(2, 2, rows, -1)
    got = swap(pair[:, 1], "core")
    across = swap(low(pair[1, 0].astype(F32) + got[1].astype(F32)), "y")
    return pair[0, 0].astype(F32) + got[0].astype(F32) + across.astype(F32)


SPAN = 256
GROUP = SPAN // HEAD
SUB = 32


def lane_head(shape, dim):
    return lax.broadcasted_iota(jnp.int32, shape, dim) // HEAD


def head_block(rows, cols):
    shape = (rows, cols)
    return jnp.where(lane_head(shape, 0) == lane_head(shape, 1), 1.0, 0.0).astype(BF16)


def head_sum(value):
    coarse = low(value)
    fine = low(value - coarse.astype(F32))
    ones = head_block(SPAN, SPAN)
    return nn(coarse, ones) + nn(fine, ones)


def exact_product(left, value):
    coarse = low(value)
    rest = value - coarse.astype(F32)
    fine = low(rest)
    last = low(rest - fine.astype(F32))
    return nn(left, coarse) + (nn(left, fine) + nn(left, last))


def triangle(length, keep):
    shape = (length, length)
    row = lax.broadcasted_iota(jnp.int32, shape, 0)
    col = lax.broadcasted_iota(jnp.int32, shape, 1)
    return jnp.where(keep(row, col), 1.0, 0.0).astype(BF16)


def spread_heads(value):
    lane = lane_head(value.shape, 1)
    return jnp.concatenate([low(jnp.where(lane == h, value, 0.0)) for h in range(GROUP)], 0)


def pick_heads(value):
    rows = value.shape[0] // GROUP
    lane = lane_head((rows, SPAN), 1)
    out = value[:rows]
    for h in range(1, GROUP):
        out = jnp.where(lane == h, value[h * rows : (h + 1) * rows], out)
    return out


def widen_state(ref):
    state = jnp.concatenate([ref[0, 0], ref[0, 1]], 1)
    return jnp.concatenate(
        [jnp.where(lane_head(state.shape, 1) == h, state, jnp.zeros_like(state)) for h in range(GROUP)], 0
    )


def store_state(ref, value):
    state = low(pick_heads(value))
    ref[0, 0] = state[:, :LANES]
    ref[0, 1] = state[:, LANES:]


def exclusive_of(inclusive):
    return jnp.concatenate([jnp.zeros_like(inclusive[:1]), inclusive[:-1]], 0)


def cap(value):
    return jnp.exp(jnp.minimum(value, 80.0))


def state_kernel(key_ref, value_ref, log_ref, inc_ref, state_ref, final_ref):
    length = log_ref.shape[0]
    inclusive = exact_product(triangle(length, lambda r, c: r >= c), log_ref[...])
    inc_ref[...] = inclusive
    final = inclusive[length - 1 :]
    weighted = low(key_ref[...] * jnp.exp(final - inclusive))
    store_state(state_ref, tn(weighted, low(value_ref[...])))
    coarse = low(final)
    fine = low(final - coarse.astype(F32))
    rows = jnp.concatenate([coarse, fine, jnp.zeros((14, SPAN), BF16)], 0)
    final_ref[0, 0] = rows[:, :LANES]
    final_ref[0, 1] = rows[:, LANES:]


def sub_block(q, inclusive, exclusive, length):
    start, stop = q * SUB, (q + 1) * SUB
    middle = inclusive[start + SUB // 2 - 1 : start + SUB // 2]
    query = cap(exclusive[start:stop] - middle)
    key = cap(middle - inclusive[:stop])
    shape = (GROUP * SUB, stop)
    row = lax.rem(lax.broadcasted_iota(jnp.int32, shape, 0), SUB) + start
    mask = row > lax.broadcasted_iota(jnp.int32, shape, 1)
    return start, stop, query, key, mask


def wkv_kernel(rec_ref, key_ref, value_ref, inc_ref, state_ref, gate_ref, row_ref, wkv_ref, gated_ref):
    length = rec_ref.shape[0]
    inclusive = inc_ref[...]
    exclusive = exclusive_of(inclusive)
    rec, key, value = rec_ref[...], key_ref[...], value_ref[...]
    value_low = low(value)
    bonus, gain, bias = row_ref[9:10], row_ref[10:11], row_ref[11:12]
    answer = nn(low(rec * jnp.exp(exclusive)), widen_state(state_ref))
    answer = answer + head_sum(rec * bonus * key) * value
    parts = []
    for q in range(length // SUB):
        start, stop, query, fade, mask = sub_block(q, inclusive, exclusive, length)
        left = spread_heads(rec[start:stop] * query)
        scores = nt(left, low(key[:stop] * fade))
        scores = low(jnp.where(mask, scores, 0.0))
        parts.append(pick_heads(nn(scores, value_low[:stop])))
    answer = answer + jnp.concatenate(parts, 0)
    wkv_ref[...] = answer
    centered = answer - head_sum(answer) * (1.0 / HEAD)
    spread = head_sum(centered * centered) * (1.0 / HEAD)
    grouped = centered * lax.rsqrt(spread + 0.00064) * gain + bias
    gate = gate_ref[...]
    gated_ref[...] = low(grouped * gate / (1.0 + jnp.exp(-gate)))


def gate_back_kernel(grad_ref, wkv_ref, gate_ref, rec_ref, inc_ref, row_ref, gwkv_ref, ggate_ref, state_ref, sum_ref):
    gain, bias = row_ref[10:11], row_ref[11:12]
    answer, gate, grad = wkv_ref[...], gate_ref[...], grad_ref[...]
    centered = answer - head_sum(answer) * (1.0 / HEAD)
    rstd = lax.rsqrt(head_sum(centered * centered) * (1.0 / HEAD) + 0.00064)
    hat = centered * rstd
    grouped = hat * gain + bias
    sig = 1.0 / (1.0 + jnp.exp(-gate))
    g_grouped = grad * gate * sig
    ggate_ref[...] = low(grad * grouped * sig * (1.0 + gate * (1.0 - sig)))
    g_gain = jnp.sum(g_grouped * hat, 0, keepdims=True)
    g_bias = jnp.sum(g_grouped, 0, keepdims=True)
    sum_ref[0] = jnp.concatenate([g_gain, g_bias, jnp.zeros((6, SPAN), F32)], 0)
    g_hat = g_grouped * gain
    back = rstd * (
        g_hat - head_sum(g_hat) * (1.0 / HEAD) - hat * (head_sum(g_hat * hat) * (1.0 / HEAD))
    )
    back = low(back)
    gwkv_ref[...] = back
    query = low(rec_ref[...] * jnp.exp(exclusive_of(inc_ref[...])))
    store_state(state_ref, tn(query, back))


def wkv_back_kernel(
    rec_ref, key_ref, value_ref, inc_ref, log_ref, state_ref, gstate_ref, gwkv_ref, row_ref,
    grec_ref, gkey_ref, gvalue_ref, gdecay_ref, sum_ref, key_acc, value_acc, pair_acc,
):
    length = rec_ref.shape[0]
    inclusive = inc_ref[...]
    exclusive = exclusive_of(inclusive)
    final = inclusive[length - 1 :]
    rec, key, value = rec_ref[...], key_ref[...], value_ref[...]
    value_low = low(value)
    grad_low = gwkv_ref[...]
    grad = grad_low.astype(F32)
    bonus = row_ref[9:10]
    state, gstate = widen_state(state_ref), widen_state(gstate_ref)
    pair = head_sum(grad * value)
    shared = pair * bonus
    g_key = shared * rec
    g_value = head_sum(rec * bonus * key) * grad
    g_bonus = jnp.sum(rec * key * pair, 0, keepdims=True)
    fade = jnp.exp(exclusive)
    back = nt(grad_low, state)
    from_state = low(rec * fade).astype(F32) * back
    g_rec = shared * key + fade * back
    fade = jnp.exp(final - inclusive)
    weighted = low(key * fade)
    back = nt(value_low, gstate)
    to_state = weighted.astype(F32) * back
    key_acc[...] = g_key + fade * back
    value_acc[...] = g_value + nn(weighted, gstate)
    pair_acc[...] = jnp.zeros_like(pair_acc)
    rec_parts, own_parts = [], []
    for q in range(length // SUB):
        start, stop, query, fade, mask = sub_block(q, inclusive, exclusive, length)
        left = rec[start:stop] * query
        spread = spread_heads(left)
        right = low(key[:stop] * fade)
        gspread = spread_heads(grad[start:stop])
        scores = low(jnp.where(mask, nt(spread, right), 0.0))
        weight = low(jnp.where(mask, nt(gspread, value_low[:stop]), 0.0))
        back = pick_heads(nn(weight, right))
        rec_parts.append(g_rec[start:stop] + query * back)
        own_parts.append(low(left).astype(F32) * back)
        back = tn(weight, spread)
        key_acc[:stop] += fade * back
        pair_acc[:stop] += right.astype(F32) * back
        value_acc[:stop] += tn(scores, gspread)
    grec_ref[...] = low(jnp.concatenate(rec_parts, 0))
    gkey_ref[...] = low(key_acc[...])
    gvalue_ref[...] = low(value_acc[...])
    inner, pairs = jnp.concatenate(own_parts, 0), pair_acc[...]
    both = head_sum(
        jnp.concatenate([state_ref[0, 0], state_ref[0, 1]], 1).astype(F32)
        * jnp.concatenate([gstate_ref[0, 0], gstate_ref[0, 1]], 1).astype(F32)
    )
    shape = both.shape
    here = lax.rem(lax.broadcasted_iota(jnp.int32, shape, 1), HEAD) == lax.broadcasted_iota(
        jnp.int32, shape, 0
    )
    through = jnp.exp(final) * jnp.sum(jnp.where(here, both, 0.0), 0, keepdims=True)
    later = exact_product(triangle(length, lambda r, c: r < c), inner + from_state - pairs)
    earlier = exact_product(triangle(length, lambda r, c: r > c), to_state)
    g_log = later - pairs + earlier + through
    g_decay = g_log * log_ref[...]
    gdecay_ref[...] = low(g_decay)
    sum_ref[0] = jnp.concatenate(
        [g_bonus, jnp.sum(g_decay, 0, keepdims=True), jnp.zeros((6, SPAN), F32)], 0
    )


def wkv_call(kernel, seqs, ins, outs, name, flops, scratch=()):
    width = ins[0].shape[1]
    length = ins[0].shape[0] // seqs

    def spec(a):
        if len(a.shape) == 4:
            return pl.BlockSpec((1, 2, a.shape[2], LANES), lambda s, g: (s, g, 0, 0))
        if len(a.shape) == 3:
            return pl.BlockSpec((1, 8, SPAN), lambda s, g: (s, 0, g))
        if a.shape[0] == 16:
            return pl.BlockSpec((16, SPAN), lambda s, g: (0, g))
        return pl.BlockSpec((length, SPAN), lambda s, g: (s, g))

    moved = sum(a.size * a.dtype.itemsize for a in ins + outs)
    return pl.pallas_call(
        kernel,
        grid=(seqs, width // SPAN),
        in_specs=[spec(a) for a in ins],
        out_specs=[spec(a) for a in outs],
        out_shape=outs,
        scratch_shapes=scratch,
        compiler_params=pltpu.CompilerParams(vmem_limit_bytes=40 << 20),
        cost_estimate=pl.CostEstimate(flops=flops, transcendentals=0, bytes_accessed=moved),
        name=name,
    )(*ins)


def chain_kernel(first_ref, packed_ref, out_ref, held_fade, *, rows, reverse):
    count = packed_ref.shape[0]
    logs = packed_ref[:, rows : rows + 1], packed_ref[:, rows + 1 : rows + 2]
    shape = (count, rows, LANES)
    lane = lax.rem(lax.broadcasted_iota(jnp.int32, shape, 2), HEAD)
    here = lane == lax.broadcasted_iota(jnp.int32, shape, 1) + first_ref[0]
    ones = head_block(LANES, LANES)
    total = None
    for part in logs:
        part = jnp.where(here, part.astype(F32), 0.0)
        part = nn(low(part.reshape(count * rows, LANES)), ones)
        total = part if total is None else total + part
    held_fade[...] = jnp.exp(total).reshape(shape)

    def one(hop, held):
        b = count - 1 - hop if reverse else hop
        out_ref[b] = low(held)
        return held_fade[b] * held + packed_ref[b, :rows].astype(F32)

    lax.fori_loop(0, count, one, jnp.zeros((rows, LANES), F32))


def chain(state, finals, reverse, beside=None):
    count = lax.axis_size(ALL)
    pairs = state.shape[0] * state.shape[1]
    split = count // pairs
    rows = state.shape[2] // split
    logs = finals.reshape(pairs, finals.shape[2], LANES)
    if split > 1:
        logs = jnp.repeat(logs, split, axis=0)
    packed = jnp.concatenate([state.reshape(count, rows, LANES), logs], 1)
    packed = lax.all_to_all(packed, ALL, 0, 0, tiled=True)
    packed, beside = tie(packed, beside)
    first = lax.rem(lax.axis_index(ALL), split) * rows
    entering = pl.pallas_call(
        lambda *refs: chain_kernel(*refs, rows=rows, reverse=reverse),
        grid_spec=pltpu.PrefetchScalarGridSpec(
            num_scalar_prefetch=1,
            grid=(1,),
            in_specs=[pl.BlockSpec(packed.shape, lambda i, c: (0, 0, 0))],
            out_specs=pl.BlockSpec((count, rows, LANES), lambda i, c: (0, 0, 0)),
            scratch_shapes=[pltpu.VMEM((count, rows, LANES), F32)],
        ),
        out_shape=jax.ShapeDtypeStruct((count, rows, LANES), BF16),
        compiler_params=pltpu.CompilerParams(vmem_limit_bytes=40 << 20),
        name="chain",
    )(first.astype(jnp.int32).reshape(1), packed)
    return lax.all_to_all(entering, ALL, 0, 0, tiled=True).reshape(state.shape), beside


def norm_forward(values, gain, bias):
    mean = jnp.mean(values, -1, keepdims=True)
    centered = values - mean
    rstd = lax.rsqrt(jnp.mean(centered * centered, -1, keepdims=True) + 1e-05)
    hat = centered * rstd
    return hat * gain + bias, hat, rstd


def norm_backward(grad, hat, rstd, gain):
    d = grad * gain
    back = rstd * (
        d - jnp.mean(d, -1, keepdims=True) - hat * jnp.mean(d * hat, -1, keepdims=True)
    )
    return back, jnp.sum(grad * hat, 0, keepdims=True), jnp.sum(grad, 0, keepdims=True)


def prior_of(values, seqs):
    shaped = values.reshape(seqs, -1, values.shape[-1])
    incoming = along(shaped[:, -1], 1)
    return jnp.concatenate([incoming[:, None], shaped[:, :-1]], 1).reshape(values.shape)


def prior_back(grad, seqs):
    shaped = grad.reshape(seqs, -1, grad.shape[-1])
    incoming = along(shaped[:, 0], -1)
    return jnp.concatenate([shaped[:, 1:], incoming[:, None]], 1).reshape(grad.shape)


def stack_nn(value, shards, which, tile=512):
    devices, _, rows, cols = shards.shape

    def kernel(a_ref, w_ref, o_ref):
        w = w_ref[...].reshape(devices * rows, tile)
        o_ref[...] = jnp.dot(a_ref[...], w, preferred_element_type=F32)

    return pl.pallas_call(
        kernel,
        grid=(cols // tile,),
        out_shape=jax.ShapeDtypeStruct((value.shape[0], cols), F32),
        in_specs=[
            pl.BlockSpec(value.shape, lambda j: (0, 0)),
            pl.BlockSpec((devices, 1, rows, tile), lambda j: (0, which, 0, j)),
        ],
        out_specs=pl.BlockSpec((value.shape[0], tile), lambda j: (0, j)),
        compiler_params=pltpu.CompilerParams(vmem_limit_bytes=40 << 20),
        cost_estimate=pl.CostEstimate(
            flops=2 * value.size * cols, transcendentals=0,
            bytes_accessed=2 * value.size + 2 * devices * rows * cols + 4 * value.shape[0] * cols,
        ),
        name="stack_nn",
    )(value, shards)


def stack_nt(value, shards, which, tile=512):
    devices, _, rows, cols = shards.shape
    group = tile // rows

    def kernel(a_ref, w_ref, o_ref):
        w = w_ref[...].reshape(tile, cols)
        o_ref[...] = lax.dot_general(
            a_ref[...], w, (((1,), (1,)), ((), ())), preferred_element_type=F32
        )

    return pl.pallas_call(
        kernel,
        grid=(devices // group,),
        out_shape=jax.ShapeDtypeStruct((value.shape[0], devices * rows), F32),
        in_specs=[
            pl.BlockSpec(value.shape, lambda j: (0, 0)),
            pl.BlockSpec((group, 1, rows, cols), lambda j: (j, which, 0, 0)),
        ],
        out_specs=pl.BlockSpec((value.shape[0], tile), lambda j: (0, j)),
        compiler_params=pltpu.CompilerParams(vmem_limit_bytes=40 << 20),
        cost_estimate=pl.CostEstimate(
            flops=2 * value.size * devices * rows, transcendentals=0,
            bytes_accessed=2 * value.size + 2 * devices * rows * cols
            + 4 * value.shape[0] * devices * rows,
        ),
        name="stack_nt",
    )(value, shards)


def other_half(shards, which):
    core = lax.axis_index("core")
    devices, n, rows, cols = shards.shape
    quarter = cols // 4
    own = lax.dynamic_slice(
        shards, (0, n - 1, 0, (2 * which + core) * quarter), (devices, 1, rows, quarter)
    )
    return swap(own.reshape(devices, rows, quarter), "y")


def places():
    return jnp.stack([lax.axis_index("y"), lax.axis_index("core")]).astype(jnp.int32)


def half_nn(value, shards, which, got, near):
    devices, n, rows, cols = shards.shape
    tile = cols // 4

    def kernel(p_ref, a_ref, w_ref, g_ref, n_ref, o_ref):
        t = pl.program_id(0)

        def put(w):
            w = w.reshape(devices * rows, tile)
            o_ref[...] = jnp.dot(a_ref[...], w, preferred_element_type=F32)

        pl.when(t < 2)(lambda: put(w_ref[...]))
        pl.when(t == 2)(lambda: put(g_ref[...]))
        pl.when(t == 3)(lambda: put(n_ref[...]))

    def out_at(t, p):
        other = 2 * (1 - p[0]) + jnp.where(t == 2, p[1], 1 - p[1])
        return 0, jnp.where(t < 2, 2 * p[0] + t, other)

    whole = pl.BlockSpec(got.shape, lambda t, p: (0, 0, 0))
    return pl.pallas_call(
        kernel,
        grid_spec=pltpu.PrefetchScalarGridSpec(
            num_scalar_prefetch=1,
            grid=(4,),
            in_specs=[
                pl.BlockSpec(value.shape, lambda t, p: (0, 0)),
                pl.BlockSpec(
                    (devices, 1, rows, tile),
                    lambda t, p: (0, n - 1, 0, 2 * which + jnp.minimum(t, 1)),
                ),
                whole,
                whole,
            ],
            out_specs=pl.BlockSpec((value.shape[0], tile), out_at),
        ),
        out_shape=jax.ShapeDtypeStruct((value.shape[0], cols), F32),
        compiler_params=pltpu.CompilerParams(vmem_limit_bytes=48 << 20),
        cost_estimate=pl.CostEstimate(
            flops=2 * value.size * cols, transcendentals=0,
            bytes_accessed=2 * value.size + 2 * devices * rows * cols + 4 * value.shape[0] * cols,
        ),
        name="half_nn",
    )(places(), value, shards, got, near)


def half_nt(value, shards, which, got, near):
    devices, n, rows, cols = shards.shape
    wide = 512
    group = wide // rows
    tile = cols // 4
    tokens = value.shape[0]

    def kernel(p_ref, a_ref, b_ref, c_ref, w_ref, g_ref, n_ref, o_ref):
        total = nt(a_ref[...], w_ref[...].reshape(wide, 2 * tile))
        total = total + nt(b_ref[...], g_ref[...].reshape(wide, tile))
        o_ref[...] = total + nt(c_ref[...], n_ref[...].reshape(wide, tile))

    part = pl.BlockSpec((group, rows, tile), lambda j, p: (j, 0, 0))
    return pl.pallas_call(
        kernel,
        grid_spec=pltpu.PrefetchScalarGridSpec(
            num_scalar_prefetch=1,
            grid=(devices // group,),
            in_specs=[
                pl.BlockSpec((tokens, 2 * tile), lambda j, p: (0, p[0])),
                pl.BlockSpec((tokens, tile), lambda j, p: (0, 2 * (1 - p[0]) + p[1])),
                pl.BlockSpec((tokens, tile), lambda j, p: (0, 2 * (1 - p[0]) + 1 - p[1])),
                pl.BlockSpec((group, 1, rows, 2 * tile), lambda j, p: (j, n - 1, 0, which)),
                part,
                part,
            ],
            out_specs=pl.BlockSpec((tokens, wide), lambda j, p: (0, j)),
        ),
        out_shape=jax.ShapeDtypeStruct((tokens, devices * rows), F32),
        compiler_params=pltpu.CompilerParams(vmem_limit_bytes=40 << 20),
        cost_estimate=pl.CostEstimate(
            flops=2 * value.size * devices * rows, transcendentals=0,
            bytes_accessed=2 * value.size + 2 * devices * rows * cols + 4 * tokens * devices * rows,
        ),
        name="half_nt",
    )(places(), value, value, value, shards, got, near)


TILE = 256


def pack_blocks(shard):
    rows, cols = shard.shape
    return jnp.swapaxes(shard.reshape(rows, cols // TILE, TILE), 0, 1).reshape(-1, TILE)


def ffn_call(kernel, core, grid, ins, specs, outs, out_specs, flops, scratch=(), name=None):
    moved = sum(a.size * a.dtype.itemsize for a in ins[:1] + outs) + flops // 1024
    return pl.pallas_call(
        kernel,
        grid_spec=pltpu.PrefetchScalarGridSpec(
            num_scalar_prefetch=1, grid=grid, in_specs=specs, out_specs=out_specs, scratch_shapes=scratch
        ),
        out_shape=outs,
        compiler_params=pltpu.CompilerParams(vmem_limit_bytes=56 << 20),
        cost_estimate=pl.CostEstimate(flops=flops, transcendentals=0, bytes_accessed=moved),
        name=name,
    )(core.reshape(1), *ins)


class PackedWeights:
    def __init__(self, packed, core, ff, width, half, chips):
        self.packed, self.core = packed, core
        self.devices = packed.shape[0]
        self.rows = width // self.devices
        self.quarter, self.width, self.half, self.chips = ff // 4, width, half, chips
        self.blocks = self.quarter // TILE
        self.fast = half % 16 == 0 and self.rows % 16 == 0 and self.rows == 128

    def _plain(self, start, rows, count):
        part = self.packed[:, start : start + rows * count]
        return part.reshape(-1, count, rows, TILE)

    def plain_key(self):
        start = self.half * (self.width // TILE)
        part = self._plain(start, self.rows, 2 * self.blocks)
        part = piece(part, self.core, self.blocks, 1)
        return jnp.swapaxes(part, 1, 2).reshape(self.width, self.quarter)

    def plain_value(self):
        part = self._plain(0, self.half, self.width // TILE)
        part = lax.dynamic_index_in_dim(
            part.reshape(self.chips, 2, *part.shape[1:]), self.core, 1, False
        )
        return jnp.swapaxes(part, 1, 2).reshape(self.quarter, self.width)

    def plain_rec(self):
        start = self.half * (self.width // TILE) + self.rows * 2 * self.blocks
        part = self._plain(start, self.rows, self.width // TILE)
        return jnp.swapaxes(part, 1, 2).reshape(self.width, self.width)

    def key_forward(self, mix):
        if not self.fast:
            relu = low(jnp.maximum(nn(mix, self.plain_key()), 0.0))
            return relu, low(relu.astype(F32) * relu.astype(F32))
        tokens = mix.shape[0]
        first = self.half * (self.width // TILE) // self.rows

        def kernel(c_ref, a_ref, w_ref, relu_ref, sq_ref):
            w = w_ref[...].reshape(self.width, TILE)
            relu = jnp.maximum(jnp.dot(a_ref[...], w, preferred_element_type=F32), 0.0)
            relu_ref[...] = low(relu)
            sq_ref[...] = low(relu * relu)

        out = jax.ShapeDtypeStruct((tokens, self.quarter), BF16)
        spec = pl.BlockSpec((tokens, TILE), lambda n, c: (0, n))
        return ffn_call(
            kernel, self.core, (self.blocks,), [mix, self.packed],
            [pl.BlockSpec(mix.shape, lambda n, c: (0, 0)),
             pl.BlockSpec((self.devices, self.rows, TILE),
                          lambda n, c: (0, first + c[0] * self.blocks + n, 0))],
            [out, out], [spec, spec], 2 * mix.size * self.quarter, name="key_forward",
        )

    def value_forward(self, squared):
        if not self.fast:
            return low(nn(squared, self.plain_value()))
        tokens = squared.shape[0]
        view = self.packed.reshape(self.chips, 2, *self.packed.shape[1:])

        def kernel(c_ref, a_ref, w_ref, o_ref):
            w = w_ref[...].reshape(self.quarter, TILE)
            o_ref[...] = low(jnp.dot(a_ref[...], w, preferred_element_type=F32))

        return ffn_call(
            kernel, self.core, (self.width // TILE,), [squared, view],
            [pl.BlockSpec(squared.shape, lambda m, c: (0, 0)),
             pl.BlockSpec((self.chips, 1, self.half, TILE), lambda m, c: (0, c[0], m, 0))],
            [jax.ShapeDtypeStruct((tokens, self.width), BF16)],
            [pl.BlockSpec((tokens, TILE), lambda m, c: (0, m))],
            2 * squared.size * self.width, name="value_forward",
        )[0]

    def rec_forward(self, mix):
        if not self.fast:
            return jax.nn.sigmoid(nn(mix, self.plain_rec()))
        tokens = mix.shape[0]
        first = self.packed.shape[1] // self.rows - self.width // TILE

        def kernel(c_ref, a_ref, w_ref, o_ref):
            w = w_ref[...].reshape(self.width, TILE)
            o_ref[...] = jax.nn.sigmoid(jnp.dot(a_ref[...], w, preferred_element_type=F32))

        return ffn_call(
            kernel, self.core, (self.width // TILE,), [mix, self.packed],
            [pl.BlockSpec(mix.shape, lambda m, c: (0, 0)),
             pl.BlockSpec((self.devices, self.rows, TILE), lambda m, c: (0, first + m, 0))],
            [jax.ShapeDtypeStruct((tokens, self.width), F32)],
            [pl.BlockSpec((tokens, TILE), lambda m, c: (0, m))],
            2 * mix.size * self.width, name="rec_forward",
        )[0]

    def value_backward(self, grad, relu):
        if not self.fast:
            return low(nt(grad, self.plain_value()) * 2.0 * relu.astype(F32))
        tokens = grad.shape[0]
        view = self.packed.reshape(self.chips, 2, *self.packed.shape[1:])
        count = self.width // TILE
        part = self.chips // 2

        def kernel(c_ref, a_ref, r_ref, w_ref, o_ref, flat):
            w = w_ref[...].reshape(part, count, self.half, TILE)
            for m in range(count):
                flat[:, m * TILE : (m + 1) * TILE] = w[:, m].reshape(part * self.half, TILE)
            back = lax.dot_general(
                a_ref[...], flat[...], (((1,), (1,)), ((), ())), preferred_element_type=F32
            )
            o_ref[...] = low(back * 2.0 * r_ref[...].astype(F32))

        wide = part * self.half
        return ffn_call(
            kernel, self.core, (2,), [grad, relu, view],
            [pl.BlockSpec(grad.shape, lambda i, c: (0, 0)),
             pl.BlockSpec((tokens, wide), lambda i, c: (0, i)),
             pl.BlockSpec((part, 1, count * self.half, TILE), lambda i, c: (i, c[0], 0, 0))],
            [jax.ShapeDtypeStruct((tokens, self.quarter), BF16)],
            [pl.BlockSpec((tokens, wide), lambda i, c: (0, i))],
            2 * grad.size * self.quarter,
            scratch=(pltpu.VMEM((wide, self.width), BF16),), name="value_backward",
        )[0]

    def key_backward(self, grad):
        if not self.fast:
            return low(nt(grad, self.plain_key()))
        tokens = grad.shape[0]
        part = 4
        rows = self.blocks * self.rows
        first = self.half * (self.width // TILE) // rows

        def kernel(c_ref, a_ref, w_ref, o_ref, flat):
            w = w_ref[...].reshape(part, self.blocks, self.rows, TILE)
            for n in range(self.blocks):
                flat[:, n * TILE : (n + 1) * TILE] = w[:, n].reshape(part * self.rows, TILE)
            o_ref[...] = low(lax.dot_general(
                a_ref[...], flat[...], (((1,), (1,)), ((), ())), preferred_element_type=F32
            ))

        wide = part * self.rows
        return ffn_call(
            kernel, self.core, (self.devices // part,), [grad, self.packed],
            [pl.BlockSpec(grad.shape, lambda i, c: (0, 0)),
             pl.BlockSpec((part, rows, TILE), lambda i, c: (i, first + c[0], 0))],
            [jax.ShapeDtypeStruct((tokens, self.width), BF16)],
            [pl.BlockSpec((tokens, wide), lambda i, c: (0, i))],
            2 * grad.size * self.width,
            scratch=(pltpu.VMEM((wide, self.quarter), BF16),), name="key_backward",
        )[0]

    def rec_backward(self, grad):
        if not self.fast:
            return nt(grad, self.plain_rec())
        tokens = grad.shape[0]
        part, count = 4, self.width // TILE
        rows = count * self.rows // 2
        first = self.packed.shape[1] // rows - 2

        def kernel(c_ref, a_ref, w_ref, v_ref, o_ref, flat):
            for k, ref in enumerate((w_ref, v_ref)):
                w = ref[...].reshape(part, count // 2, self.rows, TILE)
                for n in range(count // 2):
                    m = k * (count // 2) + n
                    flat[:, m * TILE : (m + 1) * TILE] = w[:, n].reshape(part * self.rows, TILE)
            o_ref[...] = lax.dot_general(
                a_ref[...], flat[...], (((1,), (1,)), ((), ())), preferred_element_type=F32
            )

        wide = part * self.rows
        return ffn_call(
            kernel, self.core, (self.devices // part,), [grad, self.packed, self.packed],
            [pl.BlockSpec(grad.shape, lambda i, c: (0, 0)),
             pl.BlockSpec((part, rows, TILE), lambda i, c: (i, first, 0)),
             pl.BlockSpec((part, rows, TILE), lambda i, c: (i, first + 1, 0))],
            [jax.ShapeDtypeStruct((tokens, self.width), F32)],
            [pl.BlockSpec((tokens, wide), lambda i, c: (0, i))],
            2 * grad.size * self.width,
            scratch=(pltpu.VMEM((wide, self.width), BF16),), name="rec_backward",
        )[0]


def body(tokens, att_w, down_w, up_w, key_w, value_w, rec_w, vectors, out_grad):
    seqs, length, width = tokens.shape
    total = seqs * length
    y, core = lax.axis_index("y"), lax.axis_index("core")
    zs = lax.axis_size("z")
    ff = key_w.shape[1]
    share = value_w.shape[0]
    half = share // 2
    quarter = ff // 4

    def rows(v):
        return v.reshape(total, width)

    def columns(shard):
        gathered = lax.all_gather(shard, WIDE, axis=0)
        return jnp.swapaxes(gathered, 0, 1).reshape(shard.shape[0], width)

    cols = up_w.shape[0]
    up_vec = columns(jnp.concatenate([vectors, up_w], 0))
    vec, up = up_vec[:16].astype(F32), up_vec[16:]
    down_t = columns(down_w.T)
    halves = [piece(att_w[i], y, width // 2, 1) for i in (3, 4)]
    w_att = jnp.concatenate([att_w[:3], jnp.concatenate(halves, 1)[None]], 0)
    w_att = lax.all_gather(w_att, WIDE, axis=0)
    key_sh = key_w.reshape(-1, zs, 2, 2, 2, half)
    key_sh = lax.dynamic_index_in_dim(key_sh, y, 4, False)
    key_sh = key_sh.transpose(0, 3, 1, 2, 4).reshape(-1, 2 * quarter)
    packed = jnp.concatenate(
        [pack_blocks(piece(value_w, y, half, 0)), pack_blocks(key_sh), pack_blocks(rec_w)], 0
    )
    packed = lax.all_gather(packed, WIDE, axis=0)

    x = rows(tokens.astype(F32))
    normed, hat, rstd = norm_forward(x, vec[0], vec[1])
    delta = prior_of(normed, seqs) - normed
    mix_low = low(normed + delta * vec[2])
    tanh_mix = jnp.tanh(nt(mix_low, down_t[:MIXCOLS]))
    hidden = low(tanh_mix)
    hid = [hidden[:, i * RANK : (i + 1) * RANK] for i in range(5)]
    ups = [up[i * RANK : (i + 1) * RANK] for i in range(5)]
    mixed = [low(normed + delta * (vec[3 + i] + nn(hid[i], ups[i]))) for i in range(5)]
    decay_in, key_in, value_in, rec_in, gate_in = mixed
    tanh_decay = jnp.tanh(nt(decay_in, down_t[MIXCOLS:]))
    hidden_decay = low(tanh_decay)
    logdecay = -jnp.exp(vec[8] + nn(hidden_decay, up[MIXCOLS:]))
    mix_all = group_pieces([gate_in, rec_in, key_in, value_in])
    w_att, mix_all = tie(w_att, mix_all)
    gate_other = other_half(w_att, 0)
    out_other = other_half(w_att, 1)
    keys = stack_nn(key_in, w_att, 1)
    values = stack_nn(value_in, w_att, 2)
    shaped = jax.ShapeDtypeStruct
    flat, flat_low = shaped((total, width), F32), shaped((total, width), BF16)
    states = shaped((seqs, width // LANES, HEAD, LANES), BF16)
    finals = shaped((seqs, width // LANES, 16, LANES), BF16)
    sums = shaped((seqs, 8, width), F32)
    unit = 2 * total * width
    inclusive, state, final = wkv_call(
        state_kernel, seqs, [keys, values, logdecay], [flat, states, finals], "wkv_state", unit * 512
    )
    carried, gate_other = chain(state, final, False, gate_other)
    gate_other = (gate_other, swap(gate_other, "core"))
    carried, out_other = tie(carried, out_other)
    out_other = (out_other, swap(out_other, "core"))
    recept = stack_nn(rec_in, w_att, 0)
    gate_pre = half_nn(gate_in, w_att, 0, *gate_other)
    wkv, gated = wkv_call(
        wkv_kernel, seqs, [recept, keys, values, inclusive, carried, gate_pre, vec], [flat, flat_low],
        "wkv_forward", unit * 1536,
    )
    first_sum = x + half_nn(gated, w_att, 1, *out_other)

    normed_two, hat_two, rstd_two = norm_forward(first_sum, vec[12], vec[13])
    delta_two = prior_of(normed_two, seqs) - normed_two
    key_mix = low(normed_two + delta_two * vec[14])
    rec_mix = low(normed_two + delta_two * vec[15])
    key_all = group_many([key_mix])[0]
    gated_all = group_pieces([gated])
    packed, key_all, gated_all = tie(packed, key_all, gated_all)
    ffn = PackedWeights(packed, core, ff, width, half, 2 * zs)
    relu, squared = ffn.key_forward(key_all)
    value_out = group_sum(ffn.value_forward(squared))
    rec_gate = ffn.rec_forward(rec_mix)
    block_out = low(first_sum + rec_gate * value_out).reshape(tokens.shape)

    g = rows(out_grad.astype(F32))
    grad_value = low(g * rec_gate)
    grad_gate_in = low(g * value_out * rec_gate * (1.0 - rec_gate))
    value_all = group_many([grad_value])[0]
    value_part = low(tn(squared, value_all)).reshape(-1, half, width)
    value_part, value_all = tie(value_part, value_all)
    value_part = lax.psum_scatter(value_part, ("z", "x"), scatter_dimension=0, tiled=True)[0]
    grad_key_pre = ffn.value_backward(value_all, relu)
    g_key_mix = ffn.key_backward(grad_key_pre)
    grad_key_pre, g_key_mix = tie(grad_key_pre, g_key_mix)
    key_part = low(tn(key_all, grad_key_pre))
    key_part = lax.psum_scatter(key_part, ("z", "x"), scatter_dimension=0, tiled=True)
    g_key_mix = group_sum(g_key_mix)
    g_rec_mix = ffn.rec_backward(grad_gate_in)

    g_prior = prior_back(g_key_mix * vec[14] + g_rec_mix * vec[15], seqs)
    g_normed_two = g_key_mix * (1.0 - vec[14]) + g_rec_mix * (1.0 - vec[15]) + g_prior
    g_maa_key = jnp.sum(g_key_mix * delta_two, 0, keepdims=True)
    g_maa_rec = jnp.sum(g_rec_mix * delta_two, 0, keepdims=True)
    back_two, g_gain_two, g_bias_two = norm_backward(g_normed_two, hat_two, rstd_two, vec[12])
    grad_first = g + back_two

    grad_att = low(grad_first)
    g_wkv, g_gate_low, g_state, gate_sums = wkv_call(
        gate_back_kernel, seqs,
        [half_nt(grad_att, w_att, 1, *out_other), wkv, gate_pre, recept, inclusive, vec],
        [flat_low, flat_low, states, sums], "gate_backward", unit * 1536,
    )
    g_state_out, (rights, rec_low) = chain(
        g_state, final, True, ([grad_gate_in, grad_att, g_gate_low], rec_mix)
    )
    side_near, side_across = half_cols(jnp.stack(rights, 0))
    rec_all = group_pieces([rec_low])
    g_state_out, value_part = tie(g_state_out, value_part)
    g_rec, g_key, g_val, g_decay_low, wkv_sums = wkv_call(
        wkv_back_kernel, seqs,
        [recept, keys, values, inclusive, logdecay, carried, g_state_out, g_wkv, vec],
        [flat_low, flat_low, flat_low, flat_low, sums], "wkv_backward", unit * 4096,
        scratch=[pltpu.VMEM((length, SPAN), F32)] * 3,
    )
    gate_sums, wkv_sums = jnp.sum(gate_sums, 0), jnp.sum(wkv_sums, 0)
    projs = [g_rec, g_key, g_val, g_gate_low]
    main_near, main_across = half_cols(jnp.stack([g_rec, g_key, g_val], 0))
    main_near, side_across, rec_all = tie(main_near, side_across, rec_all)
    side_lefts = [(rec_all, 0, 1), (gated_all, 0, 1), (mix_all, 0, 1)]
    side_give, side_keep = x_rows(side_lefts, quarter_cols(side_near, side_across))
    side_got = swap(side_give, "x")
    main_across, side_keep = tie(main_across, side_keep)
    main = all_rows([(mix_all, 1, 3)], quarter_cols(main_near, main_across))
    main, g_rec, g_key, g_val, g_gate_low, g_decay_low, key_part = tie(
        main, g_rec, g_key, g_val, g_gate_low, g_decay_low, key_part
    )
    main = lax.psum_scatter(main, ("z", "x"), scatter_dimension=0, tiled=True)
    projs = [g_rec, g_key, g_val, g_gate_low]

    decay_up_grad = tn(hidden_decay, g_decay_low)
    g_pre_decay = low(nt(g_decay_low, up[MIXCOLS:]) * (1.0 - tanh_decay * tanh_decay))
    decay_down_grad = tn(g_pre_decay, decay_in)
    g_mixed = [
        nn(g_pre_decay, down_t[MIXCOLS:]),
        stack_nt(projs[1], w_att, 1),
        stack_nt(projs[2], w_att, 2),
        stack_nt(projs[0], w_att, 0),
        half_nt(projs[3], w_att, 0, *gate_other),
    ]
    g_normed = g_prior_sum = None
    maa_rows, up_grads, hid_grads = [], [], []
    for i in range(5):
        offset = vec[3 + i] + nn(hid[i], ups[i])
        g_off = g_mixed[i] * delta
        maa_rows.append(jnp.sum(g_off, 0, keepdims=True))
        off_low = low(g_off)
        up_grads.append(tn(hid[i], off_low))
        hid_grads.append(nt(off_low, ups[i]))
        here = g_mixed[i] * (1.0 - offset)
        back = g_mixed[i] * offset
        g_normed = here if g_normed is None else g_normed + here
        g_prior_sum = back if g_prior_sum is None else g_prior_sum + back
    g_pre_mix = low(jnp.concatenate(hid_grads, 1) * (1.0 - tanh_mix * tanh_mix))
    g_pre_mix, value_part, key_part = tie(g_pre_mix, value_part, key_part)
    mix_down_grad = tn(g_pre_mix, mix_low)
    g_first_mix = nn(g_pre_mix, down_t[:MIXCOLS])
    maa_first = jnp.sum(g_first_mix * delta, 0, keepdims=True)
    g_prior_sum = g_prior_sum + g_first_mix * vec[2]
    g_normed = g_normed + g_first_mix * (1.0 - vec[2]) + prior_back(g_prior_sum, seqs)
    back_one, g_gain, g_bias = norm_backward(g_normed, hat, rstd, vec[0])
    input_grad = (grad_first + back_one).reshape(tokens.shape)

    vec_rows = (
        [g_gain, g_bias, maa_first] + maa_rows
        + [wkv_sums[1:2], wkv_sums[0:1], gate_sums[0:1], gate_sums[1:2], g_gain_two, g_bias_two,
           g_maa_key, g_maa_rec]
    )
    packed = pack_columns(up_grads + [decay_up_grad, mix_down_grad, decay_down_grad] + vec_rows)
    first = y == 0
    other = swap(value_part, "y")
    value_share = jnp.concatenate(
        [jnp.where(first, value_part, other), jnp.where(first, other, value_part)], 0
    ).astype(F32)
    key_share = spread_cols(key_part[:, None])[0].reshape(-1, 2, 2, zs, 2, half)
    key_share = key_share.transpose(0, 3, 4, 2, 1, 5).reshape(-1, ff)
    packed, key_share, value_share, side_got = tie(packed, key_share, value_share, side_got)
    side = low(side_keep.astype(F32) + side_got.astype(F32))
    side = side.reshape(zs, -1, side.shape[1])
    moving = line_step(side, 1, None)
    packed, moving, main = tie(small_core(packed), moving, main)
    for t in range(2, zs - 1):
        moving = line_step(side, t, moving)
    packed, moving = tie(small_cross(packed), moving)
    side = low(line_end(side, line_step(side, zs - 1, moving)))
    late = spread_cols(main.reshape(main.shape[0], 3, -1))
    early = spread_cols(side.reshape(side.shape[0], 3, -1))
    packed = small_sum(packed)
    rec_share = early[0]
    att_share = jnp.stack(late + [early[2], early[1]], 0)
    return (
        block_out, input_grad, att_share, packed[cols : 2 * cols].T, packed[:cols],
        key_share, value_share, rec_share, packed[2 * cols :],
    )


def solution(mesh):
    seq, wide = mesh.devices.shape
    fine = Mesh(mesh.devices.reshape(seq, wide // 4, 2, 2), ALL)
    token = P(None, ALL, None)
    by_row, by_col, stacked = P(WIDE, None), P(None, WIDE), P(None, WIDE, None)
    return jax.shard_map(
        body,
        mesh=fine,
        in_specs=(token, stacked, by_row, by_col, by_row, by_row, by_row, by_col, token),
        out_specs=(token, token, stacked, by_row, by_col, by_row, by_row, by_row, by_col),
        check_vma=False,
    )
```

```python
import jax
import jax.numpy as jnp
from jax import lax
from jax.experimental import pallas as pl
from jax.experimental.pallas import tpu as pltpu
from jax.sharding import Mesh
from jax.sharding import PartitionSpec as P

HEAD = 64
RANK = 32
MIXCOLS = 5 * RANK
LANES = 128
F32, BF16 = jnp.float32, jnp.bfloat16
WIDE = ("z", "x", "core")
ALL = ("y", "z", "x", "core")


def nn(a, b):
    return jnp.dot(a, b, preferred_element_type=F32)


def nt(a, b):
    return lax.dot_general(a, b, (((1,), (1,)), ((), ())), preferred_element_type=F32)


def tn(a, b):
    return lax.dot_general(a, b, (((0,), (0,)), ((), ())), preferred_element_type=F32)


def low(a):
    return a.astype(BF16)


def swap(value, axis):
    return lax.ppermute(value, axis, [(0, 1), (1, 0)])


def along(value, step):
    count = lax.axis_size(ALL)
    if step > 0:
        pairs = [(i, i + 1) for i in range(count - 1)]
    else:
        pairs = [(i + 1, i) for i in range(count - 1)]
    return lax.ppermute(value, ALL, pairs)


def piece(value, index, size, axis):
    start = [0] * value.ndim
    start[axis] = index * size
    shape = list(value.shape)
    shape[axis] = size
    return lax.dynamic_slice(value, start, shape)


def line_own(block, index):
    count = lax.axis_size("z")
    return lax.dynamic_index_in_dim(block, jnp.clip(index, 0, count - 1), 0, False).astype(F32)


def line_step(block, t, moving):
    count, place = lax.axis_size("z"), lax.axis_index("z")
    right = line_own(block, count - t + place)
    left = line_own(block, place + t - count)
    if moving is not None:
        right, left = right + moving[0].astype(F32), left + moving[1].astype(F32)
    up = lax.ppermute(low(right), "z", [(i, i + 1) for i in range(count - 1) if i <= t - 1])
    down = lax.ppermute(
        low(left), "z", [(i, i - 1) for i in range(1, count) if count - 1 - i <= t - 1]
    )
    return up, down


def line_end(block, moving):
    own = line_own(block, lax.axis_index("z"))
    return own + moving[0].astype(F32) + moving[1].astype(F32)


def line_sum(block):
    moving = None
    for t in range(1, lax.axis_size("z")):
        moving = line_step(block, t, moving)
    return line_end(block, moving)


def pack_columns(parts):
    width = parts[0].shape[1]
    counts = [p.shape[0] for p in parts]
    rows = sum(counts)
    step = 4
    block = step * LANES

    def kernel(*refs):
        out = refs[-1]
        start = 0
        while start < len(counts):
            take, n = [], 0
            while n == 0 or n % 8:
                take.append(refs[start][...])
                n += counts[start]
                start += 1
            first = sum(counts[: start - len(take)])
            rows_here = take[0] if len(take) == 1 else jnp.concatenate(take, 0)
            for b in range(step):
                out[b, first : first + n] = rows_here[:, b * LANES : (b + 1) * LANES]

    return pl.pallas_call(
        kernel,
        grid=(width // block,),
        in_specs=[pl.BlockSpec((c, block), lambda j: (0, j)) for c in counts],
        out_specs=pl.BlockSpec((step, rows, LANES), lambda j: (j, 0, 0)),
        out_shape=jax.ShapeDtypeStruct((width // LANES, rows, LANES), F32),
        compiler_params=pltpu.CompilerParams(vmem_limit_bytes=40 << 20),
        name="pack_columns",
    )(*parts)


def small_core(value):
    z, rows = lax.axis_size("z"), value.shape[1]
    share = 16 * LANES // (4 * z)
    if share != LANES:
        value = value.reshape(16, rows, LANES // share, share).swapaxes(1, 2).reshape(-1, rows, share)
    core = lax.axis_index("core")
    value = value.reshape(2 * z, 2, rows, share)
    give = low(lax.dynamic_index_in_dim(value, 1 - core, 1, False))
    value = lax.dynamic_index_in_dim(value, core, 1, False) + swap(give, "core").astype(F32)
    return value.reshape(z, 2, rows, share)


def small_cross(value):
    x = lax.axis_index("x")
    give = low(lax.dynamic_index_in_dim(value, 1 - x, 1, False))
    return lax.dynamic_index_in_dim(value, x, 1, False) + swap(give, "x").astype(F32)


def small_sum(value):
    count, place = lax.axis_size("z"), lax.axis_index("z")
    reach = count // 2
    while reach:
        value = value.reshape(2, reach, *value.shape[1:])
        bit = lax.rem(place // reach, 2)
        give = low(lax.dynamic_index_in_dim(value, 1 - bit, 0, False))
        got = lax.ppermute(give, "z", [(i, i ^ reach) for i in range(count)])
        value = lax.dynamic_index_in_dim(value, bit, 0, False) + got.astype(F32)
        reach //= 2
    value = value[0]
    return value + swap(value, "y")


def tie(*values):
    return lax.optimization_barrier(values)


def half_cols(right):
    y = lax.axis_index("y")
    half = right.shape[2] // 2
    return piece(right, y, half, 2), swap(piece(right, 1 - y, half, 2), "y")


def quarter_cols(near, across):
    core = lax.axis_index("core")
    both = jnp.stack([near, across], 1)
    quarter = near.shape[2] // 2
    mine = piece(both, core, quarter, 3)
    other = swap(piece(both, 1 - core, quarter, 3), "core")
    both = jnp.stack([mine, other], 2)
    return both.reshape(near.shape[0], -1, quarter)


def spread_cols(part):
    y, core = lax.axis_index("y"), lax.axis_index("core")
    rows = part.shape[0] // 2
    keep = piece(part, core, rows, 0)
    give = piece(part, 1 - core, rows, 0)
    near, across = swap(give, "core"), swap(keep, "y")
    far = lax.ppermute(give, ("y", "core"), [(0, 3), (1, 2), (2, 1), (3, 0)])
    quarters = []
    for q in range(4):
        this, that = jnp.where(core == q % 2, keep, near), jnp.where(core == q % 2, across, far)
        quarters.append(jnp.where(y == q // 2, this, that))
    outs = [
        jnp.concatenate([a[:, i].astype(F32) for a in quarters], 1) for i in range(part.shape[1])
    ]
    return outs


def x_parts(part):
    x, z = lax.axis_index("x"), lax.axis_size("z")
    view = part.reshape(z, 2, -1, part.shape[1])
    give = lax.dynamic_index_in_dim(view, 1 - x, 1, False)
    keep = lax.dynamic_index_in_dim(view, x, 1, False)
    return give.reshape(-1, part.shape[1]), keep.reshape(-1, part.shape[1])


def z_sum(keep, got):
    part = low(keep.astype(F32) + got.astype(F32))
    return lax.psum_scatter(part, "z", scatter_dimension=0, tiled=True)


def grad_call(lefts, rights, block, count, place):
    total, tokens, q = rights.shape
    bounds, arrays, specs = [0], [], []

    def left_spec(low_end, high_end, first, rows):
        def index(i, j, x):
            inside = jnp.logical_and(i >= low_end, i < high_end)
            which = jnp.clip(i, low_end, high_end - 1) - low_end + first
            at = jnp.where(inside, place(j, x[0]), place(jnp.where(i < low_end, 0, count - 1), x[0]))
            return which, 0, at

        return pl.BlockSpec((1, rows, block), index)

    for pieces, first, many in lefts:
        bounds.append(bounds[-1] + many)
        arrays.extend(pieces)
        specs.extend(left_spec(bounds[-2], bounds[-1], first, p.shape[1]) for p in pieces)

    def kernel(x_ref, *refs):
        *a_refs, b_ref, o_ref = refs
        i = pl.program_id(0)
        parts = len(lefts[0][0])
        for k in range(len(lefts)):

            @pl.when(jnp.logical_and(i >= bounds[k], i < bounds[k + 1]))
            def _(mine=a_refs[k * parts : (k + 1) * parts]):
                left = jnp.concatenate([a[0] for a in mine], 0)
                o_ref[...] = low(tn(left, b_ref[0]))

    return pl.pallas_call(
        kernel,
        grid_spec=pltpu.PrefetchScalarGridSpec(
            num_scalar_prefetch=1,
            grid=(total, count),
            in_specs=specs + [pl.BlockSpec((1, tokens, q), lambda i, j, x: (i, 0, 0))],
            out_specs=pl.BlockSpec((block, q), lambda i, j, x: (j, i)),
        ),
        out_shape=jax.ShapeDtypeStruct((count * block, total * q), BF16),
        compiler_params=pltpu.CompilerParams(vmem_limit_bytes=40 << 20),
        cost_estimate=pl.CostEstimate(
            flops=2 * rights.size * count * block, transcendentals=0,
            bytes_accessed=2 * (tokens * total * count * block + rights.size + count * block * total * q),
        ),
        name="weight_grad",
    )(lax.axis_index("x").astype(jnp.int32).reshape(1), *arrays, rights)


def all_rows(lefts, rights):
    return grad_call(lefts, rights, 512, lefts[0][0][0].shape[2] // 512, lambda j, x: j)


def x_rows(lefts, rights):
    z = lax.axis_size("z")
    block = lefts[0][0][0].shape[2] // (2 * z)
    if block % LANES:
        return x_parts(all_rows(lefts, rights))
    give = grad_call(lefts, rights, block, z, lambda j, x: 2 * j + 1 - x)
    return give, grad_call(lefts, rights, block, z, lambda j, x: 2 * j + x)


def group_pieces(values):
    value = jnp.stack(values, 0)
    near = swap(value, "core")
    across = swap(value, "y")
    far = swap(across, "core")
    return value, near, across, far


def group_many(values):
    return jnp.concatenate(group_pieces(values), 1)


def group_sum(value):
    rows = value.shape[0] // 4
    pair = value.reshape(2, 2, rows, -1)
    got = swap(pair[:, 1], "core")
    across = swap(low(pair[1, 0].astype(F32) + got[1].astype(F32)), "y")
    return pair[0, 0].astype(F32) + got[0].astype(F32) + across.astype(F32)


SPAN = 256
GROUP = SPAN // HEAD
SUB = 32


def lane_head(shape, dim):
    return lax.broadcasted_iota(jnp.int32, shape, dim) // HEAD


def head_block(rows, cols):
    shape = (rows, cols)
    return jnp.where(lane_head(shape, 0) == lane_head(shape, 1), 1.0, 0.0).astype(BF16)


def head_sum(value):
    coarse = low(value)
    fine = low(value - coarse.astype(F32))
    ones = head_block(SPAN, SPAN)
    return nn(coarse, ones) + nn(fine, ones)


def exact_product(left, value):
    coarse = low(value)
    rest = value - coarse.astype(F32)
    fine = low(rest)
    last = low(rest - fine.astype(F32))
    return nn(left, coarse) + (nn(left, fine) + nn(left, last))


def triangle(length, keep):
    shape = (length, length)
    row = lax.broadcasted_iota(jnp.int32, shape, 0)
    col = lax.broadcasted_iota(jnp.int32, shape, 1)
    return jnp.where(keep(row, col), 1.0, 0.0).astype(BF16)


def spread_heads(value):
    lane = lane_head(value.shape, 1)
    return jnp.concatenate([low(jnp.where(lane == h, value, 0.0)) for h in range(GROUP)], 0)


def pick_heads(value):
    rows = value.shape[0] // GROUP
    lane = lane_head((rows, SPAN), 1)
    out = value[:rows]
    for h in range(1, GROUP):
        out = jnp.where(lane == h, value[h * rows : (h + 1) * rows], out)
    return out


def widen_state(ref):
    state = jnp.concatenate([ref[0, 0], ref[0, 1]], 1)
    return jnp.concatenate(
        [jnp.where(lane_head(state.shape, 1) == h, state, jnp.zeros_like(state)) for h in range(GROUP)], 0
    )


def store_state(ref, value):
    state = low(pick_heads(value))
    ref[0, 0] = state[:, :LANES]
    ref[0, 1] = state[:, LANES:]


def exclusive_of(inclusive):
    return jnp.concatenate([jnp.zeros_like(inclusive[:1]), inclusive[:-1]], 0)


def cap(value):
    return jnp.exp(jnp.minimum(value, 80.0))


def state_kernel(key_ref, value_ref, log_ref, inc_ref, state_ref, final_ref):
    length = log_ref.shape[0]
    inclusive = exact_product(triangle(length, lambda r, c: r >= c), log_ref[...])
    inc_ref[...] = inclusive
    final = inclusive[length - 1 :]
    weighted = low(key_ref[...] * jnp.exp(final - inclusive))
    store_state(state_ref, tn(weighted, low(value_ref[...])))
    coarse = low(final)
    fine = low(final - coarse.astype(F32))
    rows = jnp.concatenate([coarse, fine, jnp.zeros((14, SPAN), BF16)], 0)
    final_ref[0, 0] = rows[:, :LANES]
    final_ref[0, 1] = rows[:, LANES:]


def sub_block(q, inclusive, exclusive, length):
    start, stop = q * SUB, (q + 1) * SUB
    middle = inclusive[start + SUB // 2 - 1 : start + SUB // 2]
    query = cap(exclusive[start:stop] - middle)
    key = cap(middle - inclusive[:stop])
    shape = (GROUP * SUB, stop)
    row = lax.rem(lax.broadcasted_iota(jnp.int32, shape, 0), SUB) + start
    mask = row > lax.broadcasted_iota(jnp.int32, shape, 1)
    return start, stop, query, key, mask


def wkv_kernel(rec_ref, key_ref, value_ref, inc_ref, state_ref, gate_ref, row_ref, wkv_ref, gated_ref):
    length = rec_ref.shape[0]
    inclusive = inc_ref[...]
    exclusive = exclusive_of(inclusive)
    rec, key, value = rec_ref[...], key_ref[...], value_ref[...]
    value_low = low(value)
    bonus, gain, bias = row_ref[9:10], row_ref[10:11], row_ref[11:12]
    answer = nn(low(rec * jnp.exp(exclusive)), widen_state(state_ref))
    answer = answer + head_sum(rec * bonus * key) * value
    parts = []
    for q in range(length // SUB):
        start, stop, query, fade, mask = sub_block(q, inclusive, exclusive, length)
        left = spread_heads(rec[start:stop] * query)
        scores = nt(left, low(key[:stop] * fade))
        scores = low(jnp.where(mask, scores, 0.0))
        parts.append(pick_heads(nn(scores, value_low[:stop])))
    answer = answer + jnp.concatenate(parts, 0)
    wkv_ref[...] = answer
    centered = answer - head_sum(answer) * (1.0 / HEAD)
    spread = head_sum(centered * centered) * (1.0 / HEAD)
    grouped = centered * lax.rsqrt(spread + 0.00064) * gain + bias
    gate = gate_ref[...]
    gated_ref[...] = low(grouped * gate / (1.0 + jnp.exp(-gate)))


def gate_back_kernel(grad_ref, wkv_ref, gate_ref, rec_ref, inc_ref, row_ref, gwkv_ref, ggate_ref, state_ref, sum_ref):
    gain, bias = row_ref[10:11], row_ref[11:12]
    answer, gate, grad = wkv_ref[...], gate_ref[...], grad_ref[...]
    centered = answer - head_sum(answer) * (1.0 / HEAD)
    rstd = lax.rsqrt(head_sum(centered * centered) * (1.0 / HEAD) + 0.00064)
    hat = centered * rstd
    grouped = hat * gain + bias
    sig = 1.0 / (1.0 + jnp.exp(-gate))
    g_grouped = grad * gate * sig
    ggate_ref[...] = low(grad * grouped * sig * (1.0 + gate * (1.0 - sig)))
    g_gain = jnp.sum(g_grouped * hat, 0, keepdims=True)
    g_bias = jnp.sum(g_grouped, 0, keepdims=True)
    sum_ref[0] = jnp.concatenate([g_gain, g_bias, jnp.zeros((6, SPAN), F32)], 0)
    g_hat = g_grouped * gain
    back = rstd * (
        g_hat - head_sum(g_hat) * (1.0 / HEAD) - hat * (head_sum(g_hat * hat) * (1.0 / HEAD))
    )
    back = low(back)
    gwkv_ref[...] = back
    query = low(rec_ref[...] * jnp.exp(exclusive_of(inc_ref[...])))
    store_state(state_ref, tn(query, back))


def wkv_back_kernel(
    rec_ref, key_ref, value_ref, inc_ref, log_ref, state_ref, gstate_ref, gwkv_ref, row_ref,
    grec_ref, gkey_ref, gvalue_ref, gdecay_ref, sum_ref, key_acc, value_acc, pair_acc,
):
    length = rec_ref.shape[0]
    inclusive = inc_ref[...]
    exclusive = exclusive_of(inclusive)
    final = inclusive[length - 1 :]
    rec, key, value = rec_ref[...], key_ref[...], value_ref[...]
    value_low = low(value)
    grad_low = gwkv_ref[...]
    grad = grad_low.astype(F32)
    bonus = row_ref[9:10]
    state, gstate = widen_state(state_ref), widen_state(gstate_ref)
    pair = head_sum(grad * value)
    shared = pair * bonus
    g_key = shared * rec
    g_value = head_sum(rec * bonus * key) * grad
    g_bonus = jnp.sum(rec * key * pair, 0, keepdims=True)
    fade = jnp.exp(exclusive)
    back = nt(grad_low, state)
    from_state = low(rec * fade).astype(F32) * back
    g_rec = shared * key + fade * back
    fade = jnp.exp(final - inclusive)
    weighted = low(key * fade)
    back = nt(value_low, gstate)
    to_state = weighted.astype(F32) * back
    key_acc[...] = g_key + fade * back
    value_acc[...] = g_value + nn(weighted, gstate)
    pair_acc[...] = jnp.zeros_like(pair_acc)
    rec_parts, own_parts = [], []
    for q in range(length // SUB):
        start, stop, query, fade, mask = sub_block(q, inclusive, exclusive, length)
        left = rec[start:stop] * query
        spread = spread_heads(left)
        right = low(key[:stop] * fade)
        gspread = spread_heads(grad[start:stop])
        scores = low(jnp.where(mask, nt(spread, right), 0.0))
        weight = low(jnp.where(mask, nt(gspread, value_low[:stop]), 0.0))
        back = pick_heads(nn(weight, right))
        rec_parts.append(g_rec[start:stop] + query * back)
        own_parts.append(low(left).astype(F32) * back)
        back = tn(weight, spread)
        key_acc[:stop] += fade * back
        pair_acc[:stop] += right.astype(F32) * back
        value_acc[:stop] += tn(scores, gspread)
    grec_ref[...] = low(jnp.concatenate(rec_parts, 0))
    gkey_ref[...] = low(key_acc[...])
    gvalue_ref[...] = low(value_acc[...])
    inner, pairs = jnp.concatenate(own_parts, 0), pair_acc[...]
    both = head_sum(
        jnp.concatenate([state_ref[0, 0], state_ref[0, 1]], 1).astype(F32)
        * jnp.concatenate([gstate_ref[0, 0], gstate_ref[0, 1]], 1).astype(F32)
    )
    shape = both.shape
    here = lax.rem(lax.broadcasted_iota(jnp.int32, shape, 1), HEAD) == lax.broadcasted_iota(
        jnp.int32, shape, 0
    )
    through = jnp.exp(final) * jnp.sum(jnp.where(here, both, 0.0), 0, keepdims=True)
    later = exact_product(triangle(length, lambda r, c: r < c), inner + from_state - pairs)
    earlier = exact_product(triangle(length, lambda r, c: r > c), to_state)
    g_log = later - pairs + earlier + through
    g_decay = g_log * log_ref[...]
    gdecay_ref[...] = low(g_decay)
    sum_ref[0] = jnp.concatenate(
        [g_bonus, jnp.sum(g_decay, 0, keepdims=True), jnp.zeros((6, SPAN), F32)], 0
    )


def wkv_call(kernel, seqs, ins, outs, name, flops, scratch=()):
    width = ins[0].shape[1]
    length = ins[0].shape[0] // seqs

    def spec(a):
        if len(a.shape) == 4:
            return pl.BlockSpec((1, 2, a.shape[2], LANES), lambda s, g: (s, g, 0, 0))
        if len(a.shape) == 3:
            return pl.BlockSpec((1, 8, SPAN), lambda s, g: (s, 0, g))
        if a.shape[0] == 16:
            return pl.BlockSpec((16, SPAN), lambda s, g: (0, g))
        return pl.BlockSpec((length, SPAN), lambda s, g: (s, g))

    moved = sum(a.size * a.dtype.itemsize for a in ins + outs)
    return pl.pallas_call(
        kernel,
        grid=(seqs, width // SPAN),
        in_specs=[spec(a) for a in ins],
        out_specs=[spec(a) for a in outs],
        out_shape=outs,
        scratch_shapes=scratch,
        compiler_params=pltpu.CompilerParams(vmem_limit_bytes=40 << 20),
        cost_estimate=pl.CostEstimate(flops=flops, transcendentals=0, bytes_accessed=moved),
        name=name,
    )(*ins)


def chain_kernel(first_ref, packed_ref, out_ref, held_fade, *, rows, reverse):
    count = packed_ref.shape[0]
    logs = packed_ref[:, rows : rows + 1], packed_ref[:, rows + 1 : rows + 2]
    shape = (count, rows, LANES)
    lane = lax.rem(lax.broadcasted_iota(jnp.int32, shape, 2), HEAD)
    here = lane == lax.broadcasted_iota(jnp.int32, shape, 1) + first_ref[0]
    ones = head_block(LANES, LANES)
    total = None
    for part in logs:
        part = jnp.where(here, part.astype(F32), 0.0)
        part = nn(low(part.reshape(count * rows, LANES)), ones)
        total = part if total is None else total + part
    held_fade[...] = jnp.exp(total).reshape(shape)

    def one(hop, held):
        b = count - 1 - hop if reverse else hop
        out_ref[b] = low(held)
        return held_fade[b] * held + packed_ref[b, :rows].astype(F32)

    lax.fori_loop(0, count, one, jnp.zeros((rows, LANES), F32))


def chain(state, finals, reverse, beside=None):
    count = lax.axis_size(ALL)
    pairs = state.shape[0] * state.shape[1]
    split = count // pairs
    rows = state.shape[2] // split
    logs = finals.reshape(pairs, finals.shape[2], LANES)
    if split > 1:
        logs = jnp.repeat(logs, split, axis=0)
    packed = jnp.concatenate([state.reshape(count, rows, LANES), logs], 1)
    packed = lax.all_to_all(packed, ALL, 0, 0, tiled=True)
    packed, beside = tie(packed, beside)
    first = lax.rem(lax.axis_index(ALL), split) * rows
    entering = pl.pallas_call(
        lambda *refs: chain_kernel(*refs, rows=rows, reverse=reverse),
        grid_spec=pltpu.PrefetchScalarGridSpec(
            num_scalar_prefetch=1,
            grid=(1,),
            in_specs=[pl.BlockSpec(packed.shape, lambda i, c: (0, 0, 0))],
            out_specs=pl.BlockSpec((count, rows, LANES), lambda i, c: (0, 0, 0)),
            scratch_shapes=[pltpu.VMEM((count, rows, LANES), F32)],
        ),
        out_shape=jax.ShapeDtypeStruct((count, rows, LANES), BF16),
        compiler_params=pltpu.CompilerParams(vmem_limit_bytes=40 << 20),
        name="chain",
    )(first.astype(jnp.int32).reshape(1), packed)
    return lax.all_to_all(entering, ALL, 0, 0, tiled=True).reshape(state.shape), beside


def norm_forward(values, gain, bias):
    mean = jnp.mean(values, -1, keepdims=True)
    centered = values - mean
    rstd = lax.rsqrt(jnp.mean(centered * centered, -1, keepdims=True) + 1e-05)
    hat = centered * rstd
    return hat * gain + bias, hat, rstd


def norm_backward(grad, hat, rstd, gain):
    d = grad * gain
    back = rstd * (
        d - jnp.mean(d, -1, keepdims=True) - hat * jnp.mean(d * hat, -1, keepdims=True)
    )
    return back, jnp.sum(grad * hat, 0, keepdims=True), jnp.sum(grad, 0, keepdims=True)


def prior_of(values, seqs):
    shaped = values.reshape(seqs, -1, values.shape[-1])
    incoming = along(shaped[:, -1], 1)
    return jnp.concatenate([incoming[:, None], shaped[:, :-1]], 1).reshape(values.shape)


def prior_back(grad, seqs):
    shaped = grad.reshape(seqs, -1, grad.shape[-1])
    incoming = along(shaped[:, 0], -1)
    return jnp.concatenate([shaped[:, 1:], incoming[:, None]], 1).reshape(grad.shape)


def stack_nn(value, shards, which, tile=512):
    devices, _, rows, cols = shards.shape

    def kernel(a_ref, w_ref, o_ref):
        w = w_ref[...].reshape(devices * rows, tile)
        o_ref[...] = jnp.dot(a_ref[...], w, preferred_element_type=F32)

    return pl.pallas_call(
        kernel,
        grid=(cols // tile,),
        out_shape=jax.ShapeDtypeStruct((value.shape[0], cols), F32),
        in_specs=[
            pl.BlockSpec(value.shape, lambda j: (0, 0)),
            pl.BlockSpec((devices, 1, rows, tile), lambda j: (0, which, 0, j)),
        ],
        out_specs=pl.BlockSpec((value.shape[0], tile), lambda j: (0, j)),
        compiler_params=pltpu.CompilerParams(vmem_limit_bytes=40 << 20),
        cost_estimate=pl.CostEstimate(
            flops=2 * value.size * cols, transcendentals=0,
            bytes_accessed=2 * value.size + 2 * devices * rows * cols + 4 * value.shape[0] * cols,
        ),
        name="stack_nn",
    )(value, shards)


def stack_nt(value, shards, which, tile=512):
    devices, _, rows, cols = shards.shape
    group = tile // rows

    def kernel(a_ref, w_ref, o_ref):
        w = w_ref[...].reshape(tile, cols)
        o_ref[...] = lax.dot_general(
            a_ref[...], w, (((1,), (1,)), ((), ())), preferred_element_type=F32
        )

    return pl.pallas_call(
        kernel,
        grid=(devices // group,),
        out_shape=jax.ShapeDtypeStruct((value.shape[0], devices * rows), F32),
        in_specs=[
            pl.BlockSpec(value.shape, lambda j: (0, 0)),
            pl.BlockSpec((group, 1, rows, cols), lambda j: (j, which, 0, 0)),
        ],
        out_specs=pl.BlockSpec((value.shape[0], tile), lambda j: (0, j)),
        compiler_params=pltpu.CompilerParams(vmem_limit_bytes=40 << 20),
        cost_estimate=pl.CostEstimate(
            flops=2 * value.size * devices * rows, transcendentals=0,
            bytes_accessed=2 * value.size + 2 * devices * rows * cols
            + 4 * value.shape[0] * devices * rows,
        ),
        name="stack_nt",
    )(value, shards)


def other_half(shards, which):
    core = lax.axis_index("core")
    devices, n, rows, cols = shards.shape
    quarter = cols // 4
    own = lax.dynamic_slice(
        shards, (0, n - 1, 0, (2 * which + core) * quarter), (devices, 1, rows, quarter)
    )
    return swap(own.reshape(devices, rows, quarter), "y")


def places():
    return jnp.stack([lax.axis_index("y"), lax.axis_index("core")]).astype(jnp.int32)


def half_nn(value, shards, which, got, near):
    devices, n, rows, cols = shards.shape
    tile = cols // 4

    def kernel(p_ref, a_ref, w_ref, g_ref, n_ref, o_ref):
        t = pl.program_id(0)

        def put(w):
            w = w.reshape(devices * rows, tile)
            o_ref[...] = jnp.dot(a_ref[...], w, preferred_element_type=F32)

        pl.when(t < 2)(lambda: put(w_ref[...]))
        pl.when(t == 2)(lambda: put(g_ref[...]))
        pl.when(t == 3)(lambda: put(n_ref[...]))

    def out_at(t, p):
        other = 2 * (1 - p[0]) + jnp.where(t == 2, p[1], 1 - p[1])
        return 0, jnp.where(t < 2, 2 * p[0] + t, other)

    whole = pl.BlockSpec(got.shape, lambda t, p: (0, 0, 0))
    return pl.pallas_call(
        kernel,
        grid_spec=pltpu.PrefetchScalarGridSpec(
            num_scalar_prefetch=1,
            grid=(4,),
            in_specs=[
                pl.BlockSpec(value.shape, lambda t, p: (0, 0)),
                pl.BlockSpec(
                    (devices, 1, rows, tile),
                    lambda t, p: (0, n - 1, 0, 2 * which + jnp.minimum(t, 1)),
                ),
                whole,
                whole,
            ],
            out_specs=pl.BlockSpec((value.shape[0], tile), out_at),
        ),
        out_shape=jax.ShapeDtypeStruct((value.shape[0], cols), F32),
        compiler_params=pltpu.CompilerParams(vmem_limit_bytes=48 << 20),
        cost_estimate=pl.CostEstimate(
            flops=2 * value.size * cols, transcendentals=0,
            bytes_accessed=2 * value.size + 2 * devices * rows * cols + 4 * value.shape[0] * cols,
        ),
        name="half_nn",
    )(places(), value, shards, got, near)


def half_nt(value, shards, which, got, near):
    devices, n, rows, cols = shards.shape
    wide = 512
    group = wide // rows
    tile = cols // 4
    tokens = value.shape[0]

    def kernel(p_ref, a_ref, b_ref, c_ref, w_ref, g_ref, n_ref, o_ref):
        total = nt(a_ref[...], w_ref[...].reshape(wide, 2 * tile))
        total = total + nt(b_ref[...], g_ref[...].reshape(wide, tile))
        o_ref[...] = total + nt(c_ref[...], n_ref[...].reshape(wide, tile))

    part = pl.BlockSpec((group, rows, tile), lambda j, p: (j, 0, 0))
    return pl.pallas_call(
        kernel,
        grid_spec=pltpu.PrefetchScalarGridSpec(
            num_scalar_prefetch=1,
            grid=(devices // group,),
            in_specs=[
                pl.BlockSpec((tokens, 2 * tile), lambda j, p: (0, p[0])),
                pl.BlockSpec((tokens, tile), lambda j, p: (0, 2 * (1 - p[0]) + p[1])),
                pl.BlockSpec((tokens, tile), lambda j, p: (0, 2 * (1 - p[0]) + 1 - p[1])),
                pl.BlockSpec((group, 1, rows, 2 * tile), lambda j, p: (j, n - 1, 0, which)),
                part,
                part,
            ],
            out_specs=pl.BlockSpec((tokens, wide), lambda j, p: (0, j)),
        ),
        out_shape=jax.ShapeDtypeStruct((tokens, devices * rows), F32),
        compiler_params=pltpu.CompilerParams(vmem_limit_bytes=40 << 20),
        cost_estimate=pl.CostEstimate(
            flops=2 * value.size * devices * rows, transcendentals=0,
            bytes_accessed=2 * value.size + 2 * devices * rows * cols + 4 * tokens * devices * rows,
        ),
        name="half_nt",
    )(places(), value, value, value, shards, got, near)


TILE = 256


def pack_blocks(shard):
    rows, cols = shard.shape
    return jnp.swapaxes(shard.reshape(rows, cols // TILE, TILE), 0, 1).reshape(-1, TILE)


def ffn_call(kernel, core, grid, ins, specs, outs, out_specs, flops, scratch=(), name=None):
    moved = sum(a.size * a.dtype.itemsize for a in ins[:1] + outs) + flops // 1024
    return pl.pallas_call(
        kernel,
        grid_spec=pltpu.PrefetchScalarGridSpec(
            num_scalar_prefetch=1, grid=grid, in_specs=specs, out_specs=out_specs, scratch_shapes=scratch
        ),
        out_shape=outs,
        compiler_params=pltpu.CompilerParams(vmem_limit_bytes=56 << 20),
        cost_estimate=pl.CostEstimate(flops=flops, transcendentals=0, bytes_accessed=moved),
        name=name,
    )(core.reshape(1), *ins)


class PackedWeights:
    def __init__(self, packed, core, ff, width, half, chips):
        self.packed, self.core = packed, core
        self.devices = packed.shape[0]
        self.rows = width // self.devices
        self.quarter, self.width, self.half, self.chips = ff // 4, width, half, chips
        self.blocks = self.quarter // TILE
        self.fast = half % 16 == 0 and self.rows % 16 == 0 and self.rows == 128

    def _plain(self, start, rows, count):
        part = self.packed[:, start : start + rows * count]
        return part.reshape(-1, count, rows, TILE)

    def plain_key(self):
        start = self.half * (self.width // TILE)
        part = self._plain(start, self.rows, 2 * self.blocks)
        part = piece(part, self.core, self.blocks, 1)
        return jnp.swapaxes(part, 1, 2).reshape(self.width, self.quarter)

    def plain_value(self):
        part = self._plain(0, self.half, self.width // TILE)
        part = lax.dynamic_index_in_dim(
            part.reshape(self.chips, 2, *part.shape[1:]), self.core, 1, False
        )
        return jnp.swapaxes(part, 1, 2).reshape(self.quarter, self.width)

    def plain_rec(self):
        start = self.half * (self.width // TILE) + self.rows * 2 * self.blocks
        part = self._plain(start, self.rows, self.width // TILE)
        return jnp.swapaxes(part, 1, 2).reshape(self.width, self.width)

    def key_forward(self, mix):
        if not self.fast:
            relu = low(jnp.maximum(nn(mix, self.plain_key()), 0.0))
            return relu, low(relu.astype(F32) * relu.astype(F32))
        tokens = mix.shape[0]
        first = self.half * (self.width // TILE) // self.rows

        def kernel(c_ref, a_ref, w_ref, relu_ref, sq_ref):
            w = w_ref[...].reshape(self.width, TILE)
            relu = jnp.maximum(jnp.dot(a_ref[...], w, preferred_element_type=F32), 0.0)
            relu_ref[...] = low(relu)
            sq_ref[...] = low(relu * relu)

        out = jax.ShapeDtypeStruct((tokens, self.quarter), BF16)
        spec = pl.BlockSpec((tokens, TILE), lambda n, c: (0, n))
        return ffn_call(
            kernel, self.core, (self.blocks,), [mix, self.packed],
            [pl.BlockSpec(mix.shape, lambda n, c: (0, 0)),
             pl.BlockSpec((self.devices, self.rows, TILE),
                          lambda n, c: (0, first + c[0] * self.blocks + n, 0))],
            [out, out], [spec, spec], 2 * mix.size * self.quarter, name="key_forward",
        )

    def value_forward(self, squared):
        if not self.fast:
            return low(nn(squared, self.plain_value()))
        tokens = squared.shape[0]
        view = self.packed.reshape(self.chips, 2, *self.packed.shape[1:])

        def kernel(c_ref, a_ref, w_ref, o_ref):
            w = w_ref[...].reshape(self.quarter, TILE)
            o_ref[...] = low(jnp.dot(a_ref[...], w, preferred_element_type=F32))

        return ffn_call(
            kernel, self.core, (self.width // TILE,), [squared, view],
            [pl.BlockSpec(squared.shape, lambda m, c: (0, 0)),
             pl.BlockSpec((self.chips, 1, self.half, TILE), lambda m, c: (0, c[0], m, 0))],
            [jax.ShapeDtypeStruct((tokens, self.width), BF16)],
            [pl.BlockSpec((tokens, TILE), lambda m, c: (0, m))],
            2 * squared.size * self.width, name="value_forward",
        )[0]

    def rec_forward(self, mix):
        if not self.fast:
            return jax.nn.sigmoid(nn(mix, self.plain_rec()))
        tokens = mix.shape[0]
        first = self.packed.shape[1] // self.rows - self.width // TILE

        def kernel(c_ref, a_ref, w_ref, o_ref):
            w = w_ref[...].reshape(self.width, TILE)
            o_ref[...] = jax.nn.sigmoid(jnp.dot(a_ref[...], w, preferred_element_type=F32))

        return ffn_call(
            kernel, self.core, (self.width // TILE,), [mix, self.packed],
            [pl.BlockSpec(mix.shape, lambda m, c: (0, 0)),
             pl.BlockSpec((self.devices, self.rows, TILE), lambda m, c: (0, first + m, 0))],
            [jax.ShapeDtypeStruct((tokens, self.width), F32)],
            [pl.BlockSpec((tokens, TILE), lambda m, c: (0, m))],
            2 * mix.size * self.width, name="rec_forward",
        )[0]

    def value_backward(self, grad, relu):
        if not self.fast:
            return low(nt(grad, self.plain_value()) * 2.0 * relu.astype(F32))
        tokens = grad.shape[0]
        view = self.packed.reshape(self.chips, 2, *self.packed.shape[1:])
        count = self.width // TILE
        part = self.chips // 2

        def kernel(c_ref, a_ref, r_ref, w_ref, o_ref, flat):
            w = w_ref[...].reshape(part, count, self.half, TILE)
            for m in range(count):
                flat[:, m * TILE : (m + 1) * TILE] = w[:, m].reshape(part * self.half, TILE)
            back = lax.dot_general(
                a_ref[...], flat[...], (((1,), (1,)), ((), ())), preferred_element_type=F32
            )
            o_ref[...] = low(back * 2.0 * r_ref[...].astype(F32))

        wide = part * self.half
        return ffn_call(
            kernel, self.core, (2,), [grad, relu, view],
            [pl.BlockSpec(grad.shape, lambda i, c: (0, 0)),
             pl.BlockSpec((tokens, wide), lambda i, c: (0, i)),
             pl.BlockSpec((part, 1, count * self.half, TILE), lambda i, c: (i, c[0], 0, 0))],
            [jax.ShapeDtypeStruct((tokens, self.quarter), BF16)],
            [pl.BlockSpec((tokens, wide), lambda i, c: (0, i))],
            2 * grad.size * self.quarter,
            scratch=(pltpu.VMEM((wide, self.width), BF16),), name="value_backward",
        )[0]

    def key_backward(self, grad):
        if not self.fast:
            return low(nt(grad, self.plain_key()))
        tokens = grad.shape[0]
        part = 4
        rows = self.blocks * self.rows
        first = self.half * (self.width // TILE) // rows

        def kernel(c_ref, a_ref, w_ref, o_ref, flat):
            w = w_ref[...].reshape(part, self.blocks, self.rows, TILE)
            for n in range(self.blocks):
                flat[:, n * TILE : (n + 1) * TILE] = w[:, n].reshape(part * self.rows, TILE)
            o_ref[...] = low(lax.dot_general(
                a_ref[...], flat[...], (((1,), (1,)), ((), ())), preferred_element_type=F32
            ))

        wide = part * self.rows
        return ffn_call(
            kernel, self.core, (self.devices // part,), [grad, self.packed],
            [pl.BlockSpec(grad.shape, lambda i, c: (0, 0)),
             pl.BlockSpec((part, rows, TILE), lambda i, c: (i, first + c[0], 0))],
            [jax.ShapeDtypeStruct((tokens, self.width), BF16)],
            [pl.BlockSpec((tokens, wide), lambda i, c: (0, i))],
            2 * grad.size * self.width,
            scratch=(pltpu.VMEM((wide, self.quarter), BF16),), name="key_backward",
        )[0]

    def rec_backward(self, grad):
        if not self.fast:
            return nt(grad, self.plain_rec())
        tokens = grad.shape[0]
        part, count = 4, self.width // TILE
        rows = count * self.rows // 2
        first = self.packed.shape[1] // rows - 2

        def kernel(c_ref, a_ref, w_ref, v_ref, o_ref, flat):
            for k, ref in enumerate((w_ref, v_ref)):
                w = ref[...].reshape(part, count // 2, self.rows, TILE)
                for n in range(count // 2):
                    m = k * (count // 2) + n
                    flat[:, m * TILE : (m + 1) * TILE] = w[:, n].reshape(part * self.rows, TILE)
            o_ref[...] = lax.dot_general(
                a_ref[...], flat[...], (((1,), (1,)), ((), ())), preferred_element_type=F32
            )

        wide = part * self.rows
        return ffn_call(
            kernel, self.core, (self.devices // part,), [grad, self.packed, self.packed],
            [pl.BlockSpec(grad.shape, lambda i, c: (0, 0)),
             pl.BlockSpec((part, rows, TILE), lambda i, c: (i, first, 0)),
             pl.BlockSpec((part, rows, TILE), lambda i, c: (i, first + 1, 0))],
            [jax.ShapeDtypeStruct((tokens, self.width), F32)],
            [pl.BlockSpec((tokens, wide), lambda i, c: (0, i))],
            2 * grad.size * self.width,
            scratch=(pltpu.VMEM((wide, self.width), BF16),), name="rec_backward",
        )[0]


def body(tokens, att_w, down_w, up_w, key_w, value_w, rec_w, vectors, out_grad):
    seqs, length, width = tokens.shape
    total = seqs * length
    y, core = lax.axis_index("y"), lax.axis_index("core")
    zs = lax.axis_size("z")
    ff = key_w.shape[1]
    share = value_w.shape[0]
    half = share // 2
    quarter = ff // 4

    def rows(v):
        return v.reshape(total, width)

    def columns(shard):
        gathered = lax.all_gather(shard, WIDE, axis=0)
        return jnp.swapaxes(gathered, 0, 1).reshape(shard.shape[0], width)

    cols = up_w.shape[0]
    up_vec = columns(jnp.concatenate([vectors, up_w], 0))
    vec, up = up_vec[:16].astype(F32), up_vec[16:]
    down_t = columns(down_w.T)
    halves = [piece(att_w[i], y, width // 2, 1) for i in (3, 4)]
    w_att = jnp.concatenate([att_w[:3], jnp.concatenate(halves, 1)[None]], 0)
    w_att = lax.all_gather(w_att, WIDE, axis=0)
    key_sh = key_w.reshape(-1, zs, 2, 2, 2, half)
    key_sh = lax.dynamic_index_in_dim(key_sh, y, 4, False)
    key_sh = key_sh.transpose(0, 3, 1, 2, 4).reshape(-1, 2 * quarter)
    packed = jnp.concatenate(
        [pack_blocks(piece(value_w, y, half, 0)), pack_blocks(key_sh), pack_blocks(rec_w)], 0
    )
    packed = lax.all_gather(packed, WIDE, axis=0)

    x = rows(tokens.astype(F32))
    normed, hat, rstd = norm_forward(x, vec[0], vec[1])
    delta = prior_of(normed, seqs) - normed
    mix_low = low(normed + delta * vec[2])
    tanh_mix = jnp.tanh(nt(mix_low, down_t[:MIXCOLS]))
    hidden = low(tanh_mix)
    hid = [hidden[:, i * RANK : (i + 1) * RANK] for i in range(5)]
    ups = [up[i * RANK : (i + 1) * RANK] for i in range(5)]
    mixed = [low(normed + delta * (vec[3 + i] + nn(hid[i], ups[i]))) for i in range(5)]
    decay_in, key_in, value_in, rec_in, gate_in = mixed
    tanh_decay = jnp.tanh(nt(decay_in, down_t[MIXCOLS:]))
    hidden_decay = low(tanh_decay)
    logdecay = -jnp.exp(vec[8] + nn(hidden_decay, up[MIXCOLS:]))
    mix_all = group_pieces([gate_in, rec_in, key_in, value_in])
    w_att, mix_all = tie(w_att, mix_all)
    gate_other = other_half(w_att, 0)
    out_other = other_half(w_att, 1)
    keys = stack_nn(key_in, w_att, 1)
    values = stack_nn(value_in, w_att, 2)
    shaped = jax.ShapeDtypeStruct
    flat, flat_low = shaped((total, width), F32), shaped((total, width), BF16)
    states = shaped((seqs, width // LANES, HEAD, LANES), BF16)
    finals = shaped((seqs, width // LANES, 16, LANES), BF16)
    sums = shaped((seqs, 8, width), F32)
    unit = 2 * total * width
    inclusive, state, final = wkv_call(
        state_kernel, seqs, [keys, values, logdecay], [flat, states, finals], "wkv_state", unit * 512
    )
    carried, gate_other = chain(state, final, False, gate_other)
    gate_other = (gate_other, swap(gate_other, "core"))
    carried, out_other = tie(carried, out_other)
    out_other = (out_other, swap(out_other, "core"))
    recept = stack_nn(rec_in, w_att, 0)
    gate_pre = half_nn(gate_in, w_att, 0, *gate_other)
    wkv, gated = wkv_call(
        wkv_kernel, seqs, [recept, keys, values, inclusive, carried, gate_pre, vec], [flat, flat_low],
        "wkv_forward", unit * 1536,
    )
    first_sum = x + half_nn(gated, w_att, 1, *out_other)

    normed_two, hat_two, rstd_two = norm_forward(first_sum, vec[12], vec[13])
    delta_two = prior_of(normed_two, seqs) - normed_two
    key_mix = low(normed_two + delta_two * vec[14])
    rec_mix = low(normed_two + delta_two * vec[15])
    key_all = group_many([key_mix])[0]
    gated_all = group_pieces([gated])
    packed, key_all, gated_all = tie(packed, key_all, gated_all)
    ffn = PackedWeights(packed, core, ff, width, half, 2 * zs)
    relu, squared = ffn.key_forward(key_all)
    value_out = group_sum(ffn.value_forward(squared))
    rec_gate = ffn.rec_forward(rec_mix)
    block_out = low(first_sum + rec_gate * value_out).reshape(tokens.shape)

    g = rows(out_grad.astype(F32))
    grad_value = low(g * rec_gate)
    grad_gate_in = low(g * value_out * rec_gate * (1.0 - rec_gate))
    value_all = group_many([grad_value])[0]
    value_part = low(tn(squared, value_all)).reshape(-1, half, width)
    value_part, value_all = tie(value_part, value_all)
    value_part = lax.psum_scatter(value_part, ("z", "x"), scatter_dimension=0, tiled=True)[0]
    grad_key_pre = ffn.value_backward(value_all, relu)
    g_key_mix = ffn.key_backward(grad_key_pre)
    grad_key_pre, g_key_mix = tie(grad_key_pre, g_key_mix)
    key_part = low(tn(key_all, grad_key_pre))
    key_part = lax.psum_scatter(key_part, ("z", "x"), scatter_dimension=0, tiled=True)
    g_key_mix = group_sum(g_key_mix)
    g_rec_mix = ffn.rec_backward(grad_gate_in)

    g_prior = prior_back(g_key_mix * vec[14] + g_rec_mix * vec[15], seqs)
    g_normed_two = g_key_mix * (1.0 - vec[14]) + g_rec_mix * (1.0 - vec[15]) + g_prior
    g_maa_key = jnp.sum(g_key_mix * delta_two, 0, keepdims=True)
    g_maa_rec = jnp.sum(g_rec_mix * delta_two, 0, keepdims=True)
    back_two, g_gain_two, g_bias_two = norm_backward(g_normed_two, hat_two, rstd_two, vec[12])
    grad_first = g + back_two

    grad_att = low(grad_first)
    g_wkv, g_gate_low, g_state, gate_sums = wkv_call(
        gate_back_kernel, seqs,
        [half_nt(grad_att, w_att, 1, *out_other), wkv, gate_pre, recept, inclusive, vec],
        [flat_low, flat_low, states, sums], "gate_backward", unit * 1536,
    )
    g_state_out, (rights, rec_low) = chain(
        g_state, final, True, ([grad_gate_in, grad_att, g_gate_low], rec_mix)
    )
    side_near, side_across = half_cols(jnp.stack(rights, 0))
    rec_low = rec_low[None]
    rec_near, rec_across = swap(rec_low, "core"), swap(rec_low, "y")
    g_state_out, value_part = tie(g_state_out, value_part)
    g_rec, g_key, g_val, g_decay_low, wkv_sums = wkv_call(
        wkv_back_kernel, seqs,
        [recept, keys, values, inclusive, logdecay, carried, g_state_out, g_wkv, vec],
        [flat_low, flat_low, flat_low, flat_low, sums], "wkv_backward", unit * 4096,
        scratch=[pltpu.VMEM((length, SPAN), F32)] * 3,
    )
    gate_sums, wkv_sums = jnp.sum(gate_sums, 0), jnp.sum(wkv_sums, 0)
    projs = [g_rec, g_key, g_val, g_gate_low]
    main_near, main_across = half_cols(jnp.stack([g_rec, g_key, g_val], 0))
    main_near, side_across, rec_across = tie(main_near, side_across, rec_across)
    rec_all = (rec_low, rec_near, rec_across, swap(rec_across, "core"))
    side_lefts = [(rec_all, 0, 1), (gated_all, 0, 1), (mix_all, 0, 1)]
    side_give, side_keep = x_rows(side_lefts, quarter_cols(side_near, side_across))
    side_got = swap(side_give, "x")
    main_across, side_keep = tie(main_across, side_keep)
    main = all_rows([(mix_all, 1, 3)], quarter_cols(main_near, main_across))
    main, g_rec, g_key, g_val, g_gate_low, g_decay_low, key_part = tie(
        main, g_rec, g_key, g_val, g_gate_low, g_decay_low, key_part
    )
    main = lax.psum_scatter(main, ("z", "x"), scatter_dimension=0, tiled=True)
    projs = [g_rec, g_key, g_val, g_gate_low]

    decay_up_grad = tn(hidden_decay, g_decay_low)
    g_pre_decay = low(nt(g_decay_low, up[MIXCOLS:]) * (1.0 - tanh_decay * tanh_decay))
    decay_down_grad = tn(g_pre_decay, decay_in)
    g_mixed = [
        nn(g_pre_decay, down_t[MIXCOLS:]),
        stack_nt(projs[1], w_att, 1),
        stack_nt(projs[2], w_att, 2),
        stack_nt(projs[0], w_att, 0),
        half_nt(projs[3], w_att, 0, *gate_other),
    ]
    g_normed = g_prior_sum = None
    maa_rows, up_grads, hid_grads = [], [], []
    for i in range(5):
        offset = vec[3 + i] + nn(hid[i], ups[i])
        g_off = g_mixed[i] * delta
        maa_rows.append(jnp.sum(g_off, 0, keepdims=True))
        off_low = low(g_off)
        up_grads.append(tn(hid[i], off_low))
        hid_grads.append(nt(off_low, ups[i]))
        here = g_mixed[i] * (1.0 - offset)
        back = g_mixed[i] * offset
        g_normed = here if g_normed is None else g_normed + here
        g_prior_sum = back if g_prior_sum is None else g_prior_sum + back
    g_pre_mix = low(jnp.concatenate(hid_grads, 1) * (1.0 - tanh_mix * tanh_mix))
    mix_down_grad = tn(g_pre_mix, mix_low)
    g_first_mix = nn(g_pre_mix, down_t[:MIXCOLS])
    maa_first = jnp.sum(g_first_mix * delta, 0, keepdims=True)
    g_prior_sum = g_prior_sum + g_first_mix * vec[2]
    g_normed = g_normed + g_first_mix * (1.0 - vec[2]) + prior_back(g_prior_sum, seqs)
    g_normed, side_got = tie(g_normed, side_got)
    side = low(side_keep.astype(F32) + side_got.astype(F32))
    side = side.reshape(zs, -1, side.shape[1])
    moving = line_step(side, 1, None)
    g_gain = jnp.sum(g_normed * hat, 0, keepdims=True)
    g_bias = jnp.sum(g_normed, 0, keepdims=True)

    vec_rows = (
        [g_gain, g_bias, maa_first] + maa_rows
        + [wkv_sums[1:2], wkv_sums[0:1], gate_sums[0:1], gate_sums[1:2], g_gain_two, g_bias_two,
           g_maa_key, g_maa_rec]
    )
    packed = pack_columns(up_grads + [decay_up_grad, mix_down_grad, decay_down_grad] + vec_rows)
    packed, moving = tie(packed, moving)
    for t in range(2, zs - 1):
        moving = line_step(side, t, moving)
    packed, moving, value_part, key_part = tie(small_core(packed), moving, value_part, key_part)
    moving = line_step(side, zs - 1, moving)
    first = y == 0
    other = swap(value_part, "y")
    value_share = jnp.concatenate(
        [jnp.where(first, value_part, other), jnp.where(first, other, value_part)], 0
    ).astype(F32)
    key_share = spread_cols(key_part[:, None])[0].reshape(-1, 2, 2, zs, 2, half)
    key_share = key_share.transpose(0, 3, 4, 2, 1, 5).reshape(-1, ff)
    packed, main, g_normed = tie(packed, main, g_normed)
    back_one, _, _ = norm_backward(g_normed, hat, rstd, vec[0])
    input_grad = (grad_first + back_one).reshape(tokens.shape)
    packed, moving, key_share, value_share = tie(small_cross(packed), moving, key_share, value_share)
    side = low(line_end(side, moving))
    late = spread_cols(main.reshape(main.shape[0], 3, -1))
    early = spread_cols(side.reshape(side.shape[0], 3, -1))
    packed = small_sum(packed)
    rec_share = early[0]
    att_share = jnp.stack(late + [early[2], early[1]], 0)
    return (
        block_out, input_grad, att_share, packed[cols : 2 * cols].T, packed[:cols],
        key_share, value_share, rec_share, packed[2 * cols :],
    )


def solution(mesh):
    seq, wide = mesh.devices.shape
    fine = Mesh(mesh.devices.reshape(seq, wide // 4, 2, 2), ALL)
    token = P(None, ALL, None)
    by_row, by_col, stacked = P(WIDE, None), P(None, WIDE), P(None, WIDE, None)
    return jax.shard_map(
        body,
        mesh=fine,
        in_specs=(token, stacked, by_row, by_col, by_row, by_row, by_row, by_col, token),
        out_specs=(token, token, stacked, by_row, by_col, by_row, by_row, by_row, by_col),
        check_vma=False,
    )
```

```python
import jax
import jax.numpy as jnp
from jax import lax
from jax.experimental import pallas as pl
from jax.experimental.pallas import tpu as pltpu
from jax.sharding import Mesh
from jax.sharding import PartitionSpec as P

HEAD = 64
RANK = 32
MIXCOLS = 5 * RANK
LANES = 128
F32, BF16 = jnp.float32, jnp.bfloat16
WIDE = ("z", "x", "core")
ALL = ("y", "z", "x", "core")


def nn(a, b):
    return jnp.dot(a, b, preferred_element_type=F32)


def nt(a, b):
    return lax.dot_general(a, b, (((1,), (1,)), ((), ())), preferred_element_type=F32)


def tn(a, b):
    return lax.dot_general(a, b, (((0,), (0,)), ((), ())), preferred_element_type=F32)


def low(a):
    return a.astype(BF16)


def swap(value, axis):
    return lax.ppermute(value, axis, [(0, 1), (1, 0)])


def along(value, step):
    count = lax.axis_size(ALL)
    if step > 0:
        pairs = [(i, i + 1) for i in range(count - 1)]
    else:
        pairs = [(i + 1, i) for i in range(count - 1)]
    return lax.ppermute(value, ALL, pairs)


def piece(value, index, size, axis):
    start = [0] * value.ndim
    start[axis] = index * size
    shape = list(value.shape)
    shape[axis] = size
    return lax.dynamic_slice(value, start, shape)


def line_own(block, index):
    count = lax.axis_size("z")
    return lax.dynamic_index_in_dim(block, jnp.clip(index, 0, count - 1), 0, False).astype(F32)


def line_step(block, t, moving):
    count, place = lax.axis_size("z"), lax.axis_index("z")
    right = line_own(block, count - t + place)
    left = line_own(block, place + t - count)
    if moving is not None:
        right, left = right + moving[0].astype(F32), left + moving[1].astype(F32)
    up = lax.ppermute(low(right), "z", [(i, i + 1) for i in range(count - 1) if i <= t - 1])
    down = lax.ppermute(
        low(left), "z", [(i, i - 1) for i in range(1, count) if count - 1 - i <= t - 1]
    )
    return up, down


def line_end(block, moving):
    own = line_own(block, lax.axis_index("z"))
    return own + moving[0].astype(F32) + moving[1].astype(F32)


def line_sum(block):
    moving = None
    for t in range(1, lax.axis_size("z")):
        moving = line_step(block, t, moving)
    return line_end(block, moving)


def pack_columns(parts):
    width = parts[0].shape[1]
    counts = [p.shape[0] for p in parts]
    rows = sum(counts)
    step = 4
    block = step * LANES

    def kernel(*refs):
        out = refs[-1]
        start = 0
        while start < len(counts):
            take, n = [], 0
            while n == 0 or n % 8:
                take.append(refs[start][...])
                n += counts[start]
                start += 1
            first = sum(counts[: start - len(take)])
            rows_here = take[0] if len(take) == 1 else jnp.concatenate(take, 0)
            for b in range(step):
                out[b, first : first + n] = rows_here[:, b * LANES : (b + 1) * LANES]

    return pl.pallas_call(
        kernel,
        grid=(width // block,),
        in_specs=[pl.BlockSpec((c, block), lambda j: (0, j)) for c in counts],
        out_specs=pl.BlockSpec((step, rows, LANES), lambda j: (j, 0, 0)),
        out_shape=jax.ShapeDtypeStruct((width // LANES, rows, LANES), F32),
        compiler_params=pltpu.CompilerParams(vmem_limit_bytes=40 << 20),
        name="pack_columns",
    )(*parts)


def small_core(value):
    z, rows = lax.axis_size("z"), value.shape[1]
    share = 16 * LANES // (4 * z)
    if share != LANES:
        value = value.reshape(16, rows, LANES // share, share).swapaxes(1, 2).reshape(-1, rows, share)
    core = lax.axis_index("core")
    value = value.reshape(2 * z, 2, rows, share)
    give = low(lax.dynamic_index_in_dim(value, 1 - core, 1, False))
    value = lax.dynamic_index_in_dim(value, core, 1, False) + swap(give, "core").astype(F32)
    return value.reshape(z, 2, rows, share)


def small_cross(value):
    x = lax.axis_index("x")
    give = low(lax.dynamic_index_in_dim(value, 1 - x, 1, False))
    return lax.dynamic_index_in_dim(value, x, 1, False) + swap(give, "x").astype(F32)


def small_sum(value):
    count, place = lax.axis_size("z"), lax.axis_index("z")
    reach = count // 2
    while reach:
        value = value.reshape(2, reach, *value.shape[1:])
        bit = lax.rem(place // reach, 2)
        give = low(lax.dynamic_index_in_dim(value, 1 - bit, 0, False))
        got = lax.ppermute(give, "z", [(i, i ^ reach) for i in range(count)])
        value = lax.dynamic_index_in_dim(value, bit, 0, False) + got.astype(F32)
        reach //= 2
    value = value[0]
    return value + swap(value, "y")


def tie(*values):
    return lax.optimization_barrier(values)


def half_cols(right):
    y = lax.axis_index("y")
    half = right.shape[2] // 2
    return piece(right, y, half, 2), swap(piece(right, 1 - y, half, 2), "y")


def quarter_cols(near, across):
    core = lax.axis_index("core")
    both = jnp.stack([near, across], 1)
    quarter = near.shape[2] // 2
    mine = piece(both, core, quarter, 3)
    other = swap(piece(both, 1 - core, quarter, 3), "core")
    both = jnp.stack([mine, other], 2)
    return both.reshape(near.shape[0], -1, quarter)


def spread_cols(part):
    y, core = lax.axis_index("y"), lax.axis_index("core")
    rows = part.shape[0] // 2
    keep = piece(part, core, rows, 0)
    give = piece(part, 1 - core, rows, 0)
    near, across = swap(give, "core"), swap(keep, "y")
    far = lax.ppermute(give, ("y", "core"), [(0, 3), (1, 2), (2, 1), (3, 0)])
    quarters = []
    for q in range(4):
        this, that = jnp.where(core == q % 2, keep, near), jnp.where(core == q % 2, across, far)
        quarters.append(jnp.where(y == q // 2, this, that))
    outs = [
        jnp.concatenate([a[:, i].astype(F32) for a in quarters], 1) for i in range(part.shape[1])
    ]
    return outs


def x_parts(part):
    x, z = lax.axis_index("x"), lax.axis_size("z")
    view = part.reshape(z, 2, -1, part.shape[1])
    give = lax.dynamic_index_in_dim(view, 1 - x, 1, False)
    keep = lax.dynamic_index_in_dim(view, x, 1, False)
    return give.reshape(-1, part.shape[1]), keep.reshape(-1, part.shape[1])


def z_sum(keep, got):
    part = low(keep.astype(F32) + got.astype(F32))
    return lax.psum_scatter(part, "z", scatter_dimension=0, tiled=True)


def grad_call(lefts, rights, block, count, place):
    total, tokens, q = rights.shape
    bounds, arrays, specs = [0], [], []

    def left_spec(low_end, high_end, first, rows):
        def index(i, j, x):
            inside = jnp.logical_and(i >= low_end, i < high_end)
            which = jnp.clip(i, low_end, high_end - 1) - low_end + first
            at = jnp.where(inside, place(j, x[0]), place(jnp.where(i < low_end, 0, count - 1), x[0]))
            return which, 0, at

        return pl.BlockSpec((1, rows, block), index)

    for pieces, first, many in lefts:
        bounds.append(bounds[-1] + many)
        arrays.extend(pieces)
        specs.extend(left_spec(bounds[-2], bounds[-1], first, p.shape[1]) for p in pieces)

    def kernel(x_ref, *refs):
        *a_refs, b_ref, o_ref = refs
        i = pl.program_id(0)
        parts = len(lefts[0][0])
        for k in range(len(lefts)):

            @pl.when(jnp.logical_and(i >= bounds[k], i < bounds[k + 1]))
            def _(mine=a_refs[k * parts : (k + 1) * parts]):
                left = jnp.concatenate([a[0] for a in mine], 0)
                o_ref[...] = low(tn(left, b_ref[0]))

    return pl.pallas_call(
        kernel,
        grid_spec=pltpu.PrefetchScalarGridSpec(
            num_scalar_prefetch=1,
            grid=(total, count),
            in_specs=specs + [pl.BlockSpec((1, tokens, q), lambda i, j, x: (i, 0, 0))],
            out_specs=pl.BlockSpec((block, q), lambda i, j, x: (j, i)),
        ),
        out_shape=jax.ShapeDtypeStruct((count * block, total * q), BF16),
        compiler_params=pltpu.CompilerParams(vmem_limit_bytes=40 << 20),
        cost_estimate=pl.CostEstimate(
            flops=2 * rights.size * count * block, transcendentals=0,
            bytes_accessed=2 * (tokens * total * count * block + rights.size + count * block * total * q),
        ),
        name="weight_grad",
    )(lax.axis_index("x").astype(jnp.int32).reshape(1), *arrays, rights)


def all_rows(lefts, rights):
    return grad_call(lefts, rights, 512, lefts[0][0][0].shape[2] // 512, lambda j, x: j)


def x_rows(lefts, rights):
    z = lax.axis_size("z")
    block = lefts[0][0][0].shape[2] // (2 * z)
    if block % LANES:
        return x_parts(all_rows(lefts, rights))
    give = grad_call(lefts, rights, block, z, lambda j, x: 2 * j + 1 - x)
    return give, grad_call(lefts, rights, block, z, lambda j, x: 2 * j + x)


def group_pieces(values):
    value = jnp.stack(values, 0)
    near = swap(value, "core")
    across = swap(value, "y")
    far = swap(across, "core")
    return value, near, across, far


def group_many(values):
    return jnp.concatenate(group_pieces(values), 1)


def group_sum(value):
    rows = value.shape[0] // 4
    pair = value.reshape(2, 2, rows, -1)
    got = swap(pair[:, 1], "core")
    across = swap(low(pair[1, 0].astype(F32) + got[1].astype(F32)), "y")
    return pair[0, 0].astype(F32) + got[0].astype(F32) + across.astype(F32)


SPAN = 256
GROUP = SPAN // HEAD
SUB = 32


def lane_head(shape, dim):
    return lax.broadcasted_iota(jnp.int32, shape, dim) // HEAD


def head_block(rows, cols):
    shape = (rows, cols)
    return jnp.where(lane_head(shape, 0) == lane_head(shape, 1), 1.0, 0.0).astype(BF16)


def head_sum(value):
    coarse = low(value)
    fine = low(value - coarse.astype(F32))
    ones = head_block(SPAN, SPAN)
    return nn(coarse, ones) + nn(fine, ones)


def exact_product(left, value):
    coarse = low(value)
    rest = value - coarse.astype(F32)
    fine = low(rest)
    last = low(rest - fine.astype(F32))
    return nn(left, coarse) + (nn(left, fine) + nn(left, last))


def triangle(length, keep):
    shape = (length, length)
    row = lax.broadcasted_iota(jnp.int32, shape, 0)
    col = lax.broadcasted_iota(jnp.int32, shape, 1)
    return jnp.where(keep(row, col), 1.0, 0.0).astype(BF16)


def spread_heads(value):
    lane = lane_head(value.shape, 1)
    return jnp.concatenate([low(jnp.where(lane == h, value, 0.0)) for h in range(GROUP)], 0)


def pick_heads(value):
    rows = value.shape[0] // GROUP
    lane = lane_head((rows, SPAN), 1)
    out = value[:rows]
    for h in range(1, GROUP):
        out = jnp.where(lane == h, value[h * rows : (h + 1) * rows], out)
    return out


def widen_state(ref):
    state = jnp.concatenate([ref[0, 0], ref[0, 1]], 1)
    return jnp.concatenate(
        [jnp.where(lane_head(state.shape, 1) == h, state, jnp.zeros_like(state)) for h in range(GROUP)], 0
    )


def store_state(ref, value):
    state = low(pick_heads(value))
    ref[0, 0] = state[:, :LANES]
    ref[0, 1] = state[:, LANES:]


def exclusive_of(inclusive):
    return jnp.concatenate([jnp.zeros_like(inclusive[:1]), inclusive[:-1]], 0)


def cap(value):
    return jnp.exp(jnp.minimum(value, 80.0))


def state_kernel(key_ref, value_ref, log_ref, inc_ref, state_ref, final_ref):
    length = log_ref.shape[0]
    inclusive = exact_product(triangle(length, lambda r, c: r >= c), log_ref[...])
    inc_ref[...] = inclusive
    final = inclusive[length - 1 :]
    weighted = low(key_ref[...] * jnp.exp(final - inclusive))
    store_state(state_ref, tn(weighted, low(value_ref[...])))
    coarse = low(final)
    fine = low(final - coarse.astype(F32))
    rows = jnp.concatenate([coarse, fine, jnp.zeros((14, SPAN), BF16)], 0)
    final_ref[0, 0] = rows[:, :LANES]
    final_ref[0, 1] = rows[:, LANES:]


def sub_block(q, inclusive, exclusive, length):
    start, stop = q * SUB, (q + 1) * SUB
    middle = inclusive[start + SUB // 2 - 1 : start + SUB // 2]
    query = cap(exclusive[start:stop] - middle)
    key = cap(middle - inclusive[:stop])
    shape = (GROUP * SUB, stop)
    row = lax.rem(lax.broadcasted_iota(jnp.int32, shape, 0), SUB) + start
    mask = row > lax.broadcasted_iota(jnp.int32, shape, 1)
    return start, stop, query, key, mask


def wkv_kernel(rec_ref, key_ref, value_ref, inc_ref, state_ref, gate_ref, row_ref, wkv_ref, gated_ref):
    length = rec_ref.shape[0]
    inclusive = inc_ref[...]
    exclusive = exclusive_of(inclusive)
    rec, key, value = rec_ref[...], key_ref[...], value_ref[...]
    value_low = low(value)
    bonus, gain, bias = row_ref[9:10], row_ref[10:11], row_ref[11:12]
    answer = nn(low(rec * jnp.exp(exclusive)), widen_state(state_ref))
    answer = answer + head_sum(rec * bonus * key) * value
    parts = []
    for q in range(length // SUB):
        start, stop, query, fade, mask = sub_block(q, inclusive, exclusive, length)
        left = spread_heads(rec[start:stop] * query)
        scores = nt(left, low(key[:stop] * fade))
        scores = low(jnp.where(mask, scores, 0.0))
        parts.append(pick_heads(nn(scores, value_low[:stop])))
    answer = answer + jnp.concatenate(parts, 0)
    wkv_ref[...] = answer
    centered = answer - head_sum(answer) * (1.0 / HEAD)
    spread = head_sum(centered * centered) * (1.0 / HEAD)
    grouped = centered * lax.rsqrt(spread + 0.00064) * gain + bias
    gate = gate_ref[...]
    gated_ref[...] = low(grouped * gate / (1.0 + jnp.exp(-gate)))


def gate_back_kernel(grad_ref, wkv_ref, gate_ref, rec_ref, inc_ref, row_ref, gwkv_ref, ggate_ref, state_ref, sum_ref):
    gain, bias = row_ref[10:11], row_ref[11:12]
    answer, gate, grad = wkv_ref[...], gate_ref[...], grad_ref[...]
    centered = answer - head_sum(answer) * (1.0 / HEAD)
    rstd = lax.rsqrt(head_sum(centered * centered) * (1.0 / HEAD) + 0.00064)
    hat = centered * rstd
    grouped = hat * gain + bias
    sig = 1.0 / (1.0 + jnp.exp(-gate))
    g_grouped = grad * gate * sig
    ggate_ref[...] = low(grad * grouped * sig * (1.0 + gate * (1.0 - sig)))
    g_gain = jnp.sum(g_grouped * hat, 0, keepdims=True)
    g_bias = jnp.sum(g_grouped, 0, keepdims=True)
    sum_ref[0] = jnp.concatenate([g_gain, g_bias, jnp.zeros((6, SPAN), F32)], 0)
    g_hat = g_grouped * gain
    back = rstd * (
        g_hat - head_sum(g_hat) * (1.0 / HEAD) - hat * (head_sum(g_hat * hat) * (1.0 / HEAD))
    )
    back = low(back)
    gwkv_ref[...] = back
    query = low(rec_ref[...] * jnp.exp(exclusive_of(inc_ref[...])))
    store_state(state_ref, tn(query, back))


def wkv_back_kernel(
    rec_ref, key_ref, value_ref, inc_ref, log_ref, state_ref, gstate_ref, gwkv_ref, row_ref,
    grec_ref, gkey_ref, gvalue_ref, gdecay_ref, sum_ref, key_acc, value_acc, pair_acc,
):
    length = rec_ref.shape[0]
    inclusive = inc_ref[...]
    exclusive = exclusive_of(inclusive)
    final = inclusive[length - 1 :]
    rec, key, value = rec_ref[...], key_ref[...], value_ref[...]
    value_low = low(value)
    grad_low = gwkv_ref[...]
    grad = grad_low.astype(F32)
    bonus = row_ref[9:10]
    state, gstate = widen_state(state_ref), widen_state(gstate_ref)
    pair = head_sum(grad * value)
    shared = pair * bonus
    g_key = shared * rec
    g_value = head_sum(rec * bonus * key) * grad
    g_bonus = jnp.sum(rec * key * pair, 0, keepdims=True)
    fade = jnp.exp(exclusive)
    back = nt(grad_low, state)
    from_state = low(rec * fade).astype(F32) * back
    g_rec = shared * key + fade * back
    fade = jnp.exp(final - inclusive)
    weighted = low(key * fade)
    back = nt(value_low, gstate)
    to_state = weighted.astype(F32) * back
    key_acc[...] = g_key + fade * back
    value_acc[...] = g_value + nn(weighted, gstate)
    pair_acc[...] = jnp.zeros_like(pair_acc)
    rec_parts, own_parts = [], []
    for q in range(length // SUB):
        start, stop, query, fade, mask = sub_block(q, inclusive, exclusive, length)
        left = rec[start:stop] * query
        spread = spread_heads(left)
        right = low(key[:stop] * fade)
        gspread = spread_heads(grad[start:stop])
        scores = low(jnp.where(mask, nt(spread, right), 0.0))
        weight = low(jnp.where(mask, nt(gspread, value_low[:stop]), 0.0))
        back = pick_heads(nn(weight, right))
        rec_parts.append(g_rec[start:stop] + query * back)
        own_parts.append(low(left).astype(F32) * back)
        back = tn(weight, spread)
        key_acc[:stop] += fade * back
        pair_acc[:stop] += right.astype(F32) * back
        value_acc[:stop] += tn(scores, gspread)
    grec_ref[...] = low(jnp.concatenate(rec_parts, 0))
    gkey_ref[...] = low(key_acc[...])
    gvalue_ref[...] = low(value_acc[...])
    inner, pairs = jnp.concatenate(own_parts, 0), pair_acc[...]
    both = head_sum(
        jnp.concatenate([state_ref[0, 0], state_ref[0, 1]], 1).astype(F32)
        * jnp.concatenate([gstate_ref[0, 0], gstate_ref[0, 1]], 1).astype(F32)
    )
    shape = both.shape
    here = lax.rem(lax.broadcasted_iota(jnp.int32, shape, 1), HEAD) == lax.broadcasted_iota(
        jnp.int32, shape, 0
    )
    through = jnp.exp(final) * jnp.sum(jnp.where(here, both, 0.0), 0, keepdims=True)
    later = exact_product(triangle(length, lambda r, c: r < c), inner + from_state - pairs)
    earlier = exact_product(triangle(length, lambda r, c: r > c), to_state)
    g_log = later - pairs + earlier + through
    g_decay = g_log * log_ref[...]
    gdecay_ref[...] = low(g_decay)
    sum_ref[0] = jnp.concatenate(
        [g_bonus, jnp.sum(g_decay, 0, keepdims=True), jnp.zeros((6, SPAN), F32)], 0
    )


def wkv_call(kernel, seqs, ins, outs, name, flops, scratch=()):
    width = ins[0].shape[1]
    length = ins[0].shape[0] // seqs

    def spec(a):
        if len(a.shape) == 4:
            return pl.BlockSpec((1, 2, a.shape[2], LANES), lambda s, g: (s, g, 0, 0))
        if len(a.shape) == 3:
            return pl.BlockSpec((1, 8, SPAN), lambda s, g: (s, 0, g))
        if a.shape[0] == 16:
            return pl.BlockSpec((16, SPAN), lambda s, g: (0, g))
        return pl.BlockSpec((length, SPAN), lambda s, g: (s, g))

    moved = sum(a.size * a.dtype.itemsize for a in ins + outs)
    return pl.pallas_call(
        kernel,
        grid=(seqs, width // SPAN),
        in_specs=[spec(a) for a in ins],
        out_specs=[spec(a) for a in outs],
        out_shape=outs,
        scratch_shapes=scratch,
        compiler_params=pltpu.CompilerParams(vmem_limit_bytes=40 << 20),
        cost_estimate=pl.CostEstimate(flops=flops, transcendentals=0, bytes_accessed=moved),
        name=name,
    )(*ins)


def chain_kernel(first_ref, packed_ref, out_ref, held_fade, *, rows, reverse):
    count = packed_ref.shape[0]
    logs = packed_ref[:, rows : rows + 1], packed_ref[:, rows + 1 : rows + 2]
    shape = (count, rows, LANES)
    lane = lax.rem(lax.broadcasted_iota(jnp.int32, shape, 2), HEAD)
    here = lane == lax.broadcasted_iota(jnp.int32, shape, 1) + first_ref[0]
    ones = head_block(LANES, LANES)
    total = None
    for part in logs:
        part = jnp.where(here, part.astype(F32), 0.0)
        part = nn(low(part.reshape(count * rows, LANES)), ones)
        total = part if total is None else total + part
    held_fade[...] = jnp.exp(total).reshape(shape)

    def one(hop, held):
        b = count - 1 - hop if reverse else hop
        out_ref[b] = low(held)
        return held_fade[b] * held + packed_ref[b, :rows].astype(F32)

    lax.fori_loop(0, count, one, jnp.zeros((rows, LANES), F32))


def chain(state, finals, reverse, beside=None):
    count = lax.axis_size(ALL)
    pairs = state.shape[0] * state.shape[1]
    split = count // pairs
    rows = state.shape[2] // split
    logs = finals.reshape(pairs, finals.shape[2], LANES)
    if split > 1:
        logs = jnp.repeat(logs, split, axis=0)
    packed = jnp.concatenate([state.reshape(count, rows, LANES), logs], 1)
    packed = lax.all_to_all(packed, ALL, 0, 0, tiled=True)
    packed, beside = tie(packed, beside)
    first = lax.rem(lax.axis_index(ALL), split) * rows
    entering = pl.pallas_call(
        lambda *refs: chain_kernel(*refs, rows=rows, reverse=reverse),
        grid_spec=pltpu.PrefetchScalarGridSpec(
            num_scalar_prefetch=1,
            grid=(1,),
            in_specs=[pl.BlockSpec(packed.shape, lambda i, c: (0, 0, 0))],
            out_specs=pl.BlockSpec((count, rows, LANES), lambda i, c: (0, 0, 0)),
            scratch_shapes=[pltpu.VMEM((count, rows, LANES), F32)],
        ),
        out_shape=jax.ShapeDtypeStruct((count, rows, LANES), BF16),
        compiler_params=pltpu.CompilerParams(vmem_limit_bytes=40 << 20),
        name="chain",
    )(first.astype(jnp.int32).reshape(1), packed)
    return lax.all_to_all(entering, ALL, 0, 0, tiled=True).reshape(state.shape), beside


def norm_forward(values, gain, bias):
    mean = jnp.mean(values, -1, keepdims=True)
    centered = values - mean
    rstd = lax.rsqrt(jnp.mean(centered * centered, -1, keepdims=True) + 1e-05)
    hat = centered * rstd
    return hat * gain + bias, hat, rstd


def norm_backward(grad, hat, rstd, gain):
    d = grad * gain
    back = rstd * (
        d - jnp.mean(d, -1, keepdims=True) - hat * jnp.mean(d * hat, -1, keepdims=True)
    )
    return back, jnp.sum(grad * hat, 0, keepdims=True), jnp.sum(grad, 0, keepdims=True)


def prior_of(values, seqs):
    shaped = values.reshape(seqs, -1, values.shape[-1])
    incoming = along(shaped[:, -1], 1)
    return jnp.concatenate([incoming[:, None], shaped[:, :-1]], 1).reshape(values.shape)


def prior_back(grad, seqs):
    shaped = grad.reshape(seqs, -1, grad.shape[-1])
    incoming = along(shaped[:, 0], -1)
    return jnp.concatenate([shaped[:, 1:], incoming[:, None]], 1).reshape(grad.shape)


def stack_nn(value, shards, which, tile=512):
    devices, _, rows, cols = shards.shape

    def kernel(a_ref, w_ref, o_ref):
        w = w_ref[...].reshape(devices * rows, tile)
        o_ref[...] = jnp.dot(a_ref[...], w, preferred_element_type=F32)

    return pl.pallas_call(
        kernel,
        grid=(cols // tile,),
        out_shape=jax.ShapeDtypeStruct((value.shape[0], cols), F32),
        in_specs=[
            pl.BlockSpec(value.shape, lambda j: (0, 0)),
            pl.BlockSpec((devices, 1, rows, tile), lambda j: (0, which, 0, j)),
        ],
        out_specs=pl.BlockSpec((value.shape[0], tile), lambda j: (0, j)),
        compiler_params=pltpu.CompilerParams(vmem_limit_bytes=40 << 20),
        cost_estimate=pl.CostEstimate(
            flops=2 * value.size * cols, transcendentals=0,
            bytes_accessed=2 * value.size + 2 * devices * rows * cols + 4 * value.shape[0] * cols,
        ),
        name="stack_nn",
    )(value, shards)


def stack_nt(value, shards, which, tile=512):
    devices, _, rows, cols = shards.shape
    group = tile // rows

    def kernel(a_ref, w_ref, o_ref):
        w = w_ref[...].reshape(tile, cols)
        o_ref[...] = lax.dot_general(
            a_ref[...], w, (((1,), (1,)), ((), ())), preferred_element_type=F32
        )

    return pl.pallas_call(
        kernel,
        grid=(devices // group,),
        out_shape=jax.ShapeDtypeStruct((value.shape[0], devices * rows), F32),
        in_specs=[
            pl.BlockSpec(value.shape, lambda j: (0, 0)),
            pl.BlockSpec((group, 1, rows, cols), lambda j: (j, which, 0, 0)),
        ],
        out_specs=pl.BlockSpec((value.shape[0], tile), lambda j: (0, j)),
        compiler_params=pltpu.CompilerParams(vmem_limit_bytes=40 << 20),
        cost_estimate=pl.CostEstimate(
            flops=2 * value.size * devices * rows, transcendentals=0,
            bytes_accessed=2 * value.size + 2 * devices * rows * cols
            + 4 * value.shape[0] * devices * rows,
        ),
        name="stack_nt",
    )(value, shards)


def other_half(shards, which):
    core = lax.axis_index("core")
    devices, n, rows, cols = shards.shape
    quarter = cols // 4
    own = lax.dynamic_slice(
        shards, (0, n - 1, 0, (2 * which + core) * quarter), (devices, 1, rows, quarter)
    )
    return swap(own.reshape(devices, rows, quarter), "y")


def places():
    return jnp.stack([lax.axis_index("y"), lax.axis_index("core")]).astype(jnp.int32)


def half_nn(value, shards, which, got, near):
    devices, n, rows, cols = shards.shape
    tile = cols // 4

    def kernel(p_ref, a_ref, w_ref, g_ref, n_ref, o_ref):
        t = pl.program_id(0)

        def put(w):
            w = w.reshape(devices * rows, tile)
            o_ref[...] = jnp.dot(a_ref[...], w, preferred_element_type=F32)

        pl.when(t < 2)(lambda: put(w_ref[...]))
        pl.when(t == 2)(lambda: put(g_ref[...]))
        pl.when(t == 3)(lambda: put(n_ref[...]))

    def out_at(t, p):
        other = 2 * (1 - p[0]) + jnp.where(t == 2, p[1], 1 - p[1])
        return 0, jnp.where(t < 2, 2 * p[0] + t, other)

    whole = pl.BlockSpec(got.shape, lambda t, p: (0, 0, 0))
    return pl.pallas_call(
        kernel,
        grid_spec=pltpu.PrefetchScalarGridSpec(
            num_scalar_prefetch=1,
            grid=(4,),
            in_specs=[
                pl.BlockSpec(value.shape, lambda t, p: (0, 0)),
                pl.BlockSpec(
                    (devices, 1, rows, tile),
                    lambda t, p: (0, n - 1, 0, 2 * which + jnp.minimum(t, 1)),
                ),
                whole,
                whole,
            ],
            out_specs=pl.BlockSpec((value.shape[0], tile), out_at),
        ),
        out_shape=jax.ShapeDtypeStruct((value.shape[0], cols), F32),
        compiler_params=pltpu.CompilerParams(vmem_limit_bytes=48 << 20),
        cost_estimate=pl.CostEstimate(
            flops=2 * value.size * cols, transcendentals=0,
            bytes_accessed=2 * value.size + 2 * devices * rows * cols + 4 * value.shape[0] * cols,
        ),
        name="half_nn",
    )(places(), value, shards, got, near)


def half_nt(value, shards, which, got, near):
    devices, n, rows, cols = shards.shape
    wide = 512
    group = wide // rows
    tile = cols // 4
    tokens = value.shape[0]

    def kernel(p_ref, a_ref, b_ref, c_ref, w_ref, g_ref, n_ref, o_ref):
        total = nt(a_ref[...], w_ref[...].reshape(wide, 2 * tile))
        total = total + nt(b_ref[...], g_ref[...].reshape(wide, tile))
        o_ref[...] = total + nt(c_ref[...], n_ref[...].reshape(wide, tile))

    part = pl.BlockSpec((group, rows, tile), lambda j, p: (j, 0, 0))
    return pl.pallas_call(
        kernel,
        grid_spec=pltpu.PrefetchScalarGridSpec(
            num_scalar_prefetch=1,
            grid=(devices // group,),
            in_specs=[
                pl.BlockSpec((tokens, 2 * tile), lambda j, p: (0, p[0])),
                pl.BlockSpec((tokens, tile), lambda j, p: (0, 2 * (1 - p[0]) + p[1])),
                pl.BlockSpec((tokens, tile), lambda j, p: (0, 2 * (1 - p[0]) + 1 - p[1])),
                pl.BlockSpec((group, 1, rows, 2 * tile), lambda j, p: (j, n - 1, 0, which)),
                part,
                part,
            ],
            out_specs=pl.BlockSpec((tokens, wide), lambda j, p: (0, j)),
        ),
        out_shape=jax.ShapeDtypeStruct((tokens, devices * rows), F32),
        compiler_params=pltpu.CompilerParams(vmem_limit_bytes=40 << 20),
        cost_estimate=pl.CostEstimate(
            flops=2 * value.size * devices * rows, transcendentals=0,
            bytes_accessed=2 * value.size + 2 * devices * rows * cols + 4 * tokens * devices * rows,
        ),
        name="half_nt",
    )(places(), value, value, value, shards, got, near)


TILE = 256


def pack_blocks(shard):
    rows, cols = shard.shape
    return jnp.swapaxes(shard.reshape(rows, cols // TILE, TILE), 0, 1).reshape(-1, TILE)


def ffn_call(kernel, core, grid, ins, specs, outs, out_specs, flops, scratch=(), name=None):
    moved = sum(a.size * a.dtype.itemsize for a in ins[:1] + outs) + flops // 1024
    return pl.pallas_call(
        kernel,
        grid_spec=pltpu.PrefetchScalarGridSpec(
            num_scalar_prefetch=1, grid=grid, in_specs=specs, out_specs=out_specs, scratch_shapes=scratch
        ),
        out_shape=outs,
        compiler_params=pltpu.CompilerParams(vmem_limit_bytes=56 << 20),
        cost_estimate=pl.CostEstimate(flops=flops, transcendentals=0, bytes_accessed=moved),
        name=name,
    )(core.reshape(1), *ins)


class PackedWeights:
    def __init__(self, packed, core, ff, width, half, chips):
        self.packed, self.core = packed, core
        self.devices = packed.shape[0]
        self.rows = width // self.devices
        self.quarter, self.width, self.half, self.chips = ff // 4, width, half, chips
        self.blocks = self.quarter // TILE
        self.fast = half % 16 == 0 and self.rows % 16 == 0 and self.rows == 128

    def _plain(self, start, rows, count):
        part = self.packed[:, start : start + rows * count]
        return part.reshape(-1, count, rows, TILE)

    def plain_key(self):
        start = self.half * (self.width // TILE)
        part = self._plain(start, self.rows, 2 * self.blocks)
        part = piece(part, self.core, self.blocks, 1)
        return jnp.swapaxes(part, 1, 2).reshape(self.width, self.quarter)

    def plain_value(self):
        part = self._plain(0, self.half, self.width // TILE)
        part = lax.dynamic_index_in_dim(
            part.reshape(self.chips, 2, *part.shape[1:]), self.core, 1, False
        )
        return jnp.swapaxes(part, 1, 2).reshape(self.quarter, self.width)

    def plain_rec(self):
        start = self.half * (self.width // TILE) + self.rows * 2 * self.blocks
        part = self._plain(start, self.rows, self.width // TILE)
        return jnp.swapaxes(part, 1, 2).reshape(self.width, self.width)

    def key_forward(self, mix):
        if not self.fast:
            relu = low(jnp.maximum(nn(mix, self.plain_key()), 0.0))
            return relu, low(relu.astype(F32) * relu.astype(F32))
        tokens = mix.shape[0]
        first = self.half * (self.width // TILE) // self.rows

        def kernel(c_ref, a_ref, w_ref, relu_ref, sq_ref):
            w = w_ref[...].reshape(self.width, TILE)
            relu = jnp.maximum(jnp.dot(a_ref[...], w, preferred_element_type=F32), 0.0)
            relu_ref[...] = low(relu)
            sq_ref[...] = low(relu * relu)

        out = jax.ShapeDtypeStruct((tokens, self.quarter), BF16)
        spec = pl.BlockSpec((tokens, TILE), lambda n, c: (0, n))
        return ffn_call(
            kernel, self.core, (self.blocks,), [mix, self.packed],
            [pl.BlockSpec(mix.shape, lambda n, c: (0, 0)),
             pl.BlockSpec((self.devices, self.rows, TILE),
                          lambda n, c: (0, first + c[0] * self.blocks + n, 0))],
            [out, out], [spec, spec], 2 * mix.size * self.quarter, name="key_forward",
        )

    def value_forward(self, squared):
        if not self.fast:
            return low(nn(squared, self.plain_value()))
        tokens = squared.shape[0]
        view = self.packed.reshape(self.chips, 2, *self.packed.shape[1:])

        def kernel(c_ref, a_ref, w_ref, o_ref):
            w = w_ref[...].reshape(self.quarter, TILE)
            o_ref[...] = low(jnp.dot(a_ref[...], w, preferred_element_type=F32))

        return ffn_call(
            kernel, self.core, (self.width // TILE,), [squared, view],
            [pl.BlockSpec(squared.shape, lambda m, c: (0, 0)),
             pl.BlockSpec((self.chips, 1, self.half, TILE), lambda m, c: (0, c[0], m, 0))],
            [jax.ShapeDtypeStruct((tokens, self.width), BF16)],
            [pl.BlockSpec((tokens, TILE), lambda m, c: (0, m))],
            2 * squared.size * self.width, name="value_forward",
        )[0]

    def rec_forward(self, mix):
        if not self.fast:
            return jax.nn.sigmoid(nn(mix, self.plain_rec()))
        tokens = mix.shape[0]
        first = self.packed.shape[1] // self.rows - self.width // TILE

        def kernel(c_ref, a_ref, w_ref, o_ref):
            w = w_ref[...].reshape(self.width, TILE)
            o_ref[...] = jax.nn.sigmoid(jnp.dot(a_ref[...], w, preferred_element_type=F32))

        return ffn_call(
            kernel, self.core, (self.width // TILE,), [mix, self.packed],
            [pl.BlockSpec(mix.shape, lambda m, c: (0, 0)),
             pl.BlockSpec((self.devices, self.rows, TILE), lambda m, c: (0, first + m, 0))],
            [jax.ShapeDtypeStruct((tokens, self.width), F32)],
            [pl.BlockSpec((tokens, TILE), lambda m, c: (0, m))],
            2 * mix.size * self.width, name="rec_forward",
        )[0]

    def value_backward(self, grad, relu):
        if not self.fast:
            return low(nt(grad, self.plain_value()) * 2.0 * relu.astype(F32))
        tokens = grad.shape[0]
        view = self.packed.reshape(self.chips, 2, *self.packed.shape[1:])
        count = self.width // TILE
        part = self.chips // 2

        def kernel(c_ref, a_ref, r_ref, w_ref, o_ref, flat):
            w = w_ref[...].reshape(part, count, self.half, TILE)
            for m in range(count):
                flat[:, m * TILE : (m + 1) * TILE] = w[:, m].reshape(part * self.half, TILE)
            back = lax.dot_general(
                a_ref[...], flat[...], (((1,), (1,)), ((), ())), preferred_element_type=F32
            )
            o_ref[...] = low(back * 2.0 * r_ref[...].astype(F32))

        wide = part * self.half
        return ffn_call(
            kernel, self.core, (2,), [grad, relu, view],
            [pl.BlockSpec(grad.shape, lambda i, c: (0, 0)),
             pl.BlockSpec((tokens, wide), lambda i, c: (0, i)),
             pl.BlockSpec((part, 1, count * self.half, TILE), lambda i, c: (i, c[0], 0, 0))],
            [jax.ShapeDtypeStruct((tokens, self.quarter), BF16)],
            [pl.BlockSpec((tokens, wide), lambda i, c: (0, i))],
            2 * grad.size * self.quarter,
            scratch=(pltpu.VMEM((wide, self.width), BF16),), name="value_backward",
        )[0]

    def key_backward(self, grad):
        if not self.fast:
            return low(nt(grad, self.plain_key()))
        tokens = grad.shape[0]
        part = 4
        rows = self.blocks * self.rows
        first = self.half * (self.width // TILE) // rows

        def kernel(c_ref, a_ref, w_ref, o_ref, flat):
            w = w_ref[...].reshape(part, self.blocks, self.rows, TILE)
            for n in range(self.blocks):
                flat[:, n * TILE : (n + 1) * TILE] = w[:, n].reshape(part * self.rows, TILE)
            o_ref[...] = low(lax.dot_general(
                a_ref[...], flat[...], (((1,), (1,)), ((), ())), preferred_element_type=F32
            ))

        wide = part * self.rows
        return ffn_call(
            kernel, self.core, (self.devices // part,), [grad, self.packed],
            [pl.BlockSpec(grad.shape, lambda i, c: (0, 0)),
             pl.BlockSpec((part, rows, TILE), lambda i, c: (i, first + c[0], 0))],
            [jax.ShapeDtypeStruct((tokens, self.width), BF16)],
            [pl.BlockSpec((tokens, wide), lambda i, c: (0, i))],
            2 * grad.size * self.width,
            scratch=(pltpu.VMEM((wide, self.quarter), BF16),), name="key_backward",
        )[0]

    def rec_backward(self, grad):
        if not self.fast:
            return nt(grad, self.plain_rec())
        tokens = grad.shape[0]
        part, count = 4, self.width // TILE
        rows = count * self.rows // 2
        first = self.packed.shape[1] // rows - 2

        def kernel(c_ref, a_ref, w_ref, v_ref, o_ref, flat):
            for k, ref in enumerate((w_ref, v_ref)):
                w = ref[...].reshape(part, count // 2, self.rows, TILE)
                for n in range(count // 2):
                    m = k * (count // 2) + n
                    flat[:, m * TILE : (m + 1) * TILE] = w[:, n].reshape(part * self.rows, TILE)
            o_ref[...] = lax.dot_general(
                a_ref[...], flat[...], (((1,), (1,)), ((), ())), preferred_element_type=F32
            )

        wide = part * self.rows
        return ffn_call(
            kernel, self.core, (self.devices // part,), [grad, self.packed, self.packed],
            [pl.BlockSpec(grad.shape, lambda i, c: (0, 0)),
             pl.BlockSpec((part, rows, TILE), lambda i, c: (i, first, 0)),
             pl.BlockSpec((part, rows, TILE), lambda i, c: (i, first + 1, 0))],
            [jax.ShapeDtypeStruct((tokens, self.width), F32)],
            [pl.BlockSpec((tokens, wide), lambda i, c: (0, i))],
            2 * grad.size * self.width,
            scratch=(pltpu.VMEM((wide, self.width), BF16),), name="rec_backward",
        )[0]


def body(tokens, att_w, down_w, up_w, key_w, value_w, rec_w, vectors, out_grad):
    seqs, length, width = tokens.shape
    total = seqs * length
    y, core = lax.axis_index("y"), lax.axis_index("core")
    zs = lax.axis_size("z")
    ff = key_w.shape[1]
    share = value_w.shape[0]
    half = share // 2
    quarter = ff // 4

    def rows(v):
        return v.reshape(total, width)

    def columns(shard):
        gathered = lax.all_gather(shard, WIDE, axis=0)
        return jnp.swapaxes(gathered, 0, 1).reshape(shard.shape[0], width)

    cols = up_w.shape[0]
    up_vec = columns(jnp.concatenate([vectors, up_w], 0))
    vec, up = up_vec[:16].astype(F32), up_vec[16:]
    down_t = columns(down_w.T)
    halves = [piece(att_w[i], y, width // 2, 1) for i in (3, 4)]
    w_att = jnp.concatenate([att_w[:3], jnp.concatenate(halves, 1)[None]], 0)
    w_att = lax.all_gather(w_att, WIDE, axis=0)
    key_sh = key_w.reshape(-1, zs, 2, 2, 2, half)
    key_sh = lax.dynamic_index_in_dim(key_sh, y, 4, False)
    key_sh = key_sh.transpose(0, 3, 1, 2, 4).reshape(-1, 2 * quarter)
    packed = jnp.concatenate(
        [pack_blocks(piece(value_w, y, half, 0)), pack_blocks(key_sh), pack_blocks(rec_w)], 0
    )
    packed = lax.all_gather(packed, WIDE, axis=0)

    x = rows(tokens.astype(F32))
    normed, hat, rstd = norm_forward(x, vec[0], vec[1])
    delta = prior_of(normed, seqs) - normed
    mix_low = low(normed + delta * vec[2])
    tanh_mix = jnp.tanh(nt(mix_low, down_t[:MIXCOLS]))
    hidden = low(tanh_mix)
    hid = [hidden[:, i * RANK : (i + 1) * RANK] for i in range(5)]
    ups = [up[i * RANK : (i + 1) * RANK] for i in range(5)]
    mixed = [low(normed + delta * (vec[3 + i] + nn(hid[i], ups[i]))) for i in range(5)]
    decay_in, key_in, value_in, rec_in, gate_in = mixed
    tanh_decay = jnp.tanh(nt(decay_in, down_t[MIXCOLS:]))
    hidden_decay = low(tanh_decay)
    logdecay = -jnp.exp(vec[8] + nn(hidden_decay, up[MIXCOLS:]))
    mix_all = group_pieces([gate_in, rec_in, key_in, value_in])
    w_att, mix_all = tie(w_att, mix_all)
    gate_other = other_half(w_att, 0)
    out_other = other_half(w_att, 1)
    keys = stack_nn(key_in, w_att, 1)
    values = stack_nn(value_in, w_att, 2)
    shaped = jax.ShapeDtypeStruct
    flat, flat_low = shaped((total, width), F32), shaped((total, width), BF16)
    states = shaped((seqs, width // LANES, HEAD, LANES), BF16)
    finals = shaped((seqs, width // LANES, 16, LANES), BF16)
    sums = shaped((seqs, 8, width), F32)
    unit = 2 * total * width
    inclusive, state, final = wkv_call(
        state_kernel, seqs, [keys, values, logdecay], [flat, states, finals], "wkv_state", unit * 512
    )
    carried, gate_other = chain(state, final, False, gate_other)
    gate_other = (gate_other, swap(gate_other, "core"))
    carried, out_other = tie(carried, out_other)
    out_other = (out_other, swap(out_other, "core"))
    recept = stack_nn(rec_in, w_att, 0)
    gate_pre = half_nn(gate_in, w_att, 0, *gate_other)
    wkv, gated = wkv_call(
        wkv_kernel, seqs, [recept, keys, values, inclusive, carried, gate_pre, vec], [flat, flat_low],
        "wkv_forward", unit * 1536,
    )
    first_sum = x + half_nn(gated, w_att, 1, *out_other)

    normed_two, hat_two, rstd_two = norm_forward(first_sum, vec[12], vec[13])
    delta_two = prior_of(normed_two, seqs) - normed_two
    key_mix = low(normed_two + delta_two * vec[14])
    rec_mix = low(normed_two + delta_two * vec[15])
    key_all = group_many([key_mix])[0]
    gated_all = group_pieces([gated])
    packed, key_all, gated_all = tie(packed, key_all, gated_all)
    ffn = PackedWeights(packed, core, ff, width, half, 2 * zs)
    relu, squared = ffn.key_forward(key_all)
    value_out = group_sum(ffn.value_forward(squared))
    rec_gate = ffn.rec_forward(rec_mix)
    block_out = low(first_sum + rec_gate * value_out).reshape(tokens.shape)

    g = rows(out_grad.astype(F32))
    grad_value = low(g * rec_gate)
    grad_gate_in = low(g * value_out * rec_gate * (1.0 - rec_gate))
    value_all = group_many([grad_value])[0]
    value_part = low(tn(squared, value_all)).reshape(-1, half, width)
    value_part, value_all = tie(value_part, value_all)
    value_part = lax.psum_scatter(value_part, ("z", "x"), scatter_dimension=0, tiled=True)[0]
    grad_key_pre = ffn.value_backward(value_all, relu)
    g_key_mix = ffn.key_backward(grad_key_pre)
    grad_key_pre, g_key_mix = tie(grad_key_pre, g_key_mix)
    key_part = low(tn(key_all, grad_key_pre))
    key_part = lax.psum_scatter(key_part, ("z", "x"), scatter_dimension=0, tiled=True)
    g_key_mix = group_sum(g_key_mix)
    g_rec_mix = ffn.rec_backward(grad_gate_in)

    g_prior = prior_back(g_key_mix * vec[14] + g_rec_mix * vec[15], seqs)
    g_normed_two = g_key_mix * (1.0 - vec[14]) + g_rec_mix * (1.0 - vec[15]) + g_prior
    g_maa_key = jnp.sum(g_key_mix * delta_two, 0, keepdims=True)
    g_maa_rec = jnp.sum(g_rec_mix * delta_two, 0, keepdims=True)
    back_two, g_gain_two, g_bias_two = norm_backward(g_normed_two, hat_two, rstd_two, vec[12])
    grad_first = g + back_two

    grad_att = low(grad_first)
    g_wkv, g_gate_low, g_state, gate_sums = wkv_call(
        gate_back_kernel, seqs,
        [half_nt(grad_att, w_att, 1, *out_other), wkv, gate_pre, recept, inclusive, vec],
        [flat_low, flat_low, states, sums], "gate_backward", unit * 1536,
    )
    g_state_out, (rights, rec_low) = chain(
        g_state, final, True, ([grad_gate_in, grad_att, g_gate_low], rec_mix)
    )
    side_near, side_across = half_cols(jnp.stack(rights, 0))
    rec_low = rec_low[None]
    rec_near, rec_across = swap(rec_low, "core"), swap(rec_low, "y")
    g_state_out, value_part = tie(g_state_out, value_part)
    g_rec, g_key, g_val, g_decay_low, wkv_sums = wkv_call(
        wkv_back_kernel, seqs,
        [recept, keys, values, inclusive, logdecay, carried, g_state_out, g_wkv, vec],
        [flat_low, flat_low, flat_low, flat_low, sums], "wkv_backward", unit * 4096,
        scratch=[pltpu.VMEM((length, SPAN), F32)] * 3,
    )
    gate_sums, wkv_sums = jnp.sum(gate_sums, 0), jnp.sum(wkv_sums, 0)
    projs = [g_rec, g_key, g_val, g_gate_low]
    main_near, main_across = half_cols(jnp.stack([g_rec, g_key, g_val], 0))
    main_near, side_across, rec_across = tie(main_near, side_across, rec_across)
    rec_all = (rec_low, rec_near, rec_across, swap(rec_across, "core"))
    side_lefts = [(rec_all, 0, 1), (gated_all, 0, 1), (mix_all, 0, 1)]
    side_right, g_rec, g_key, g_val, g_gate_low, g_decay_low = tie(
        quarter_cols(side_near, side_across), g_rec, g_key, g_val, g_gate_low, g_decay_low
    )
    side_give, side_keep = x_rows(side_lefts, side_right)
    side_got = swap(side_give, "x")
    main_across, side_keep = tie(main_across, side_keep)
    main = all_rows([(mix_all, 1, 3)], quarter_cols(main_near, main_across))
    main, key_part = tie(main, key_part)
    main = lax.psum_scatter(main, ("z", "x"), scatter_dimension=0, tiled=True)
    projs = [g_rec, g_key, g_val, g_gate_low]

    decay_up_grad = tn(hidden_decay, g_decay_low)
    g_pre_decay = low(nt(g_decay_low, up[MIXCOLS:]) * (1.0 - tanh_decay * tanh_decay))
    decay_down_grad = tn(g_pre_decay, decay_in)
    g_mixed = [
        nn(g_pre_decay, down_t[MIXCOLS:]),
        stack_nt(projs[1], w_att, 1),
        stack_nt(projs[2], w_att, 2),
        stack_nt(projs[0], w_att, 0),
        half_nt(projs[3], w_att, 0, *gate_other),
    ]
    g_normed = g_prior_sum = None
    maa_rows, up_grads, hid_grads = [], [], []
    for i in range(5):
        offset = vec[3 + i] + nn(hid[i], ups[i])
        g_off = g_mixed[i] * delta
        maa_rows.append(jnp.sum(g_off, 0, keepdims=True))
        off_low = low(g_off)
        up_grads.append(tn(hid[i], off_low))
        hid_grads.append(nt(off_low, ups[i]))
        here = g_mixed[i] * (1.0 - offset)
        back = g_mixed[i] * offset
        g_normed = here if g_normed is None else g_normed + here
        g_prior_sum = back if g_prior_sum is None else g_prior_sum + back
    g_pre_mix = low(jnp.concatenate(hid_grads, 1) * (1.0 - tanh_mix * tanh_mix))
    mix_down_grad = tn(g_pre_mix, mix_low)
    g_first_mix = nn(g_pre_mix, down_t[:MIXCOLS])
    maa_first = jnp.sum(g_first_mix * delta, 0, keepdims=True)
    g_prior_sum = g_prior_sum + g_first_mix * vec[2]
    g_normed = g_normed + g_first_mix * (1.0 - vec[2]) + prior_back(g_prior_sum, seqs)
    g_normed, side_got = tie(g_normed, side_got)
    side = low(side_keep.astype(F32) + side_got.astype(F32))
    side = side.reshape(zs, -1, side.shape[1])
    moving = line_step(side, 1, None)
    g_gain = jnp.sum(g_normed * hat, 0, keepdims=True)
    g_bias = jnp.sum(g_normed, 0, keepdims=True)

    vec_rows = (
        [g_gain, g_bias, maa_first] + maa_rows
        + [wkv_sums[1:2], wkv_sums[0:1], gate_sums[0:1], gate_sums[1:2], g_gain_two, g_bias_two,
           g_maa_key, g_maa_rec]
    )
    packed = pack_columns(up_grads + [decay_up_grad, mix_down_grad, decay_down_grad] + vec_rows)
    packed, moving, value_part, key_part = tie(packed, moving, value_part, key_part)
    for t in range(2, zs - 1):
        moving = line_step(side, t, moving)
    first = y == 0
    other = swap(value_part, "y")
    value_share = jnp.concatenate(
        [jnp.where(first, value_part, other), jnp.where(first, other, value_part)], 0
    ).astype(F32)
    key_share = spread_cols(key_part[:, None])[0].reshape(-1, 2, 2, zs, 2, half)
    key_share = key_share.transpose(0, 3, 4, 2, 1, 5).reshape(-1, ff)
    packed, moving = tie(small_core(packed), moving)
    moving = line_step(side, zs - 1, moving)
    packed, main, g_normed = tie(packed, main, g_normed)
    back_one, _, _ = norm_backward(g_normed, hat, rstd, vec[0])
    input_grad = (grad_first + back_one).reshape(tokens.shape)
    packed, moving, key_share, value_share = tie(small_cross(packed), moving, key_share, value_share)
    side = low(line_end(side, moving))
    late = spread_cols(main.reshape(main.shape[0], 3, -1))
    early = spread_cols(side.reshape(side.shape[0], 3, -1))
    packed = small_sum(packed)
    rec_share = early[0]
    att_share = jnp.stack(late + [early[2], early[1]], 0)
    return (
        block_out, input_grad, att_share, packed[cols : 2 * cols].T, packed[:cols],
        key_share, value_share, rec_share, packed[2 * cols :],
    )


def solution(mesh):
    seq, wide = mesh.devices.shape
    fine = Mesh(mesh.devices.reshape(seq, wide // 4, 2, 2), ALL)
    token = P(None, ALL, None)
    by_row, by_col, stacked = P(WIDE, None), P(None, WIDE), P(None, WIDE, None)
    return jax.shard_map(
        body,
        mesh=fine,
        in_specs=(token, stacked, by_row, by_col, by_row, by_row, by_row, by_col, token),
        out_specs=(token, token, stacked, by_row, by_col, by_row, by_row, by_row, by_col),
        check_vma=False,
    )
```

```python
import jax
import jax.numpy as jnp
from jax import lax
from jax.experimental import pallas as pl
from jax.experimental.pallas import tpu as pltpu
from jax.sharding import Mesh
from jax.sharding import PartitionSpec as P

HEAD = 64
RANK = 32
MIXCOLS = 5 * RANK
LANES = 128
F32, BF16 = jnp.float32, jnp.bfloat16
WIDE = ("z", "x", "core")
ALL = ("y", "z", "x", "core")


def nn(a, b):
    return jnp.dot(a, b, preferred_element_type=F32)


def nt(a, b):
    return lax.dot_general(a, b, (((1,), (1,)), ((), ())), preferred_element_type=F32)


def tn(a, b):
    return lax.dot_general(a, b, (((0,), (0,)), ((), ())), preferred_element_type=F32)


def low(a):
    return a.astype(BF16)


def swap(value, axis):
    return lax.ppermute(value, axis, [(0, 1), (1, 0)])


def along(value, step):
    count = lax.axis_size(ALL)
    if step > 0:
        pairs = [(i, i + 1) for i in range(count - 1)]
    else:
        pairs = [(i + 1, i) for i in range(count - 1)]
    return lax.ppermute(value, ALL, pairs)


def piece(value, index, size, axis):
    start = [0] * value.ndim
    start[axis] = index * size
    shape = list(value.shape)
    shape[axis] = size
    return lax.dynamic_slice(value, start, shape)


def line_own(block, index):
    count = lax.axis_size("z")
    return lax.dynamic_index_in_dim(block, jnp.clip(index, 0, count - 1), 0, False).astype(F32)


def line_step(block, t, moving):
    count, place = lax.axis_size("z"), lax.axis_index("z")
    right = line_own(block, count - t + place)
    left = line_own(block, place + t - count)
    if moving is not None:
        right, left = right + moving[0].astype(F32), left + moving[1].astype(F32)
    up = lax.ppermute(low(right), "z", [(i, i + 1) for i in range(count - 1) if i <= t - 1])
    down = lax.ppermute(
        low(left), "z", [(i, i - 1) for i in range(1, count) if count - 1 - i <= t - 1]
    )
    return up, down


def line_end(block, moving):
    own = line_own(block, lax.axis_index("z"))
    return own + moving[0].astype(F32) + moving[1].astype(F32)


def line_sum(block):
    moving = None
    for t in range(1, lax.axis_size("z")):
        moving = line_step(block, t, moving)
    return line_end(block, moving)


def pack_columns(parts):
    width = parts[0].shape[1]
    counts = [p.shape[0] for p in parts]
    rows = sum(counts)
    step = 4
    block = step * LANES

    def kernel(*refs):
        out = refs[-1]
        start = 0
        while start < len(counts):
            take, n = [], 0
            while n == 0 or n % 8:
                take.append(refs[start][...])
                n += counts[start]
                start += 1
            first = sum(counts[: start - len(take)])
            rows_here = take[0] if len(take) == 1 else jnp.concatenate(take, 0)
            for b in range(step):
                out[b, first : first + n] = rows_here[:, b * LANES : (b + 1) * LANES]

    return pl.pallas_call(
        kernel,
        grid=(width // block,),
        in_specs=[pl.BlockSpec((c, block), lambda j: (0, j)) for c in counts],
        out_specs=pl.BlockSpec((step, rows, LANES), lambda j: (j, 0, 0)),
        out_shape=jax.ShapeDtypeStruct((width // LANES, rows, LANES), F32),
        compiler_params=pltpu.CompilerParams(vmem_limit_bytes=40 << 20),
        name="pack_columns",
    )(*parts)


def small_core(value):
    z, rows = lax.axis_size("z"), value.shape[1]
    share = 16 * LANES // (4 * z)
    if share != LANES:
        value = value.reshape(16, rows, LANES // share, share).swapaxes(1, 2).reshape(-1, rows, share)
    core = lax.axis_index("core")
    value = value.reshape(2 * z, 2, rows, share)
    give = low(lax.dynamic_index_in_dim(value, 1 - core, 1, False))
    value = lax.dynamic_index_in_dim(value, core, 1, False) + swap(give, "core").astype(F32)
    return value.reshape(z, 2, rows, share)


def small_cross(value):
    x = lax.axis_index("x")
    give = low(lax.dynamic_index_in_dim(value, 1 - x, 1, False))
    return lax.dynamic_index_in_dim(value, x, 1, False) + swap(give, "x").astype(F32)


def small_sum(value):
    count, place = lax.axis_size("z"), lax.axis_index("z")
    reach = count // 2
    while reach:
        value = value.reshape(2, reach, *value.shape[1:])
        bit = lax.rem(place // reach, 2)
        give = low(lax.dynamic_index_in_dim(value, 1 - bit, 0, False))
        got = lax.ppermute(give, "z", [(i, i ^ reach) for i in range(count)])
        value = lax.dynamic_index_in_dim(value, bit, 0, False) + got.astype(F32)
        reach //= 2
    value = value[0]
    return value + swap(value, "y")


def tie(*values):
    return lax.optimization_barrier(values)


def half_cols(right):
    y = lax.axis_index("y")
    half = right.shape[2] // 2
    return piece(right, y, half, 2), swap(piece(right, 1 - y, half, 2), "y")


def quarter_cols(near, across):
    core = lax.axis_index("core")
    both = jnp.stack([near, across], 1)
    quarter = near.shape[2] // 2
    mine = piece(both, core, quarter, 3)
    other = swap(piece(both, 1 - core, quarter, 3), "core")
    both = jnp.stack([mine, other], 2)
    return both.reshape(near.shape[0], -1, quarter)


def spread_cols(part):
    y, core = lax.axis_index("y"), lax.axis_index("core")
    rows = part.shape[0] // 2
    keep = piece(part, core, rows, 0)
    give = piece(part, 1 - core, rows, 0)
    near, across = swap(give, "core"), swap(keep, "y")
    far = lax.ppermute(give, ("y", "core"), [(0, 3), (1, 2), (2, 1), (3, 0)])
    quarters = []
    for q in range(4):
        this, that = jnp.where(core == q % 2, keep, near), jnp.where(core == q % 2, across, far)
        quarters.append(jnp.where(y == q // 2, this, that))
    outs = [
        jnp.concatenate([a[:, i].astype(F32) for a in quarters], 1) for i in range(part.shape[1])
    ]
    return outs


def x_parts(part):
    x, z = lax.axis_index("x"), lax.axis_size("z")
    view = part.reshape(z, 2, -1, part.shape[1])
    give = lax.dynamic_index_in_dim(view, 1 - x, 1, False)
    keep = lax.dynamic_index_in_dim(view, x, 1, False)
    return give.reshape(-1, part.shape[1]), keep.reshape(-1, part.shape[1])


def z_sum(keep, got):
    part = low(keep.astype(F32) + got.astype(F32))
    return lax.psum_scatter(part, "z", scatter_dimension=0, tiled=True)


def grad_call(lefts, rights, block, count, place):
    total, tokens, q = rights.shape
    bounds, arrays, specs = [0], [], []

    def left_spec(low_end, high_end, first, rows):
        def index(i, j, x):
            inside = jnp.logical_and(i >= low_end, i < high_end)
            which = jnp.clip(i, low_end, high_end - 1) - low_end + first
            at = jnp.where(inside, place(j, x[0]), place(jnp.where(i < low_end, 0, count - 1), x[0]))
            return which, 0, at

        return pl.BlockSpec((1, rows, block), index)

    for pieces, first, many in lefts:
        bounds.append(bounds[-1] + many)
        arrays.extend(pieces)
        specs.extend(left_spec(bounds[-2], bounds[-1], first, p.shape[1]) for p in pieces)

    def kernel(x_ref, *refs):
        *a_refs, b_ref, o_ref = refs
        i = pl.program_id(0)
        parts = len(lefts[0][0])
        for k in range(len(lefts)):

            @pl.when(jnp.logical_and(i >= bounds[k], i < bounds[k + 1]))
            def _(mine=a_refs[k * parts : (k + 1) * parts]):
                left = jnp.concatenate([a[0] for a in mine], 0)
                o_ref[...] = low(tn(left, b_ref[0]))

    return pl.pallas_call(
        kernel,
        grid_spec=pltpu.PrefetchScalarGridSpec(
            num_scalar_prefetch=1,
            grid=(total, count),
            in_specs=specs + [pl.BlockSpec((1, tokens, q), lambda i, j, x: (i, 0, 0))],
            out_specs=pl.BlockSpec((block, q), lambda i, j, x: (j, i)),
        ),
        out_shape=jax.ShapeDtypeStruct((count * block, total * q), BF16),
        compiler_params=pltpu.CompilerParams(vmem_limit_bytes=40 << 20),
        cost_estimate=pl.CostEstimate(
            flops=2 * rights.size * count * block, transcendentals=0,
            bytes_accessed=2 * (tokens * total * count * block + rights.size + count * block * total * q),
        ),
        name="weight_grad",
    )(lax.axis_index("x").astype(jnp.int32).reshape(1), *arrays, rights)


def all_rows(lefts, rights):
    return grad_call(lefts, rights, 512, lefts[0][0][0].shape[2] // 512, lambda j, x: j)


def x_rows(lefts, rights, own):
    z = lax.axis_size("z")
    block = lefts[0][0][0].shape[2] // (2 * z)
    if block % LANES:
        return x_parts(all_rows(lefts, rights))[int(own)]
    if own:
        return grad_call(lefts, rights, block, z, lambda j, x: 2 * j + x)
    return grad_call(lefts, rights, block, z, lambda j, x: 2 * j + 1 - x)


def group_pieces(values):
    value = jnp.stack(values, 0)
    near = swap(value, "core")
    across = swap(value, "y")
    far = swap(across, "core")
    return value, near, across, far


def group_many(values):
    return jnp.concatenate(group_pieces(values), 1)


def group_sum(value):
    rows = value.shape[0] // 4
    pair = value.reshape(2, 2, rows, -1)
    got = swap(pair[:, 1], "core")
    across = swap(low(pair[1, 0].astype(F32) + got[1].astype(F32)), "y")
    return pair[0, 0].astype(F32) + got[0].astype(F32) + across.astype(F32)


SPAN = 256
GROUP = SPAN // HEAD
SUB = 32


def lane_head(shape, dim):
    return lax.broadcasted_iota(jnp.int32, shape, dim) // HEAD


def head_block(rows, cols):
    shape = (rows, cols)
    return jnp.where(lane_head(shape, 0) == lane_head(shape, 1), 1.0, 0.0).astype(BF16)


def head_sum(value):
    coarse = low(value)
    fine = low(value - coarse.astype(F32))
    ones = head_block(SPAN, SPAN)
    return nn(coarse, ones) + nn(fine, ones)


def exact_product(left, value):
    coarse = low(value)
    rest = value - coarse.astype(F32)
    fine = low(rest)
    last = low(rest - fine.astype(F32))
    return nn(left, coarse) + (nn(left, fine) + nn(left, last))


def triangle(length, keep):
    shape = (length, length)
    row = lax.broadcasted_iota(jnp.int32, shape, 0)
    col = lax.broadcasted_iota(jnp.int32, shape, 1)
    return jnp.where(keep(row, col), 1.0, 0.0).astype(BF16)


def spread_heads(value):
    lane = lane_head(value.shape, 1)
    return jnp.concatenate([low(jnp.where(lane == h, value, 0.0)) for h in range(GROUP)], 0)


def pick_heads(value):
    rows = value.shape[0] // GROUP
    lane = lane_head((rows, SPAN), 1)
    out = value[:rows]
    for h in range(1, GROUP):
        out = jnp.where(lane == h, value[h * rows : (h + 1) * rows], out)
    return out


def widen_state(ref):
    state = jnp.concatenate([ref[0, 0], ref[0, 1]], 1)
    return jnp.concatenate(
        [jnp.where(lane_head(state.shape, 1) == h, state, jnp.zeros_like(state)) for h in range(GROUP)], 0
    )


def store_state(ref, value):
    state = low(pick_heads(value))
    ref[0, 0] = state[:, :LANES]
    ref[0, 1] = state[:, LANES:]


def exclusive_of(inclusive):
    return jnp.concatenate([jnp.zeros_like(inclusive[:1]), inclusive[:-1]], 0)


def cap(value):
    return jnp.exp(jnp.minimum(value, 80.0))


def state_kernel(key_ref, value_ref, log_ref, inc_ref, state_ref, final_ref):
    length = log_ref.shape[0]
    inclusive = exact_product(triangle(length, lambda r, c: r >= c), log_ref[...])
    inc_ref[...] = inclusive
    final = inclusive[length - 1 :]
    weighted = low(key_ref[...] * jnp.exp(final - inclusive))
    store_state(state_ref, tn(weighted, low(value_ref[...])))
    coarse = low(final)
    fine = low(final - coarse.astype(F32))
    rows = jnp.concatenate([coarse, fine, jnp.zeros((14, SPAN), BF16)], 0)
    final_ref[0, 0] = rows[:, :LANES]
    final_ref[0, 1] = rows[:, LANES:]


def sub_block(q, inclusive, exclusive, length):
    start, stop = q * SUB, (q + 1) * SUB
    middle = inclusive[start + SUB // 2 - 1 : start + SUB // 2]
    query = cap(exclusive[start:stop] - middle)
    key = cap(middle - inclusive[:stop])
    shape = (GROUP * SUB, stop)
    row = lax.rem(lax.broadcasted_iota(jnp.int32, shape, 0), SUB) + start
    mask = row > lax.broadcasted_iota(jnp.int32, shape, 1)
    return start, stop, query, key, mask


def wkv_kernel(rec_ref, key_ref, value_ref, inc_ref, state_ref, gate_ref, row_ref, wkv_ref, gated_ref):
    length = rec_ref.shape[0]
    inclusive = inc_ref[...]
    exclusive = exclusive_of(inclusive)
    rec, key, value = rec_ref[...], key_ref[...], value_ref[...]
    value_low = low(value)
    bonus, gain, bias = row_ref[9:10], row_ref[10:11], row_ref[11:12]
    answer = nn(low(rec * jnp.exp(exclusive)), widen_state(state_ref))
    answer = answer + head_sum(rec * bonus * key) * value
    parts = []
    for q in range(length // SUB):
        start, stop, query, fade, mask = sub_block(q, inclusive, exclusive, length)
        left = spread_heads(rec[start:stop] * query)
        scores = nt(left, low(key[:stop] * fade))
        scores = low(jnp.where(mask, scores, 0.0))
        parts.append(pick_heads(nn(scores, value_low[:stop])))
    answer = answer + jnp.concatenate(parts, 0)
    wkv_ref[...] = answer
    centered = answer - head_sum(answer) * (1.0 / HEAD)
    spread = head_sum(centered * centered) * (1.0 / HEAD)
    grouped = centered * lax.rsqrt(spread + 0.00064) * gain + bias
    gate = gate_ref[...]
    gated_ref[...] = low(grouped * gate / (1.0 + jnp.exp(-gate)))


def gate_back_kernel(grad_ref, wkv_ref, gate_ref, rec_ref, inc_ref, row_ref, gwkv_ref, ggate_ref, state_ref, sum_ref):
    gain, bias = row_ref[10:11], row_ref[11:12]
    answer, gate, grad = wkv_ref[...], gate_ref[...], grad_ref[...]
    centered = answer - head_sum(answer) * (1.0 / HEAD)
    rstd = lax.rsqrt(head_sum(centered * centered) * (1.0 / HEAD) + 0.00064)
    hat = centered * rstd
    grouped = hat * gain + bias
    sig = 1.0 / (1.0 + jnp.exp(-gate))
    g_grouped = grad * gate * sig
    ggate_ref[...] = low(grad * grouped * sig * (1.0 + gate * (1.0 - sig)))
    g_gain = jnp.sum(g_grouped * hat, 0, keepdims=True)
    g_bias = jnp.sum(g_grouped, 0, keepdims=True)
    sum_ref[0] = jnp.concatenate([g_gain, g_bias, jnp.zeros((6, SPAN), F32)], 0)
    g_hat = g_grouped * gain
    back = rstd * (
        g_hat - head_sum(g_hat) * (1.0 / HEAD) - hat * (head_sum(g_hat * hat) * (1.0 / HEAD))
    )
    back = low(back)
    gwkv_ref[...] = back
    query = low(rec_ref[...] * jnp.exp(exclusive_of(inc_ref[...])))
    store_state(state_ref, tn(query, back))


def wkv_back_kernel(
    rec_ref, key_ref, value_ref, inc_ref, log_ref, state_ref, gstate_ref, gwkv_ref, row_ref,
    grec_ref, gkey_ref, gvalue_ref, gdecay_ref, sum_ref, key_acc, value_acc, pair_acc,
):
    length = rec_ref.shape[0]
    inclusive = inc_ref[...]
    exclusive = exclusive_of(inclusive)
    final = inclusive[length - 1 :]
    rec, key, value = rec_ref[...], key_ref[...], value_ref[...]
    value_low = low(value)
    grad_low = gwkv_ref[...]
    grad = grad_low.astype(F32)
    bonus = row_ref[9:10]
    state, gstate = widen_state(state_ref), widen_state(gstate_ref)
    pair = head_sum(grad * value)
    shared = pair * bonus
    g_key = shared * rec
    g_value = head_sum(rec * bonus * key) * grad
    g_bonus = jnp.sum(rec * key * pair, 0, keepdims=True)
    fade = jnp.exp(exclusive)
    back = nt(grad_low, state)
    from_state = low(rec * fade).astype(F32) * back
    g_rec = shared * key + fade * back
    fade = jnp.exp(final - inclusive)
    weighted = low(key * fade)
    back = nt(value_low, gstate)
    to_state = weighted.astype(F32) * back
    key_acc[...] = g_key + fade * back
    value_acc[...] = g_value + nn(weighted, gstate)
    pair_acc[...] = jnp.zeros_like(pair_acc)
    rec_parts, own_parts = [], []
    for q in range(length // SUB):
        start, stop, query, fade, mask = sub_block(q, inclusive, exclusive, length)
        left = rec[start:stop] * query
        spread = spread_heads(left)
        right = low(key[:stop] * fade)
        gspread = spread_heads(grad[start:stop])
        scores = low(jnp.where(mask, nt(spread, right), 0.0))
        weight = low(jnp.where(mask, nt(gspread, value_low[:stop]), 0.0))
        back = pick_heads(nn(weight, right))
        rec_parts.append(g_rec[start:stop] + query * back)
        own_parts.append(low(left).astype(F32) * back)
        back = tn(weight, spread)
        key_acc[:stop] += fade * back
        pair_acc[:stop] += right.astype(F32) * back
        value_acc[:stop] += tn(scores, gspread)
    grec_ref[...] = low(jnp.concatenate(rec_parts, 0))
    gkey_ref[...] = low(key_acc[...])
    gvalue_ref[...] = low(value_acc[...])
    inner, pairs = jnp.concatenate(own_parts, 0), pair_acc[...]
    both = head_sum(
        jnp.concatenate([state_ref[0, 0], state_ref[0, 1]], 1).astype(F32)
        * jnp.concatenate([gstate_ref[0, 0], gstate_ref[0, 1]], 1).astype(F32)
    )
    shape = both.shape
    here = lax.rem(lax.broadcasted_iota(jnp.int32, shape, 1), HEAD) == lax.broadcasted_iota(
        jnp.int32, shape, 0
    )
    through = jnp.exp(final) * jnp.sum(jnp.where(here, both, 0.0), 0, keepdims=True)
    later = exact_product(triangle(length, lambda r, c: r < c), inner + from_state - pairs)
    earlier = exact_product(triangle(length, lambda r, c: r > c), to_state)
    g_log = later - pairs + earlier + through
    g_decay = g_log * log_ref[...]
    gdecay_ref[...] = low(g_decay)
    sum_ref[0] = jnp.concatenate(
        [g_bonus, jnp.sum(g_decay, 0, keepdims=True), jnp.zeros((6, SPAN), F32)], 0
    )


def wkv_call(kernel, seqs, ins, outs, name, flops, scratch=()):
    width = ins[0].shape[1]
    length = ins[0].shape[0] // seqs

    def spec(a):
        if len(a.shape) == 4:
            return pl.BlockSpec((1, 2, a.shape[2], LANES), lambda s, g: (s, g, 0, 0))
        if len(a.shape) == 3:
            return pl.BlockSpec((1, 8, SPAN), lambda s, g: (s, 0, g))
        if a.shape[0] == 16:
            return pl.BlockSpec((16, SPAN), lambda s, g: (0, g))
        return pl.BlockSpec((length, SPAN), lambda s, g: (s, g))

    moved = sum(a.size * a.dtype.itemsize for a in ins + outs)
    return pl.pallas_call(
        kernel,
        grid=(seqs, width // SPAN),
        in_specs=[spec(a) for a in ins],
        out_specs=[spec(a) for a in outs],
        out_shape=outs,
        scratch_shapes=scratch,
        compiler_params=pltpu.CompilerParams(vmem_limit_bytes=40 << 20),
        cost_estimate=pl.CostEstimate(flops=flops, transcendentals=0, bytes_accessed=moved),
        name=name,
    )(*ins)


def chain_kernel(first_ref, packed_ref, out_ref, held_fade, *, rows, reverse):
    count = packed_ref.shape[0]
    logs = packed_ref[:, rows : rows + 1], packed_ref[:, rows + 1 : rows + 2]
    shape = (count, rows, LANES)
    lane = lax.rem(lax.broadcasted_iota(jnp.int32, shape, 2), HEAD)
    here = lane == lax.broadcasted_iota(jnp.int32, shape, 1) + first_ref[0]
    ones = head_block(LANES, LANES)
    total = None
    for part in logs:
        part = jnp.where(here, part.astype(F32), 0.0)
        part = nn(low(part.reshape(count * rows, LANES)), ones)
        total = part if total is None else total + part
    held_fade[...] = jnp.exp(total).reshape(shape)

    def one(hop, held):
        b = count - 1 - hop if reverse else hop
        out_ref[b] = low(held)
        return held_fade[b] * held + packed_ref[b, :rows].astype(F32)

    lax.fori_loop(0, count, one, jnp.zeros((rows, LANES), F32))


def chain(state, finals, reverse, beside=None):
    count = lax.axis_size(ALL)
    pairs = state.shape[0] * state.shape[1]
    split = count // pairs
    rows = state.shape[2] // split
    logs = finals.reshape(pairs, finals.shape[2], LANES)
    if split > 1:
        logs = jnp.repeat(logs, split, axis=0)
    packed = jnp.concatenate([state.reshape(count, rows, LANES), logs], 1)
    packed = lax.all_to_all(packed, ALL, 0, 0, tiled=True)
    packed, beside = tie(packed, beside)
    first = lax.rem(lax.axis_index(ALL), split) * rows
    entering = pl.pallas_call(
        lambda *refs: chain_kernel(*refs, rows=rows, reverse=reverse),
        grid_spec=pltpu.PrefetchScalarGridSpec(
            num_scalar_prefetch=1,
            grid=(1,),
            in_specs=[pl.BlockSpec(packed.shape, lambda i, c: (0, 0, 0))],
            out_specs=pl.BlockSpec((count, rows, LANES), lambda i, c: (0, 0, 0)),
            scratch_shapes=[pltpu.VMEM((count, rows, LANES), F32)],
        ),
        out_shape=jax.ShapeDtypeStruct((count, rows, LANES), BF16),
        compiler_params=pltpu.CompilerParams(vmem_limit_bytes=40 << 20),
        name="chain",
    )(first.astype(jnp.int32).reshape(1), packed)
    return lax.all_to_all(entering, ALL, 0, 0, tiled=True).reshape(state.shape), beside


def norm_forward(values, gain, bias):
    mean = jnp.mean(values, -1, keepdims=True)
    centered = values - mean
    rstd = lax.rsqrt(jnp.mean(centered * centered, -1, keepdims=True) + 1e-05)
    hat = centered * rstd
    return hat * gain + bias, hat, rstd


def norm_backward(grad, hat, rstd, gain):
    d = grad * gain
    back = rstd * (
        d - jnp.mean(d, -1, keepdims=True) - hat * jnp.mean(d * hat, -1, keepdims=True)
    )
    return back, jnp.sum(grad * hat, 0, keepdims=True), jnp.sum(grad, 0, keepdims=True)


def prior_of(values, seqs):
    shaped = values.reshape(seqs, -1, values.shape[-1])
    incoming = along(shaped[:, -1], 1)
    return jnp.concatenate([incoming[:, None], shaped[:, :-1]], 1).reshape(values.shape)


def prior_back(grad, seqs):
    shaped = grad.reshape(seqs, -1, grad.shape[-1])
    incoming = along(shaped[:, 0], -1)
    return jnp.concatenate([shaped[:, 1:], incoming[:, None]], 1).reshape(grad.shape)


def stack_nn(value, shards, which, tile=512):
    devices, _, rows, cols = shards.shape

    def kernel(a_ref, w_ref, o_ref):
        w = w_ref[...].reshape(devices * rows, tile)
        o_ref[...] = jnp.dot(a_ref[...], w, preferred_element_type=F32)

    return pl.pallas_call(
        kernel,
        grid=(cols // tile,),
        out_shape=jax.ShapeDtypeStruct((value.shape[0], cols), F32),
        in_specs=[
            pl.BlockSpec(value.shape, lambda j: (0, 0)),
            pl.BlockSpec((devices, 1, rows, tile), lambda j: (0, which, 0, j)),
        ],
        out_specs=pl.BlockSpec((value.shape[0], tile), lambda j: (0, j)),
        compiler_params=pltpu.CompilerParams(vmem_limit_bytes=40 << 20),
        cost_estimate=pl.CostEstimate(
            flops=2 * value.size * cols, transcendentals=0,
            bytes_accessed=2 * value.size + 2 * devices * rows * cols + 4 * value.shape[0] * cols,
        ),
        name="stack_nn",
    )(value, shards)


def stack_nt(value, shards, which, tile=512):
    devices, _, rows, cols = shards.shape
    group = tile // rows

    def kernel(a_ref, w_ref, o_ref):
        w = w_ref[...].reshape(tile, cols)
        o_ref[...] = lax.dot_general(
            a_ref[...], w, (((1,), (1,)), ((), ())), preferred_element_type=F32
        )

    return pl.pallas_call(
        kernel,
        grid=(devices // group,),
        out_shape=jax.ShapeDtypeStruct((value.shape[0], devices * rows), F32),
        in_specs=[
            pl.BlockSpec(value.shape, lambda j: (0, 0)),
            pl.BlockSpec((group, 1, rows, cols), lambda j: (j, which, 0, 0)),
        ],
        out_specs=pl.BlockSpec((value.shape[0], tile), lambda j: (0, j)),
        compiler_params=pltpu.CompilerParams(vmem_limit_bytes=40 << 20),
        cost_estimate=pl.CostEstimate(
            flops=2 * value.size * devices * rows, transcendentals=0,
            bytes_accessed=2 * value.size + 2 * devices * rows * cols
            + 4 * value.shape[0] * devices * rows,
        ),
        name="stack_nt",
    )(value, shards)


def other_half(shards, which):
    core = lax.axis_index("core")
    devices, n, rows, cols = shards.shape
    quarter = cols // 4
    own = lax.dynamic_slice(
        shards, (0, n - 1, 0, (2 * which + core) * quarter), (devices, 1, rows, quarter)
    )
    return swap(own.reshape(devices, rows, quarter), "y")


def places():
    return jnp.stack([lax.axis_index("y"), lax.axis_index("core")]).astype(jnp.int32)


def half_nn(value, shards, which, got, near):
    devices, n, rows, cols = shards.shape
    tile = cols // 4

    def kernel(p_ref, a_ref, w_ref, g_ref, n_ref, o_ref):
        t = pl.program_id(0)

        def put(w):
            w = w.reshape(devices * rows, tile)
            o_ref[...] = jnp.dot(a_ref[...], w, preferred_element_type=F32)

        pl.when(t < 2)(lambda: put(w_ref[...]))
        pl.when(t == 2)(lambda: put(g_ref[...]))
        pl.when(t == 3)(lambda: put(n_ref[...]))

    def out_at(t, p):
        other = 2 * (1 - p[0]) + jnp.where(t == 2, p[1], 1 - p[1])
        return 0, jnp.where(t < 2, 2 * p[0] + t, other)

    whole = pl.BlockSpec(got.shape, lambda t, p: (0, 0, 0))
    return pl.pallas_call(
        kernel,
        grid_spec=pltpu.PrefetchScalarGridSpec(
            num_scalar_prefetch=1,
            grid=(4,),
            in_specs=[
                pl.BlockSpec(value.shape, lambda t, p: (0, 0)),
                pl.BlockSpec(
                    (devices, 1, rows, tile),
                    lambda t, p: (0, n - 1, 0, 2 * which + jnp.minimum(t, 1)),
                ),
                whole,
                whole,
            ],
            out_specs=pl.BlockSpec((value.shape[0], tile), out_at),
        ),
        out_shape=jax.ShapeDtypeStruct((value.shape[0], cols), F32),
        compiler_params=pltpu.CompilerParams(vmem_limit_bytes=48 << 20),
        cost_estimate=pl.CostEstimate(
            flops=2 * value.size * cols, transcendentals=0,
            bytes_accessed=2 * value.size + 2 * devices * rows * cols + 4 * value.shape[0] * cols,
        ),
        name="half_nn",
    )(places(), value, shards, got, near)


def half_nt(value, shards, which, got, near):
    devices, n, rows, cols = shards.shape
    wide = 512
    group = wide // rows
    tile = cols // 4
    tokens = value.shape[0]

    def kernel(p_ref, a_ref, b_ref, c_ref, w_ref, g_ref, n_ref, o_ref):
        total = nt(a_ref[...], w_ref[...].reshape(wide, 2 * tile))
        total = total + nt(b_ref[...], g_ref[...].reshape(wide, tile))
        o_ref[...] = total + nt(c_ref[...], n_ref[...].reshape(wide, tile))

    part = pl.BlockSpec((group, rows, tile), lambda j, p: (j, 0, 0))
    return pl.pallas_call(
        kernel,
        grid_spec=pltpu.PrefetchScalarGridSpec(
            num_scalar_prefetch=1,
            grid=(devices // group,),
            in_specs=[
                pl.BlockSpec((tokens, 2 * tile), lambda j, p: (0, p[0])),
                pl.BlockSpec((tokens, tile), lambda j, p: (0, 2 * (1 - p[0]) + p[1])),
                pl.BlockSpec((tokens, tile), lambda j, p: (0, 2 * (1 - p[0]) + 1 - p[1])),
                pl.BlockSpec((group, 1, rows, 2 * tile), lambda j, p: (j, n - 1, 0, which)),
                part,
                part,
            ],
            out_specs=pl.BlockSpec((tokens, wide), lambda j, p: (0, j)),
        ),
        out_shape=jax.ShapeDtypeStruct((tokens, devices * rows), F32),
        compiler_params=pltpu.CompilerParams(vmem_limit_bytes=40 << 20),
        cost_estimate=pl.CostEstimate(
            flops=2 * value.size * devices * rows, transcendentals=0,
            bytes_accessed=2 * value.size + 2 * devices * rows * cols + 4 * tokens * devices * rows,
        ),
        name="half_nt",
    )(places(), value, value, value, shards, got, near)


TILE = 256


def pack_blocks(shard):
    rows, cols = shard.shape
    return jnp.swapaxes(shard.reshape(rows, cols // TILE, TILE), 0, 1).reshape(-1, TILE)


def ffn_call(kernel, core, grid, ins, specs, outs, out_specs, flops, scratch=(), name=None):
    moved = sum(a.size * a.dtype.itemsize for a in ins[:1] + outs) + flops // 1024
    return pl.pallas_call(
        kernel,
        grid_spec=pltpu.PrefetchScalarGridSpec(
            num_scalar_prefetch=1, grid=grid, in_specs=specs, out_specs=out_specs, scratch_shapes=scratch
        ),
        out_shape=outs,
        compiler_params=pltpu.CompilerParams(vmem_limit_bytes=56 << 20),
        cost_estimate=pl.CostEstimate(flops=flops, transcendentals=0, bytes_accessed=moved),
        name=name,
    )(core.reshape(1), *ins)


class PackedWeights:
    def __init__(self, packed, core, ff, width, half, chips):
        self.packed, self.core = packed, core
        self.devices = packed.shape[0]
        self.rows = width // self.devices
        self.quarter, self.width, self.half, self.chips = ff // 4, width, half, chips
        self.blocks = self.quarter // TILE
        self.fast = half % 16 == 0 and self.rows % 16 == 0 and self.rows == 128

    def _plain(self, start, rows, count):
        part = self.packed[:, start : start + rows * count]
        return part.reshape(-1, count, rows, TILE)

    def plain_key(self):
        start = self.half * (self.width // TILE)
        part = self._plain(start, self.rows, 2 * self.blocks)
        part = piece(part, self.core, self.blocks, 1)
        return jnp.swapaxes(part, 1, 2).reshape(self.width, self.quarter)

    def plain_value(self):
        part = self._plain(0, self.half, self.width // TILE)
        part = lax.dynamic_index_in_dim(
            part.reshape(self.chips, 2, *part.shape[1:]), self.core, 1, False
        )
        return jnp.swapaxes(part, 1, 2).reshape(self.quarter, self.width)

    def plain_rec(self):
        start = self.half * (self.width // TILE) + self.rows * 2 * self.blocks
        part = self._plain(start, self.rows, self.width // TILE)
        return jnp.swapaxes(part, 1, 2).reshape(self.width, self.width)

    def key_forward(self, mix):
        if not self.fast:
            relu = low(jnp.maximum(nn(mix, self.plain_key()), 0.0))
            return relu, low(relu.astype(F32) * relu.astype(F32))
        tokens = mix.shape[0]
        first = self.half * (self.width // TILE) // self.rows

        def kernel(c_ref, a_ref, w_ref, relu_ref, sq_ref):
            w = w_ref[...].reshape(self.width, TILE)
            relu = jnp.maximum(jnp.dot(a_ref[...], w, preferred_element_type=F32), 0.0)
            relu_ref[...] = low(relu)
            sq_ref[...] = low(relu * relu)

        out = jax.ShapeDtypeStruct((tokens, self.quarter), BF16)
        spec = pl.BlockSpec((tokens, TILE), lambda n, c: (0, n))
        return ffn_call(
            kernel, self.core, (self.blocks,), [mix, self.packed],
            [pl.BlockSpec(mix.shape, lambda n, c: (0, 0)),
             pl.BlockSpec((self.devices, self.rows, TILE),
                          lambda n, c: (0, first + c[0] * self.blocks + n, 0))],
            [out, out], [spec, spec], 2 * mix.size * self.quarter, name="key_forward",
        )

    def value_forward(self, squared):
        if not self.fast:
            return low(nn(squared, self.plain_value()))
        tokens = squared.shape[0]
        view = self.packed.reshape(self.chips, 2, *self.packed.shape[1:])

        def kernel(c_ref, a_ref, w_ref, o_ref):
            w = w_ref[...].reshape(self.quarter, TILE)
            o_ref[...] = low(jnp.dot(a_ref[...], w, preferred_element_type=F32))

        return ffn_call(
            kernel, self.core, (self.width // TILE,), [squared, view],
            [pl.BlockSpec(squared.shape, lambda m, c: (0, 0)),
             pl.BlockSpec((self.chips, 1, self.half, TILE), lambda m, c: (0, c[0], m, 0))],
            [jax.ShapeDtypeStruct((tokens, self.width), BF16)],
            [pl.BlockSpec((tokens, TILE), lambda m, c: (0, m))],
            2 * squared.size * self.width, name="value_forward",
        )[0]

    def rec_forward(self, mix):
        if not self.fast:
            return jax.nn.sigmoid(nn(mix, self.plain_rec()))
        tokens = mix.shape[0]
        first = self.packed.shape[1] // self.rows - self.width // TILE

        def kernel(c_ref, a_ref, w_ref, o_ref):
            w = w_ref[...].reshape(self.width, TILE)
            o_ref[...] = jax.nn.sigmoid(jnp.dot(a_ref[...], w, preferred_element_type=F32))

        return ffn_call(
            kernel, self.core, (self.width // TILE,), [mix, self.packed],
            [pl.BlockSpec(mix.shape, lambda m, c: (0, 0)),
             pl.BlockSpec((self.devices, self.rows, TILE), lambda m, c: (0, first + m, 0))],
            [jax.ShapeDtypeStruct((tokens, self.width), F32)],
            [pl.BlockSpec((tokens, TILE), lambda m, c: (0, m))],
            2 * mix.size * self.width, name="rec_forward",
        )[0]

    def value_backward(self, grad, relu):
        if not self.fast:
            return low(nt(grad, self.plain_value()) * 2.0 * relu.astype(F32))
        tokens = grad.shape[0]
        view = self.packed.reshape(self.chips, 2, *self.packed.shape[1:])
        count = self.width // TILE
        part = self.chips // 2

        def kernel(c_ref, a_ref, r_ref, w_ref, o_ref, flat):
            w = w_ref[...].reshape(part, count, self.half, TILE)
            for m in range(count):
                flat[:, m * TILE : (m + 1) * TILE] = w[:, m].reshape(part * self.half, TILE)
            back = lax.dot_general(
                a_ref[...], flat[...], (((1,), (1,)), ((), ())), preferred_element_type=F32
            )
            o_ref[...] = low(back * 2.0 * r_ref[...].astype(F32))

        wide = part * self.half
        return ffn_call(
            kernel, self.core, (2,), [grad, relu, view],
            [pl.BlockSpec(grad.shape, lambda i, c: (0, 0)),
             pl.BlockSpec((tokens, wide), lambda i, c: (0, i)),
             pl.BlockSpec((part, 1, count * self.half, TILE), lambda i, c: (i, c[0], 0, 0))],
            [jax.ShapeDtypeStruct((tokens, self.quarter), BF16)],
            [pl.BlockSpec((tokens, wide), lambda i, c: (0, i))],
            2 * grad.size * self.quarter,
            scratch=(pltpu.VMEM((wide, self.width), BF16),), name="value_backward",
        )[0]

    def key_backward(self, grad):
        if not self.fast:
            return low(nt(grad, self.plain_key()))
        tokens = grad.shape[0]
        part = 4
        rows = self.blocks * self.rows
        first = self.half * (self.width // TILE) // rows

        def kernel(c_ref, a_ref, w_ref, o_ref, flat):
            w = w_ref[...].reshape(part, self.blocks, self.rows, TILE)
            for n in range(self.blocks):
                flat[:, n * TILE : (n + 1) * TILE] = w[:, n].reshape(part * self.rows, TILE)
            o_ref[...] = low(lax.dot_general(
                a_ref[...], flat[...], (((1,), (1,)), ((), ())), preferred_element_type=F32
            ))

        wide = part * self.rows
        return ffn_call(
            kernel, self.core, (self.devices // part,), [grad, self.packed],
            [pl.BlockSpec(grad.shape, lambda i, c: (0, 0)),
             pl.BlockSpec((part, rows, TILE), lambda i, c: (i, first + c[0], 0))],
            [jax.ShapeDtypeStruct((tokens, self.width), BF16)],
            [pl.BlockSpec((tokens, wide), lambda i, c: (0, i))],
            2 * grad.size * self.width,
            scratch=(pltpu.VMEM((wide, self.quarter), BF16),), name="key_backward",
        )[0]

    def rec_backward(self, grad):
        if not self.fast:
            return nt(grad, self.plain_rec())
        tokens = grad.shape[0]
        part, count = 4, self.width // TILE
        rows = count * self.rows // 2
        first = self.packed.shape[1] // rows - 2

        def kernel(c_ref, a_ref, w_ref, v_ref, o_ref, flat):
            for k, ref in enumerate((w_ref, v_ref)):
                w = ref[...].reshape(part, count // 2, self.rows, TILE)
                for n in range(count // 2):
                    m = k * (count // 2) + n
                    flat[:, m * TILE : (m + 1) * TILE] = w[:, n].reshape(part * self.rows, TILE)
            o_ref[...] = lax.dot_general(
                a_ref[...], flat[...], (((1,), (1,)), ((), ())), preferred_element_type=F32
            )

        wide = part * self.rows
        return ffn_call(
            kernel, self.core, (self.devices // part,), [grad, self.packed, self.packed],
            [pl.BlockSpec(grad.shape, lambda i, c: (0, 0)),
             pl.BlockSpec((part, rows, TILE), lambda i, c: (i, first, 0)),
             pl.BlockSpec((part, rows, TILE), lambda i, c: (i, first + 1, 0))],
            [jax.ShapeDtypeStruct((tokens, self.width), F32)],
            [pl.BlockSpec((tokens, wide), lambda i, c: (0, i))],
            2 * grad.size * self.width,
            scratch=(pltpu.VMEM((wide, self.width), BF16),), name="rec_backward",
        )[0]


def body(tokens, att_w, down_w, up_w, key_w, value_w, rec_w, vectors, out_grad):
    seqs, length, width = tokens.shape
    total = seqs * length
    y, core = lax.axis_index("y"), lax.axis_index("core")
    zs = lax.axis_size("z")
    ff = key_w.shape[1]
    share = value_w.shape[0]
    half = share // 2
    quarter = ff // 4

    def rows(v):
        return v.reshape(total, width)

    def columns(shard):
        gathered = lax.all_gather(shard, WIDE, axis=0)
        return jnp.swapaxes(gathered, 0, 1).reshape(shard.shape[0], width)

    cols = up_w.shape[0]
    up_vec = columns(jnp.concatenate([vectors, up_w], 0))
    vec, up = up_vec[:16].astype(F32), up_vec[16:]
    down_t = columns(down_w.T)
    halves = [piece(att_w[i], y, width // 2, 1) for i in (3, 4)]
    w_att = jnp.concatenate([att_w[:3], jnp.concatenate(halves, 1)[None]], 0)
    w_att = lax.all_gather(w_att, WIDE, axis=0)
    key_sh = key_w.reshape(-1, zs, 2, 2, 2, half)
    key_sh = lax.dynamic_index_in_dim(key_sh, y, 4, False)
    key_sh = key_sh.transpose(0, 3, 1, 2, 4).reshape(-1, 2 * quarter)
    packed = jnp.concatenate(
        [pack_blocks(piece(value_w, y, half, 0)), pack_blocks(key_sh), pack_blocks(rec_w)], 0
    )
    packed = lax.all_gather(packed, WIDE, axis=0)

    x = rows(tokens.astype(F32))
    normed, hat, rstd = norm_forward(x, vec[0], vec[1])
    delta = prior_of(normed, seqs) - normed
    mix_low = low(normed + delta * vec[2])
    tanh_mix = jnp.tanh(nt(mix_low, down_t[:MIXCOLS]))
    hidden = low(tanh_mix)
    hid = [hidden[:, i * RANK : (i + 1) * RANK] for i in range(5)]
    ups = [up[i * RANK : (i + 1) * RANK] for i in range(5)]
    mixed = [low(normed + delta * (vec[3 + i] + nn(hid[i], ups[i]))) for i in range(5)]
    decay_in, key_in, value_in, rec_in, gate_in = mixed
    tanh_decay = jnp.tanh(nt(decay_in, down_t[MIXCOLS:]))
    hidden_decay = low(tanh_decay)
    logdecay = -jnp.exp(vec[8] + nn(hidden_decay, up[MIXCOLS:]))
    mix_all = group_pieces([gate_in, rec_in, key_in, value_in])
    w_att, mix_all = tie(w_att, mix_all)
    gate_other = other_half(w_att, 0)
    out_other = other_half(w_att, 1)
    keys = stack_nn(key_in, w_att, 1)
    values = stack_nn(value_in, w_att, 2)
    shaped = jax.ShapeDtypeStruct
    flat, flat_low = shaped((total, width), F32), shaped((total, width), BF16)
    states = shaped((seqs, width // LANES, HEAD, LANES), BF16)
    finals = shaped((seqs, width // LANES, 16, LANES), BF16)
    sums = shaped((seqs, 8, width), F32)
    unit = 2 * total * width
    inclusive, state, final = wkv_call(
        state_kernel, seqs, [keys, values, logdecay], [flat, states, finals], "wkv_state", unit * 512
    )
    carried, gate_other = chain(state, final, False, gate_other)
    gate_other = (gate_other, swap(gate_other, "core"))
    carried, out_other = tie(carried, out_other)
    out_other = (out_other, swap(out_other, "core"))
    recept = stack_nn(rec_in, w_att, 0)
    gate_pre = half_nn(gate_in, w_att, 0, *gate_other)
    wkv, gated = wkv_call(
        wkv_kernel, seqs, [recept, keys, values, inclusive, carried, gate_pre, vec], [flat, flat_low],
        "wkv_forward", unit * 1536,
    )
    first_sum = x + half_nn(gated, w_att, 1, *out_other)

    normed_two, hat_two, rstd_two = norm_forward(first_sum, vec[12], vec[13])
    delta_two = prior_of(normed_two, seqs) - normed_two
    key_mix = low(normed_two + delta_two * vec[14])
    rec_mix = low(normed_two + delta_two * vec[15])
    key_all = group_many([key_mix])[0]
    gated_all = group_pieces([gated])
    packed, key_all, gated_all = tie(packed, key_all, gated_all)
    ffn = PackedWeights(packed, core, ff, width, half, 2 * zs)
    relu, squared = ffn.key_forward(key_all)
    value_out = group_sum(ffn.value_forward(squared))
    rec_gate = ffn.rec_forward(rec_mix)
    block_out = low(first_sum + rec_gate * value_out).reshape(tokens.shape)

    g = rows(out_grad.astype(F32))
    grad_value = low(g * rec_gate)
    grad_gate_in = low(g * value_out * rec_gate * (1.0 - rec_gate))
    value_all = group_many([grad_value])[0]
    value_part = low(tn(squared, value_all)).reshape(-1, half, width)
    value_part, value_all = tie(value_part, value_all)
    value_part = lax.psum_scatter(value_part, ("z", "x"), scatter_dimension=0, tiled=True)[0]
    grad_key_pre = ffn.value_backward(value_all, relu)
    g_key_mix = ffn.key_backward(grad_key_pre)
    grad_key_pre, g_key_mix = tie(grad_key_pre, g_key_mix)
    key_part = low(tn(key_all, grad_key_pre))
    key_part = lax.psum_scatter(key_part, ("z", "x"), scatter_dimension=0, tiled=True)
    g_key_mix = group_sum(g_key_mix)
    g_rec_mix = ffn.rec_backward(grad_gate_in)

    g_prior = prior_back(g_key_mix * vec[14] + g_rec_mix * vec[15], seqs)
    g_normed_two = g_key_mix * (1.0 - vec[14]) + g_rec_mix * (1.0 - vec[15]) + g_prior
    g_maa_key = jnp.sum(g_key_mix * delta_two, 0, keepdims=True)
    g_maa_rec = jnp.sum(g_rec_mix * delta_two, 0, keepdims=True)
    back_two, g_gain_two, g_bias_two = norm_backward(g_normed_two, hat_two, rstd_two, vec[12])
    grad_first = g + back_two

    grad_att = low(grad_first)
    g_wkv, g_gate_low, g_state, gate_sums = wkv_call(
        gate_back_kernel, seqs,
        [half_nt(grad_att, w_att, 1, *out_other), wkv, gate_pre, recept, inclusive, vec],
        [flat_low, flat_low, states, sums], "gate_backward", unit * 1536,
    )
    g_state_out, (rights, rec_low) = chain(
        g_state, final, True, ([grad_gate_in, grad_att, g_gate_low], rec_mix)
    )
    side_near, side_across = half_cols(jnp.stack(rights, 0))
    rec_low = rec_low[None]
    rec_near, rec_across = swap(rec_low, "core"), swap(rec_low, "y")
    g_state_out, value_part = tie(g_state_out, value_part)
    g_rec, g_key, g_val, g_decay_low, wkv_sums = wkv_call(
        wkv_back_kernel, seqs,
        [recept, keys, values, inclusive, logdecay, carried, g_state_out, g_wkv, vec],
        [flat_low, flat_low, flat_low, flat_low, sums], "wkv_backward", unit * 4096,
        scratch=[pltpu.VMEM((length, SPAN), F32)] * 3,
    )
    gate_sums, wkv_sums = jnp.sum(gate_sums, 0), jnp.sum(wkv_sums, 0)
    projs = [g_rec, g_key, g_val, g_gate_low]
    main_near, main_across = half_cols(jnp.stack([g_rec, g_key, g_val], 0))
    main_near, side_across, rec_across = tie(main_near, side_across, rec_across)
    rec_all = (rec_low, rec_near, rec_across, swap(rec_across, "core"))
    side_lefts = [(rec_all, 0, 1), (gated_all, 0, 1), (mix_all, 0, 1)]
    side_right, g_rec, g_key = tie(quarter_cols(side_near, side_across), g_rec, g_key)
    side_give = x_rows(side_lefts, side_right, False)
    side_got = swap(side_give, "x")
    main_across, side_give = tie(main_across, side_give)
    main = all_rows([(mix_all, 1, 3)], quarter_cols(main_near, main_across))
    main, key_part, side_right, g_val, g_gate_low, g_decay_low = tie(
        main, key_part, side_right, g_val, g_gate_low, g_decay_low
    )
    side_keep = x_rows(side_lefts, side_right, True)
    main = lax.psum_scatter(main, ("z", "x"), scatter_dimension=0, tiled=True)
    projs = [g_rec, g_key, g_val, g_gate_low]

    decay_up_grad = tn(hidden_decay, g_decay_low)
    g_pre_decay = low(nt(g_decay_low, up[MIXCOLS:]) * (1.0 - tanh_decay * tanh_decay))
    decay_down_grad = tn(g_pre_decay, decay_in)
    g_mixed = [
        nn(g_pre_decay, down_t[MIXCOLS:]),
        stack_nt(projs[1], w_att, 1),
        stack_nt(projs[2], w_att, 2),
        stack_nt(projs[0], w_att, 0),
        half_nt(projs[3], w_att, 0, *gate_other),
    ]
    g_normed = g_prior_sum = None
    maa_rows, up_grads, hid_grads = [], [], []
    for i in range(5):
        offset = vec[3 + i] + nn(hid[i], ups[i])
        g_off = g_mixed[i] * delta
        maa_rows.append(jnp.sum(g_off, 0, keepdims=True))
        off_low = low(g_off)
        up_grads.append(tn(hid[i], off_low))
        hid_grads.append(nt(off_low, ups[i]))
        here = g_mixed[i] * (1.0 - offset)
        back = g_mixed[i] * offset
        g_normed = here if g_normed is None else g_normed + here
        g_prior_sum = back if g_prior_sum is None else g_prior_sum + back
    g_pre_mix = low(jnp.concatenate(hid_grads, 1) * (1.0 - tanh_mix * tanh_mix))
    mix_down_grad = tn(g_pre_mix, mix_low)
    g_first_mix = nn(g_pre_mix, down_t[:MIXCOLS])
    maa_first = jnp.sum(g_first_mix * delta, 0, keepdims=True)
    g_prior_sum = g_prior_sum + g_first_mix * vec[2]
    g_normed = g_normed + g_first_mix * (1.0 - vec[2]) + prior_back(g_prior_sum, seqs)
    g_normed, side_got = tie(g_normed, side_got)
    side = low(side_keep.astype(F32) + side_got.astype(F32))
    side = side.reshape(zs, -1, side.shape[1])
    moving = line_step(side, 1, None)
    g_gain = jnp.sum(g_normed * hat, 0, keepdims=True)
    g_bias = jnp.sum(g_normed, 0, keepdims=True)

    vec_rows = (
        [g_gain, g_bias, maa_first] + maa_rows
        + [wkv_sums[1:2], wkv_sums[0:1], gate_sums[0:1], gate_sums[1:2], g_gain_two, g_bias_two,
           g_maa_key, g_maa_rec]
    )
    packed = pack_columns(up_grads + [decay_up_grad, mix_down_grad, decay_down_grad] + vec_rows)
    packed, moving, value_part = tie(packed, moving, value_part)
    for t in range(2, zs - 1):
        moving = line_step(side, t, moving)
    first = y == 0
    other = swap(value_part, "y")
    value_share = jnp.concatenate(
        [jnp.where(first, value_part, other), jnp.where(first, other, value_part)], 0
    ).astype(F32)
    packed, moving, value_share, main, g_normed, key_part = tie(
        packed, moving, value_share, main, g_normed, key_part
    )
    late = spread_cols(main.reshape(main.shape[0], 3, -1))
    key_share = spread_cols(key_part[:, None])[0].reshape(-1, 2, 2, zs, 2, half)
    key_share = key_share.transpose(0, 3, 4, 2, 1, 5).reshape(-1, ff)
    moving = line_step(side, zs - 1, moving)
    back_one, _, _ = norm_backward(g_normed, hat, rstd, vec[0])
    input_grad = (grad_first + back_one).reshape(tokens.shape)
    packed = small_cross(small_core(packed))
    packed, moving, key_share, late = tie(packed, moving, key_share, late)
    side = low(line_end(side, moving))
    early = spread_cols(side.reshape(side.shape[0], 3, -1))
    packed = small_sum(packed)
    rec_share = early[0]
    att_share = jnp.stack(late + [early[2], early[1]], 0)
    return (
        block_out, input_grad, att_share, packed[cols : 2 * cols].T, packed[:cols],
        key_share, value_share, rec_share, packed[2 * cols :],
    )


def solution(mesh):
    seq, wide = mesh.devices.shape
    fine = Mesh(mesh.devices.reshape(seq, wide // 4, 2, 2), ALL)
    token = P(None, ALL, None)
    by_row, by_col, stacked = P(WIDE, None), P(None, WIDE), P(None, WIDE, None)
    return jax.shard_map(
        body,
        mesh=fine,
        in_specs=(token, stacked, by_row, by_col, by_row, by_row, by_row, by_col, token),
        out_specs=(token, token, stacked, by_row, by_col, by_row, by_row, by_row, by_col),
        check_vma=False,
    )
```

```python
import jax
import jax.numpy as jnp
from jax import lax
from jax.experimental import pallas as pl
from jax.experimental.pallas import tpu as pltpu
from jax.sharding import Mesh
from jax.sharding import PartitionSpec as P

HEAD = 64
RANK = 32
MIXCOLS = 5 * RANK
LANES = 128
F32, BF16 = jnp.float32, jnp.bfloat16
WIDE = ("z", "x", "core")
ALL = ("y", "z", "x", "core")


def nn(a, b):
    return jnp.dot(a, b, preferred_element_type=F32)


def nt(a, b):
    return lax.dot_general(a, b, (((1,), (1,)), ((), ())), preferred_element_type=F32)


def tn(a, b):
    return lax.dot_general(a, b, (((0,), (0,)), ((), ())), preferred_element_type=F32)


def low(a):
    return a.astype(BF16)


def swap(value, axis):
    return lax.ppermute(value, axis, [(0, 1), (1, 0)])


def along(value, step):
    count = lax.axis_size(ALL)
    if step > 0:
        pairs = [(i, i + 1) for i in range(count - 1)]
    else:
        pairs = [(i + 1, i) for i in range(count - 1)]
    return lax.ppermute(value, ALL, pairs)


def piece(value, index, size, axis):
    start = [0] * value.ndim
    start[axis] = index * size
    shape = list(value.shape)
    shape[axis] = size
    return lax.dynamic_slice(value, start, shape)


def line_own(block, index):
    count = lax.axis_size("z")
    return lax.dynamic_index_in_dim(block, jnp.clip(index, 0, count - 1), 0, False).astype(F32)


def line_step(block, t, moving):
    count, place = lax.axis_size("z"), lax.axis_index("z")
    right = line_own(block, count - t + place)
    left = line_own(block, place + t - count)
    if moving is not None:
        right, left = right + moving[0].astype(F32), left + moving[1].astype(F32)
    up = lax.ppermute(low(right), "z", [(i, i + 1) for i in range(count - 1) if i <= t - 1])
    down = lax.ppermute(
        low(left), "z", [(i, i - 1) for i in range(1, count) if count - 1 - i <= t - 1]
    )
    return up, down


def line_end(block, moving):
    own = line_own(block, lax.axis_index("z"))
    return own + moving[0].astype(F32) + moving[1].astype(F32)


def line_sum(block):
    moving = None
    for t in range(1, lax.axis_size("z")):
        moving = line_step(block, t, moving)
    return line_end(block, moving)


def pack_columns(parts):
    width = parts[0].shape[1]
    counts = [p.shape[0] for p in parts]
    rows = sum(counts)
    step = 4
    block = step * LANES

    def kernel(*refs):
        out = refs[-1]
        start = 0
        while start < len(counts):
            take, n = [], 0
            while n == 0 or n % 8:
                take.append(refs[start][...])
                n += counts[start]
                start += 1
            first = sum(counts[: start - len(take)])
            rows_here = take[0] if len(take) == 1 else jnp.concatenate(take, 0)
            for b in range(step):
                out[b, first : first + n] = rows_here[:, b * LANES : (b + 1) * LANES]

    return pl.pallas_call(
        kernel,
        grid=(width // block,),
        in_specs=[pl.BlockSpec((c, block), lambda j: (0, j)) for c in counts],
        out_specs=pl.BlockSpec((step, rows, LANES), lambda j: (j, 0, 0)),
        out_shape=jax.ShapeDtypeStruct((width // LANES, rows, LANES), F32),
        compiler_params=pltpu.CompilerParams(vmem_limit_bytes=40 << 20),
        name="pack_columns",
    )(*parts)


def small_core(value):
    z, rows = lax.axis_size("z"), value.shape[1]
    share = 16 * LANES // (4 * z)
    if share != LANES:
        value = value.reshape(16, rows, LANES // share, share).swapaxes(1, 2).reshape(-1, rows, share)
    core = lax.axis_index("core")
    value = value.reshape(2 * z, 2, rows, share)
    give = low(lax.dynamic_index_in_dim(value, 1 - core, 1, False))
    value = lax.dynamic_index_in_dim(value, core, 1, False) + swap(give, "core").astype(F32)
    return value.reshape(z, 2, rows, share)


def small_cross(value):
    x = lax.axis_index("x")
    give = low(lax.dynamic_index_in_dim(value, 1 - x, 1, False))
    return lax.dynamic_index_in_dim(value, x, 1, False) + swap(give, "x").astype(F32)


def small_sum(value):
    count, place = lax.axis_size("z"), lax.axis_index("z")
    reach = count // 2
    while reach:
        value = value.reshape(2, reach, *value.shape[1:])
        bit = lax.rem(place // reach, 2)
        give = low(lax.dynamic_index_in_dim(value, 1 - bit, 0, False))
        got = lax.ppermute(give, "z", [(i, i ^ reach) for i in range(count)])
        value = lax.dynamic_index_in_dim(value, bit, 0, False) + got.astype(F32)
        reach //= 2
    value = value[0]
    return value + swap(value, "y")


def tie(*values):
    return lax.optimization_barrier(values)


def half_cols(right):
    y = lax.axis_index("y")
    half = right.shape[2] // 2
    return piece(right, y, half, 2), swap(piece(right, 1 - y, half, 2), "y")


def quarter_cols(near, across):
    core = lax.axis_index("core")
    both = jnp.stack([near, across], 1)
    quarter = near.shape[2] // 2
    mine = piece(both, core, quarter, 3)
    other = swap(piece(both, 1 - core, quarter, 3), "core")
    both = jnp.stack([mine, other], 2)
    return both.reshape(near.shape[0], -1, quarter)


def spread_cols(part):
    y, core = lax.axis_index("y"), lax.axis_index("core")
    rows = part.shape[0] // 2
    keep = piece(part, core, rows, 0)
    give = piece(part, 1 - core, rows, 0)
    near, across = swap(give, "core"), swap(keep, "y")
    far = lax.ppermute(give, ("y", "core"), [(0, 3), (1, 2), (2, 1), (3, 0)])
    quarters = []
    for q in range(4):
        this, that = jnp.where(core == q % 2, keep, near), jnp.where(core == q % 2, across, far)
        quarters.append(jnp.where(y == q // 2, this, that))
    outs = [
        jnp.concatenate([a[:, i].astype(F32) for a in quarters], 1) for i in range(part.shape[1])
    ]
    return outs


def x_parts(part):
    x, z = lax.axis_index("x"), lax.axis_size("z")
    view = part.reshape(z, 2, -1, part.shape[1])
    give = lax.dynamic_index_in_dim(view, 1 - x, 1, False)
    keep = lax.dynamic_index_in_dim(view, x, 1, False)
    return give.reshape(-1, part.shape[1]), keep.reshape(-1, part.shape[1])


def z_sum(keep, got):
    part = low(keep.astype(F32) + got.astype(F32))
    return lax.psum_scatter(part, "z", scatter_dimension=0, tiled=True)


def grad_call(lefts, rights, block, count, place):
    total, tokens, q = rights.shape
    bounds, arrays, specs = [0], [], []

    def left_spec(low_end, high_end, first, rows):
        def index(i, j, x):
            inside = jnp.logical_and(i >= low_end, i < high_end)
            which = jnp.clip(i, low_end, high_end - 1) - low_end + first
            at = jnp.where(inside, place(j, x[0]), place(jnp.where(i < low_end, 0, count - 1), x[0]))
            return which, 0, at

        return pl.BlockSpec((1, rows, block), index)

    for pieces, first, many in lefts:
        bounds.append(bounds[-1] + many)
        arrays.extend(pieces)
        specs.extend(left_spec(bounds[-2], bounds[-1], first, p.shape[1]) for p in pieces)

    def kernel(x_ref, *refs):
        *a_refs, b_ref, o_ref = refs
        i = pl.program_id(0)
        parts = len(lefts[0][0])
        for k in range(len(lefts)):

            @pl.when(jnp.logical_and(i >= bounds[k], i < bounds[k + 1]))
            def _(mine=a_refs[k * parts : (k + 1) * parts]):
                left = jnp.concatenate([a[0] for a in mine], 0)
                o_ref[...] = low(tn(left, b_ref[0]))

    return pl.pallas_call(
        kernel,
        grid_spec=pltpu.PrefetchScalarGridSpec(
            num_scalar_prefetch=1,
            grid=(total, count),
            in_specs=specs + [pl.BlockSpec((1, tokens, q), lambda i, j, x: (i, 0, 0))],
            out_specs=pl.BlockSpec((block, q), lambda i, j, x: (j, i)),
        ),
        out_shape=jax.ShapeDtypeStruct((count * block, total * q), BF16),
        compiler_params=pltpu.CompilerParams(vmem_limit_bytes=40 << 20),
        cost_estimate=pl.CostEstimate(
            flops=2 * rights.size * count * block, transcendentals=0,
            bytes_accessed=2 * (tokens * total * count * block + rights.size + count * block * total * q),
        ),
        name="weight_grad",
    )(lax.axis_index("x").astype(jnp.int32).reshape(1), *arrays, rights)


def all_rows(lefts, rights):
    return grad_call(lefts, rights, 512, lefts[0][0][0].shape[2] // 512, lambda j, x: j)


def x_rows(lefts, rights, own):
    z = lax.axis_size("z")
    block = lefts[0][0][0].shape[2] // (2 * z)
    if block % LANES:
        return x_parts(all_rows(lefts, rights))[int(own)]
    if own:
        return grad_call(lefts, rights, block, z, lambda j, x: 2 * j + x)
    return grad_call(lefts, rights, block, z, lambda j, x: 2 * j + 1 - x)


def group_pieces(values):
    value = jnp.stack(values, 0)
    near = swap(value, "core")
    across = swap(value, "y")
    far = swap(across, "core")
    return value, near, across, far


def group_many(values):
    return jnp.concatenate(group_pieces(values), 1)


def group_sum(value):
    rows = value.shape[0] // 4
    pair = value.reshape(2, 2, rows, -1)
    got = swap(pair[:, 1], "core")
    across = swap(low(pair[1, 0].astype(F32) + got[1].astype(F32)), "y")
    return pair[0, 0].astype(F32) + got[0].astype(F32) + across.astype(F32)


SPAN = 256
GROUP = SPAN // HEAD
SUB = 32


def lane_head(shape, dim):
    return lax.broadcasted_iota(jnp.int32, shape, dim) // HEAD


def head_block(rows, cols):
    shape = (rows, cols)
    return jnp.where(lane_head(shape, 0) == lane_head(shape, 1), 1.0, 0.0).astype(BF16)


def head_sum(value):
    coarse = low(value)
    fine = low(value - coarse.astype(F32))
    ones = head_block(SPAN, SPAN)
    return nn(coarse, ones) + nn(fine, ones)


def exact_product(left, value):
    coarse = low(value)
    rest = value - coarse.astype(F32)
    fine = low(rest)
    last = low(rest - fine.astype(F32))
    return nn(left, coarse) + (nn(left, fine) + nn(left, last))


def triangle(length, keep):
    shape = (length, length)
    row = lax.broadcasted_iota(jnp.int32, shape, 0)
    col = lax.broadcasted_iota(jnp.int32, shape, 1)
    return jnp.where(keep(row, col), 1.0, 0.0).astype(BF16)


def spread_heads(value):
    lane = lane_head(value.shape, 1)
    return jnp.concatenate([low(jnp.where(lane == h, value, 0.0)) for h in range(GROUP)], 0)


def pick_heads(value):
    rows = value.shape[0] // GROUP
    lane = lane_head((rows, SPAN), 1)
    out = value[:rows]
    for h in range(1, GROUP):
        out = jnp.where(lane == h, value[h * rows : (h + 1) * rows], out)
    return out


def widen_state(ref):
    state = jnp.concatenate([ref[0, 0], ref[0, 1]], 1)
    return jnp.concatenate(
        [jnp.where(lane_head(state.shape, 1) == h, state, jnp.zeros_like(state)) for h in range(GROUP)], 0
    )


def store_state(ref, value):
    state = low(pick_heads(value))
    ref[0, 0] = state[:, :LANES]
    ref[0, 1] = state[:, LANES:]


def exclusive_of(inclusive):
    return jnp.concatenate([jnp.zeros_like(inclusive[:1]), inclusive[:-1]], 0)


def cap(value):
    return jnp.exp(jnp.minimum(value, 80.0))


def state_kernel(key_ref, value_ref, log_ref, inc_ref, state_ref, final_ref):
    length = log_ref.shape[0]
    inclusive = exact_product(triangle(length, lambda r, c: r >= c), log_ref[...])
    inc_ref[...] = inclusive
    final = inclusive[length - 1 :]
    weighted = low(key_ref[...] * jnp.exp(final - inclusive))
    store_state(state_ref, tn(weighted, low(value_ref[...])))
    coarse = low(final)
    fine = low(final - coarse.astype(F32))
    rows = jnp.concatenate([coarse, fine, jnp.zeros((14, SPAN), BF16)], 0)
    final_ref[0, 0] = rows[:, :LANES]
    final_ref[0, 1] = rows[:, LANES:]


def sub_block(q, inclusive, exclusive, length):
    start, stop = q * SUB, (q + 1) * SUB
    middle = inclusive[start + SUB // 2 - 1 : start + SUB // 2]
    query = cap(exclusive[start:stop] - middle)
    key = cap(middle - inclusive[:stop])
    shape = (GROUP * SUB, stop)
    row = lax.rem(lax.broadcasted_iota(jnp.int32, shape, 0), SUB) + start
    mask = row > lax.broadcasted_iota(jnp.int32, shape, 1)
    return start, stop, query, key, mask


def wkv_kernel(rec_ref, key_ref, value_ref, inc_ref, state_ref, gate_ref, row_ref, wkv_ref, gated_ref):
    length = rec_ref.shape[0]
    inclusive = inc_ref[...]
    exclusive = exclusive_of(inclusive)
    rec, key, value = rec_ref[...], key_ref[...], value_ref[...]
    value_low = low(value)
    bonus, gain, bias = row_ref[9:10], row_ref[10:11], row_ref[11:12]
    answer = nn(low(rec * jnp.exp(exclusive)), widen_state(state_ref))
    answer = answer + head_sum(rec * bonus * key) * value
    parts = []
    for q in range(length // SUB):
        start, stop, query, fade, mask = sub_block(q, inclusive, exclusive, length)
        left = spread_heads(rec[start:stop] * query)
        scores = nt(left, low(key[:stop] * fade))
        scores = low(jnp.where(mask, scores, 0.0))
        parts.append(pick_heads(nn(scores, value_low[:stop])))
    answer = answer + jnp.concatenate(parts, 0)
    wkv_ref[...] = answer
    centered = answer - head_sum(answer) * (1.0 / HEAD)
    spread = head_sum(centered * centered) * (1.0 / HEAD)
    grouped = centered * lax.rsqrt(spread + 0.00064) * gain + bias
    gate = gate_ref[...]
    gated_ref[...] = low(grouped * gate / (1.0 + jnp.exp(-gate)))


def gate_back_kernel(grad_ref, wkv_ref, gate_ref, rec_ref, inc_ref, row_ref, gwkv_ref, ggate_ref, state_ref, sum_ref):
    gain, bias = row_ref[10:11], row_ref[11:12]
    answer, gate, grad = wkv_ref[...], gate_ref[...], grad_ref[...]
    centered = answer - head_sum(answer) * (1.0 / HEAD)
    rstd = lax.rsqrt(head_sum(centered * centered) * (1.0 / HEAD) + 0.00064)
    hat = centered * rstd
    grouped = hat * gain + bias
    sig = 1.0 / (1.0 + jnp.exp(-gate))
    g_grouped = grad * gate * sig
    ggate_ref[...] = low(grad * grouped * sig * (1.0 + gate * (1.0 - sig)))
    g_gain = jnp.sum(g_grouped * hat, 0, keepdims=True)
    g_bias = jnp.sum(g_grouped, 0, keepdims=True)
    sum_ref[0] = jnp.concatenate([g_gain, g_bias, jnp.zeros((6, SPAN), F32)], 0)
    g_hat = g_grouped * gain
    back = rstd * (
        g_hat - head_sum(g_hat) * (1.0 / HEAD) - hat * (head_sum(g_hat * hat) * (1.0 / HEAD))
    )
    back = low(back)
    gwkv_ref[...] = back
    query = low(rec_ref[...] * jnp.exp(exclusive_of(inc_ref[...])))
    store_state(state_ref, tn(query, back))


def wkv_back_kernel(
    rec_ref, key_ref, value_ref, inc_ref, log_ref, state_ref, gstate_ref, gwkv_ref, row_ref,
    grec_ref, gkey_ref, gvalue_ref, gdecay_ref, sum_ref, key_acc, value_acc, pair_acc,
):
    length = rec_ref.shape[0]
    inclusive = inc_ref[...]
    exclusive = exclusive_of(inclusive)
    final = inclusive[length - 1 :]
    rec, key, value = rec_ref[...], key_ref[...], value_ref[...]
    value_low = low(value)
    grad_low = gwkv_ref[...]
    grad = grad_low.astype(F32)
    bonus = row_ref[9:10]
    state, gstate = widen_state(state_ref), widen_state(gstate_ref)
    pair = head_sum(grad * value)
    shared = pair * bonus
    g_key = shared * rec
    g_value = head_sum(rec * bonus * key) * grad
    g_bonus = jnp.sum(rec * key * pair, 0, keepdims=True)
    fade = jnp.exp(exclusive)
    back = nt(grad_low, state)
    from_state = low(rec * fade).astype(F32) * back
    g_rec = shared * key + fade * back
    fade = jnp.exp(final - inclusive)
    weighted = low(key * fade)
    back = nt(value_low, gstate)
    to_state = weighted.astype(F32) * back
    key_acc[...] = g_key + fade * back
    value_acc[...] = g_value + nn(weighted, gstate)
    pair_acc[...] = jnp.zeros_like(pair_acc)
    rec_parts, own_parts = [], []
    for q in range(length // SUB):
        start, stop, query, fade, mask = sub_block(q, inclusive, exclusive, length)
        left = rec[start:stop] * query
        spread = spread_heads(left)
        right = low(key[:stop] * fade)
        gspread = spread_heads(grad[start:stop])
        scores = low(jnp.where(mask, nt(spread, right), 0.0))
        weight = low(jnp.where(mask, nt(gspread, value_low[:stop]), 0.0))
        back = pick_heads(nn(weight, right))
        rec_parts.append(g_rec[start:stop] + query * back)
        own_parts.append(low(left).astype(F32) * back)
        back = tn(weight, spread)
        key_acc[:stop] += fade * back
        pair_acc[:stop] += right.astype(F32) * back
        value_acc[:stop] += tn(scores, gspread)
    grec_ref[...] = low(jnp.concatenate(rec_parts, 0))
    gkey_ref[...] = low(key_acc[...])
    gvalue_ref[...] = low(value_acc[...])
    inner, pairs = jnp.concatenate(own_parts, 0), pair_acc[...]
    both = head_sum(
        jnp.concatenate([state_ref[0, 0], state_ref[0, 1]], 1).astype(F32)
        * jnp.concatenate([gstate_ref[0, 0], gstate_ref[0, 1]], 1).astype(F32)
    )
    shape = both.shape
    here = lax.rem(lax.broadcasted_iota(jnp.int32, shape, 1), HEAD) == lax.broadcasted_iota(
        jnp.int32, shape, 0
    )
    through = jnp.exp(final) * jnp.sum(jnp.where(here, both, 0.0), 0, keepdims=True)
    later = exact_product(triangle(length, lambda r, c: r < c), inner + from_state - pairs)
    earlier = exact_product(triangle(length, lambda r, c: r > c), to_state)
    g_log = later - pairs + earlier + through
    g_decay = g_log * log_ref[...]
    gdecay_ref[...] = low(g_decay)
    sum_ref[0] = jnp.concatenate(
        [g_bonus, jnp.sum(g_decay, 0, keepdims=True), jnp.zeros((6, SPAN), F32)], 0
    )


def wkv_call(kernel, seqs, ins, outs, name, flops, scratch=()):
    width = ins[0].shape[1]
    length = ins[0].shape[0] // seqs

    def spec(a):
        if len(a.shape) == 4:
            return pl.BlockSpec((1, 2, a.shape[2], LANES), lambda s, g: (s, g, 0, 0))
        if len(a.shape) == 3:
            return pl.BlockSpec((1, 8, SPAN), lambda s, g: (s, 0, g))
        if a.shape[0] == 16:
            return pl.BlockSpec((16, SPAN), lambda s, g: (0, g))
        return pl.BlockSpec((length, SPAN), lambda s, g: (s, g))

    moved = sum(a.size * a.dtype.itemsize for a in ins + outs)
    return pl.pallas_call(
        kernel,
        grid=(seqs, width // SPAN),
        in_specs=[spec(a) for a in ins],
        out_specs=[spec(a) for a in outs],
        out_shape=outs,
        scratch_shapes=scratch,
        compiler_params=pltpu.CompilerParams(vmem_limit_bytes=40 << 20),
        cost_estimate=pl.CostEstimate(flops=flops, transcendentals=0, bytes_accessed=moved),
        name=name,
    )(*ins)


def chain_kernel(first_ref, packed_ref, out_ref, held_fade, *, rows, reverse):
    count = packed_ref.shape[0]
    logs = packed_ref[:, rows : rows + 1], packed_ref[:, rows + 1 : rows + 2]
    shape = (count, rows, LANES)
    lane = lax.rem(lax.broadcasted_iota(jnp.int32, shape, 2), HEAD)
    here = lane == lax.broadcasted_iota(jnp.int32, shape, 1) + first_ref[0]
    ones = head_block(LANES, LANES)
    total = None
    for part in logs:
        part = jnp.where(here, part.astype(F32), 0.0)
        part = nn(low(part.reshape(count * rows, LANES)), ones)
        total = part if total is None else total + part
    held_fade[...] = jnp.exp(total).reshape(shape)

    def one(hop, held):
        b = count - 1 - hop if reverse else hop
        out_ref[b] = low(held)
        return held_fade[b] * held + packed_ref[b, :rows].astype(F32)

    lax.fori_loop(0, count, one, jnp.zeros((rows, LANES), F32))


def chain(state, finals, reverse, beside=None):
    count = lax.axis_size(ALL)
    pairs = state.shape[0] * state.shape[1]
    split = count // pairs
    rows = state.shape[2] // split
    logs = finals.reshape(pairs, finals.shape[2], LANES)
    if split > 1:
        logs = jnp.repeat(logs, split, axis=0)
    packed = jnp.concatenate([state.reshape(count, rows, LANES), logs], 1)
    packed = lax.all_to_all(packed, ALL, 0, 0, tiled=True)
    packed, beside = tie(packed, beside)
    first = lax.rem(lax.axis_index(ALL), split) * rows
    entering = pl.pallas_call(
        lambda *refs: chain_kernel(*refs, rows=rows, reverse=reverse),
        grid_spec=pltpu.PrefetchScalarGridSpec(
            num_scalar_prefetch=1,
            grid=(1,),
            in_specs=[pl.BlockSpec(packed.shape, lambda i, c: (0, 0, 0))],
            out_specs=pl.BlockSpec((count, rows, LANES), lambda i, c: (0, 0, 0)),
            scratch_shapes=[pltpu.VMEM((count, rows, LANES), F32)],
        ),
        out_shape=jax.ShapeDtypeStruct((count, rows, LANES), BF16),
        compiler_params=pltpu.CompilerParams(vmem_limit_bytes=40 << 20),
        name="chain",
    )(first.astype(jnp.int32).reshape(1), packed)
    return lax.all_to_all(entering, ALL, 0, 0, tiled=True).reshape(state.shape), beside


def norm_forward(values, gain, bias):
    mean = jnp.mean(values, -1, keepdims=True)
    centered = values - mean
    rstd = lax.rsqrt(jnp.mean(centered * centered, -1, keepdims=True) + 1e-05)
    hat = centered * rstd
    return hat * gain + bias, hat, rstd


def norm_backward(grad, hat, rstd, gain):
    d = grad * gain
    back = rstd * (
        d - jnp.mean(d, -1, keepdims=True) - hat * jnp.mean(d * hat, -1, keepdims=True)
    )
    return back, jnp.sum(grad * hat, 0, keepdims=True), jnp.sum(grad, 0, keepdims=True)


def prior_of(values, seqs):
    shaped = values.reshape(seqs, -1, values.shape[-1])
    incoming = along(shaped[:, -1], 1)
    return jnp.concatenate([incoming[:, None], shaped[:, :-1]], 1).reshape(values.shape)


def prior_back(grad, seqs):
    shaped = grad.reshape(seqs, -1, grad.shape[-1])
    incoming = along(shaped[:, 0], -1)
    return jnp.concatenate([shaped[:, 1:], incoming[:, None]], 1).reshape(grad.shape)


def stack_nn(value, shards, which, tile=512):
    devices, _, rows, cols = shards.shape

    def kernel(a_ref, w_ref, o_ref):
        w = w_ref[...].reshape(devices * rows, tile)
        o_ref[...] = jnp.dot(a_ref[...], w, preferred_element_type=F32)

    return pl.pallas_call(
        kernel,
        grid=(cols // tile,),
        out_shape=jax.ShapeDtypeStruct((value.shape[0], cols), F32),
        in_specs=[
            pl.BlockSpec(value.shape, lambda j: (0, 0)),
            pl.BlockSpec((devices, 1, rows, tile), lambda j: (0, which, 0, j)),
        ],
        out_specs=pl.BlockSpec((value.shape[0], tile), lambda j: (0, j)),
        compiler_params=pltpu.CompilerParams(vmem_limit_bytes=40 << 20),
        cost_estimate=pl.CostEstimate(
            flops=2 * value.size * cols, transcendentals=0,
            bytes_accessed=2 * value.size + 2 * devices * rows * cols + 4 * value.shape[0] * cols,
        ),
        name="stack_nn",
    )(value, shards)


def stack_nt(value, shards, which, tile=512):
    devices, _, rows, cols = shards.shape
    group = tile // rows

    def kernel(a_ref, w_ref, o_ref):
        w = w_ref[...].reshape(tile, cols)
        o_ref[...] = lax.dot_general(
            a_ref[...], w, (((1,), (1,)), ((), ())), preferred_element_type=F32
        )

    return pl.pallas_call(
        kernel,
        grid=(devices // group,),
        out_shape=jax.ShapeDtypeStruct((value.shape[0], devices * rows), F32),
        in_specs=[
            pl.BlockSpec(value.shape, lambda j: (0, 0)),
            pl.BlockSpec((group, 1, rows, cols), lambda j: (j, which, 0, 0)),
        ],
        out_specs=pl.BlockSpec((value.shape[0], tile), lambda j: (0, j)),
        compiler_params=pltpu.CompilerParams(vmem_limit_bytes=40 << 20),
        cost_estimate=pl.CostEstimate(
            flops=2 * value.size * devices * rows, transcendentals=0,
            bytes_accessed=2 * value.size + 2 * devices * rows * cols
            + 4 * value.shape[0] * devices * rows,
        ),
        name="stack_nt",
    )(value, shards)


def other_half(shards, which):
    core = lax.axis_index("core")
    devices, n, rows, cols = shards.shape
    quarter = cols // 4
    own = lax.dynamic_slice(
        shards, (0, n - 1, 0, (2 * which + core) * quarter), (devices, 1, rows, quarter)
    )
    return swap(own.reshape(devices, rows, quarter), "y")


def places():
    return jnp.stack([lax.axis_index("y"), lax.axis_index("core")]).astype(jnp.int32)


def half_nn(value, shards, which, got, near):
    devices, n, rows, cols = shards.shape
    tile = cols // 4

    def kernel(p_ref, a_ref, w_ref, g_ref, n_ref, o_ref):
        t = pl.program_id(0)

        def put(w):
            w = w.reshape(devices * rows, tile)
            o_ref[...] = jnp.dot(a_ref[...], w, preferred_element_type=F32)

        pl.when(t < 2)(lambda: put(w_ref[...]))
        pl.when(t == 2)(lambda: put(g_ref[...]))
        pl.when(t == 3)(lambda: put(n_ref[...]))

    def out_at(t, p):
        other = 2 * (1 - p[0]) + jnp.where(t == 2, p[1], 1 - p[1])
        return 0, jnp.where(t < 2, 2 * p[0] + t, other)

    whole = pl.BlockSpec(got.shape, lambda t, p: (0, 0, 0))
    return pl.pallas_call(
        kernel,
        grid_spec=pltpu.PrefetchScalarGridSpec(
            num_scalar_prefetch=1,
            grid=(4,),
            in_specs=[
                pl.BlockSpec(value.shape, lambda t, p: (0, 0)),
                pl.BlockSpec(
                    (devices, 1, rows, tile),
                    lambda t, p: (0, n - 1, 0, 2 * which + jnp.minimum(t, 1)),
                ),
                whole,
                whole,
            ],
            out_specs=pl.BlockSpec((value.shape[0], tile), out_at),
        ),
        out_shape=jax.ShapeDtypeStruct((value.shape[0], cols), F32),
        compiler_params=pltpu.CompilerParams(vmem_limit_bytes=48 << 20),
        cost_estimate=pl.CostEstimate(
            flops=2 * value.size * cols, transcendentals=0,
            bytes_accessed=2 * value.size + 2 * devices * rows * cols + 4 * value.shape[0] * cols,
        ),
        name="half_nn",
    )(places(), value, shards, got, near)


def half_nt(value, shards, which, got, near):
    devices, n, rows, cols = shards.shape
    wide = 512
    group = wide // rows
    tile = cols // 4
    tokens = value.shape[0]

    def kernel(p_ref, a_ref, b_ref, c_ref, w_ref, g_ref, n_ref, o_ref):
        total = nt(a_ref[...], w_ref[...].reshape(wide, 2 * tile))
        total = total + nt(b_ref[...], g_ref[...].reshape(wide, tile))
        o_ref[...] = total + nt(c_ref[...], n_ref[...].reshape(wide, tile))

    part = pl.BlockSpec((group, rows, tile), lambda j, p: (j, 0, 0))
    return pl.pallas_call(
        kernel,
        grid_spec=pltpu.PrefetchScalarGridSpec(
            num_scalar_prefetch=1,
            grid=(devices // group,),
            in_specs=[
                pl.BlockSpec((tokens, 2 * tile), lambda j, p: (0, p[0])),
                pl.BlockSpec((tokens, tile), lambda j, p: (0, 2 * (1 - p[0]) + p[1])),
                pl.BlockSpec((tokens, tile), lambda j, p: (0, 2 * (1 - p[0]) + 1 - p[1])),
                pl.BlockSpec((group, 1, rows, 2 * tile), lambda j, p: (j, n - 1, 0, which)),
                part,
                part,
            ],
            out_specs=pl.BlockSpec((tokens, wide), lambda j, p: (0, j)),
        ),
        out_shape=jax.ShapeDtypeStruct((tokens, devices * rows), F32),
        compiler_params=pltpu.CompilerParams(vmem_limit_bytes=40 << 20),
        cost_estimate=pl.CostEstimate(
            flops=2 * value.size * devices * rows, transcendentals=0,
            bytes_accessed=2 * value.size + 2 * devices * rows * cols + 4 * tokens * devices * rows,
        ),
        name="half_nt",
    )(places(), value, value, value, shards, got, near)


TILE = 256


def pack_blocks(shard):
    rows, cols = shard.shape
    return jnp.swapaxes(shard.reshape(rows, cols // TILE, TILE), 0, 1).reshape(-1, TILE)


def ffn_call(kernel, core, grid, ins, specs, outs, out_specs, flops, scratch=(), name=None):
    moved = sum(a.size * a.dtype.itemsize for a in ins[:1] + outs) + flops // 1024
    return pl.pallas_call(
        kernel,
        grid_spec=pltpu.PrefetchScalarGridSpec(
            num_scalar_prefetch=1, grid=grid, in_specs=specs, out_specs=out_specs, scratch_shapes=scratch
        ),
        out_shape=outs,
        compiler_params=pltpu.CompilerParams(vmem_limit_bytes=56 << 20),
        cost_estimate=pl.CostEstimate(flops=flops, transcendentals=0, bytes_accessed=moved),
        name=name,
    )(core.reshape(1), *ins)


class PackedWeights:
    def __init__(self, packed, core, ff, width, half, chips):
        self.packed, self.core = packed, core
        self.devices = packed.shape[0]
        self.rows = width // self.devices
        self.quarter, self.width, self.half, self.chips = ff // 4, width, half, chips
        self.blocks = self.quarter // TILE
        self.fast = half % 16 == 0 and self.rows % 16 == 0 and self.rows == 128

    def _plain(self, start, rows, count):
        part = self.packed[:, start : start + rows * count]
        return part.reshape(-1, count, rows, TILE)

    def plain_key(self):
        start = self.half * (self.width // TILE)
        part = self._plain(start, self.rows, 2 * self.blocks)
        part = piece(part, self.core, self.blocks, 1)
        return jnp.swapaxes(part, 1, 2).reshape(self.width, self.quarter)

    def plain_value(self):
        part = self._plain(0, self.half, self.width // TILE)
        part = lax.dynamic_index_in_dim(
            part.reshape(self.chips, 2, *part.shape[1:]), self.core, 1, False
        )
        return jnp.swapaxes(part, 1, 2).reshape(self.quarter, self.width)

    def plain_rec(self):
        start = self.half * (self.width // TILE) + self.rows * 2 * self.blocks
        part = self._plain(start, self.rows, self.width // TILE)
        return jnp.swapaxes(part, 1, 2).reshape(self.width, self.width)

    def key_forward(self, mix):
        if not self.fast:
            relu = low(jnp.maximum(nn(mix, self.plain_key()), 0.0))
            return relu, low(relu.astype(F32) * relu.astype(F32))
        tokens = mix.shape[0]
        first = self.half * (self.width // TILE) // self.rows

        def kernel(c_ref, a_ref, w_ref, relu_ref, sq_ref):
            w = w_ref[...].reshape(self.width, TILE)
            relu = jnp.maximum(jnp.dot(a_ref[...], w, preferred_element_type=F32), 0.0)
            relu_ref[...] = low(relu)
            sq_ref[...] = low(relu * relu)

        out = jax.ShapeDtypeStruct((tokens, self.quarter), BF16)
        spec = pl.BlockSpec((tokens, TILE), lambda n, c: (0, n))
        return ffn_call(
            kernel, self.core, (self.blocks,), [mix, self.packed],
            [pl.BlockSpec(mix.shape, lambda n, c: (0, 0)),
             pl.BlockSpec((self.devices, self.rows, TILE),
                          lambda n, c: (0, first + c[0] * self.blocks + n, 0))],
            [out, out], [spec, spec], 2 * mix.size * self.quarter, name="key_forward",
        )

    def value_forward(self, squared):
        if not self.fast:
            return low(nn(squared, self.plain_value()))
        tokens = squared.shape[0]
        view = self.packed.reshape(self.chips, 2, *self.packed.shape[1:])

        def kernel(c_ref, a_ref, w_ref, o_ref):
            w = w_ref[...].reshape(self.quarter, TILE)
            o_ref[...] = low(jnp.dot(a_ref[...], w, preferred_element_type=F32))

        return ffn_call(
            kernel, self.core, (self.width // TILE,), [squared, view],
            [pl.BlockSpec(squared.shape, lambda m, c: (0, 0)),
             pl.BlockSpec((self.chips, 1, self.half, TILE), lambda m, c: (0, c[0], m, 0))],
            [jax.ShapeDtypeStruct((tokens, self.width), BF16)],
            [pl.BlockSpec((tokens, TILE), lambda m, c: (0, m))],
            2 * squared.size * self.width, name="value_forward",
        )[0]

    def rec_forward(self, mix):
        if not self.fast:
            return jax.nn.sigmoid(nn(mix, self.plain_rec()))
        tokens = mix.shape[0]
        first = self.packed.shape[1] // self.rows - self.width // TILE

        def kernel(c_ref, a_ref, w_ref, o_ref):
            w = w_ref[...].reshape(self.width, TILE)
            o_ref[...] = jax.nn.sigmoid(jnp.dot(a_ref[...], w, preferred_element_type=F32))

        return ffn_call(
            kernel, self.core, (self.width // TILE,), [mix, self.packed],
            [pl.BlockSpec(mix.shape, lambda m, c: (0, 0)),
             pl.BlockSpec((self.devices, self.rows, TILE), lambda m, c: (0, first + m, 0))],
            [jax.ShapeDtypeStruct((tokens, self.width), F32)],
            [pl.BlockSpec((tokens, TILE), lambda m, c: (0, m))],
            2 * mix.size * self.width, name="rec_forward",
        )[0]

    def value_backward(self, grad, relu):
        if not self.fast:
            return low(nt(grad, self.plain_value()) * 2.0 * relu.astype(F32))
        tokens = grad.shape[0]
        view = self.packed.reshape(self.chips, 2, *self.packed.shape[1:])
        count = self.width // TILE
        part = self.chips // 2

        def kernel(c_ref, a_ref, r_ref, w_ref, o_ref, flat):
            w = w_ref[...].reshape(part, count, self.half, TILE)
            for m in range(count):
                flat[:, m * TILE : (m + 1) * TILE] = w[:, m].reshape(part * self.half, TILE)
            back = lax.dot_general(
                a_ref[...], flat[...], (((1,), (1,)), ((), ())), preferred_element_type=F32
            )
            o_ref[...] = low(back * 2.0 * r_ref[...].astype(F32))

        wide = part * self.half
        return ffn_call(
            kernel, self.core, (2,), [grad, relu, view],
            [pl.BlockSpec(grad.shape, lambda i, c: (0, 0)),
             pl.BlockSpec((tokens, wide), lambda i, c: (0, i)),
             pl.BlockSpec((part, 1, count * self.half, TILE), lambda i, c: (i, c[0], 0, 0))],
            [jax.ShapeDtypeStruct((tokens, self.quarter), BF16)],
            [pl.BlockSpec((tokens, wide), lambda i, c: (0, i))],
            2 * grad.size * self.quarter,
            scratch=(pltpu.VMEM((wide, self.width), BF16),), name="value_backward",
        )[0]

    def key_backward(self, grad):
        if not self.fast:
            return low(nt(grad, self.plain_key()))
        tokens = grad.shape[0]
        part = 4
        rows = self.blocks * self.rows
        first = self.half * (self.width // TILE) // rows

        def kernel(c_ref, a_ref, w_ref, o_ref, flat):
            w = w_ref[...].reshape(part, self.blocks, self.rows, TILE)
            for n in range(self.blocks):
                flat[:, n * TILE : (n + 1) * TILE] = w[:, n].reshape(part * self.rows, TILE)
            o_ref[...] = low(lax.dot_general(
                a_ref[...], flat[...], (((1,), (1,)), ((), ())), preferred_element_type=F32
            ))

        wide = part * self.rows
        return ffn_call(
            kernel, self.core, (self.devices // part,), [grad, self.packed],
            [pl.BlockSpec(grad.shape, lambda i, c: (0, 0)),
             pl.BlockSpec((part, rows, TILE), lambda i, c: (i, first + c[0], 0))],
            [jax.ShapeDtypeStruct((tokens, self.width), BF16)],
            [pl.BlockSpec((tokens, wide), lambda i, c: (0, i))],
            2 * grad.size * self.width,
            scratch=(pltpu.VMEM((wide, self.quarter), BF16),), name="key_backward",
        )[0]

    def rec_backward(self, grad):
        if not self.fast:
            return nt(grad, self.plain_rec())
        tokens = grad.shape[0]
        part, count = 4, self.width // TILE
        rows = count * self.rows // 2
        first = self.packed.shape[1] // rows - 2

        def kernel(c_ref, a_ref, w_ref, v_ref, o_ref, flat):
            for k, ref in enumerate((w_ref, v_ref)):
                w = ref[...].reshape(part, count // 2, self.rows, TILE)
                for n in range(count // 2):
                    m = k * (count // 2) + n
                    flat[:, m * TILE : (m + 1) * TILE] = w[:, n].reshape(part * self.rows, TILE)
            o_ref[...] = lax.dot_general(
                a_ref[...], flat[...], (((1,), (1,)), ((), ())), preferred_element_type=F32
            )

        wide = part * self.rows
        return ffn_call(
            kernel, self.core, (self.devices // part,), [grad, self.packed, self.packed],
            [pl.BlockSpec(grad.shape, lambda i, c: (0, 0)),
             pl.BlockSpec((part, rows, TILE), lambda i, c: (i, first, 0)),
             pl.BlockSpec((part, rows, TILE), lambda i, c: (i, first + 1, 0))],
            [jax.ShapeDtypeStruct((tokens, self.width), F32)],
            [pl.BlockSpec((tokens, wide), lambda i, c: (0, i))],
            2 * grad.size * self.width,
            scratch=(pltpu.VMEM((wide, self.width), BF16),), name="rec_backward",
        )[0]


def body(tokens, att_w, down_w, up_w, key_w, value_w, rec_w, vectors, out_grad):
    seqs, length, width = tokens.shape
    total = seqs * length
    y, core = lax.axis_index("y"), lax.axis_index("core")
    zs = lax.axis_size("z")
    ff = key_w.shape[1]
    share = value_w.shape[0]
    half = share // 2
    quarter = ff // 4

    def rows(v):
        return v.reshape(total, width)

    def columns(shard):
        gathered = lax.all_gather(shard, WIDE, axis=0)
        return jnp.swapaxes(gathered, 0, 1).reshape(shard.shape[0], width)

    cols = up_w.shape[0]
    up_vec = columns(jnp.concatenate([vectors, up_w], 0))
    vec, up = up_vec[:16].astype(F32), up_vec[16:]
    down_t = columns(down_w.T)
    halves = [piece(att_w[i], y, width // 2, 1) for i in (3, 4)]
    w_att = jnp.concatenate([att_w[:3], jnp.concatenate(halves, 1)[None]], 0)
    w_att = lax.all_gather(w_att, WIDE, axis=0)
    key_sh = key_w.reshape(-1, zs, 2, 2, 2, half)
    key_sh = lax.dynamic_index_in_dim(key_sh, y, 4, False)
    key_sh = key_sh.transpose(0, 3, 1, 2, 4).reshape(-1, 2 * quarter)
    packed = jnp.concatenate(
        [pack_blocks(piece(value_w, y, half, 0)), pack_blocks(key_sh), pack_blocks(rec_w)], 0
    )
    packed = lax.all_gather(packed, WIDE, axis=0)

    x = rows(tokens.astype(F32))
    normed, hat, rstd = norm_forward(x, vec[0], vec[1])
    delta = prior_of(normed, seqs) - normed
    mix_low = low(normed + delta * vec[2])
    tanh_mix = jnp.tanh(nt(mix_low, down_t[:MIXCOLS]))
    hidden = low(tanh_mix)
    hid = [hidden[:, i * RANK : (i + 1) * RANK] for i in range(5)]
    ups = [up[i * RANK : (i + 1) * RANK] for i in range(5)]
    mixed = [low(normed + delta * (vec[3 + i] + nn(hid[i], ups[i]))) for i in range(5)]
    decay_in, key_in, value_in, rec_in, gate_in = mixed
    tanh_decay = jnp.tanh(nt(decay_in, down_t[MIXCOLS:]))
    hidden_decay = low(tanh_decay)
    logdecay = -jnp.exp(vec[8] + nn(hidden_decay, up[MIXCOLS:]))
    mix_all = group_pieces([gate_in, rec_in, key_in, value_in])
    w_att, mix_all = tie(w_att, mix_all)
    gate_other = other_half(w_att, 0)
    out_other = other_half(w_att, 1)
    keys = stack_nn(key_in, w_att, 1)
    values = stack_nn(value_in, w_att, 2)
    shaped = jax.ShapeDtypeStruct
    flat, flat_low = shaped((total, width), F32), shaped((total, width), BF16)
    states = shaped((seqs, width // LANES, HEAD, LANES), BF16)
    finals = shaped((seqs, width // LANES, 16, LANES), BF16)
    sums = shaped((seqs, 8, width), F32)
    unit = 2 * total * width
    inclusive, state, final = wkv_call(
        state_kernel, seqs, [keys, values, logdecay], [flat, states, finals], "wkv_state", unit * 512
    )
    carried, gate_other = chain(state, final, False, gate_other)
    gate_other = (gate_other, swap(gate_other, "core"))
    carried, out_other = tie(carried, out_other)
    out_other = (out_other, swap(out_other, "core"))
    recept = stack_nn(rec_in, w_att, 0)
    gate_pre = half_nn(gate_in, w_att, 0, *gate_other)
    wkv, gated = wkv_call(
        wkv_kernel, seqs, [recept, keys, values, inclusive, carried, gate_pre, vec], [flat, flat_low],
        "wkv_forward", unit * 1536,
    )
    first_sum = x + half_nn(gated, w_att, 1, *out_other)

    normed_two, hat_two, rstd_two = norm_forward(first_sum, vec[12], vec[13])
    delta_two = prior_of(normed_two, seqs) - normed_two
    key_mix = low(normed_two + delta_two * vec[14])
    rec_mix = low(normed_two + delta_two * vec[15])
    key_all = group_many([key_mix])[0]
    gated_all = group_pieces([gated])
    packed, key_all, gated_all = tie(packed, key_all, gated_all)
    ffn = PackedWeights(packed, core, ff, width, half, 2 * zs)
    relu, squared = ffn.key_forward(key_all)
    value_out = group_sum(ffn.value_forward(squared))
    rec_gate = ffn.rec_forward(rec_mix)
    block_out = low(first_sum + rec_gate * value_out).reshape(tokens.shape)

    g = rows(out_grad.astype(F32))
    grad_value = low(g * rec_gate)
    grad_gate_in = low(g * value_out * rec_gate * (1.0 - rec_gate))
    value_all = group_many([grad_value])[0]
    value_part = low(tn(squared, value_all)).reshape(-1, half, width)
    value_part, value_all = tie(value_part, value_all)
    value_part = lax.psum_scatter(value_part, ("z", "x"), scatter_dimension=0, tiled=True)[0]
    grad_key_pre = ffn.value_backward(value_all, relu)
    g_key_mix = ffn.key_backward(grad_key_pre)
    grad_key_pre, g_key_mix = tie(grad_key_pre, g_key_mix)
    key_part = low(tn(key_all, grad_key_pre))
    key_part = lax.psum_scatter(key_part, ("z", "x"), scatter_dimension=0, tiled=True)
    g_key_mix = group_sum(g_key_mix)
    g_rec_mix = ffn.rec_backward(grad_gate_in)

    g_prior = prior_back(g_key_mix * vec[14] + g_rec_mix * vec[15], seqs)
    g_normed_two = g_key_mix * (1.0 - vec[14]) + g_rec_mix * (1.0 - vec[15]) + g_prior
    g_maa_key = jnp.sum(g_key_mix * delta_two, 0, keepdims=True)
    g_maa_rec = jnp.sum(g_rec_mix * delta_two, 0, keepdims=True)
    back_two, g_gain_two, g_bias_two = norm_backward(g_normed_two, hat_two, rstd_two, vec[12])
    grad_first = g + back_two

    grad_att = low(grad_first)
    g_wkv, g_gate_low, g_state, gate_sums = wkv_call(
        gate_back_kernel, seqs,
        [half_nt(grad_att, w_att, 1, *out_other), wkv, gate_pre, recept, inclusive, vec],
        [flat_low, flat_low, states, sums], "gate_backward", unit * 1536,
    )
    g_state_out, (rights, rec_low) = chain(
        g_state, final, True, ([grad_gate_in, grad_att, g_gate_low], rec_mix)
    )
    side_near, side_across = half_cols(jnp.stack(rights, 0))
    rec_low = rec_low[None]
    rec_near, rec_across = swap(rec_low, "core"), swap(rec_low, "y")
    g_state_out, value_part = tie(g_state_out, value_part)
    g_rec, g_key, g_val, g_decay_low, wkv_sums = wkv_call(
        wkv_back_kernel, seqs,
        [recept, keys, values, inclusive, logdecay, carried, g_state_out, g_wkv, vec],
        [flat_low, flat_low, flat_low, flat_low, sums], "wkv_backward", unit * 4096,
        scratch=[pltpu.VMEM((length, SPAN), F32)] * 3,
    )
    gate_sums, wkv_sums = jnp.sum(gate_sums, 0), jnp.sum(wkv_sums, 0)
    projs = [g_rec, g_key, g_val, g_gate_low]
    main_near, main_across = half_cols(jnp.stack([g_rec, g_key, g_val], 0))
    main_near, side_across, rec_across = tie(main_near, side_across, rec_across)
    rec_all = (rec_low, rec_near, rec_across, swap(rec_across, "core"))
    side_lefts = [(rec_all, 0, 1), (gated_all, 0, 1), (mix_all, 0, 1)]
    side_right, g_rec, g_key = tie(quarter_cols(side_near, side_across), g_rec, g_key)
    side_give = x_rows(side_lefts, side_right, False)
    side_got = swap(side_give, "x")
    main_across, side_give = tie(main_across, side_give)
    main = all_rows([(mix_all, 1, 3)], quarter_cols(main_near, main_across))
    main, key_part, side_right, g_val, g_gate_low, g_decay_low = tie(
        main, key_part, side_right, g_val, g_gate_low, g_decay_low
    )
    side_keep = x_rows(side_lefts, side_right, True)
    main = lax.psum_scatter(main, ("z", "x"), scatter_dimension=0, tiled=True)
    projs = [g_rec, g_key, g_val, g_gate_low]

    decay_up_grad = tn(hidden_decay, g_decay_low)
    g_pre_decay = low(nt(g_decay_low, up[MIXCOLS:]) * (1.0 - tanh_decay * tanh_decay))
    decay_down_grad = tn(g_pre_decay, decay_in)
    g_mixed = [
        nn(g_pre_decay, down_t[MIXCOLS:]),
        stack_nt(projs[1], w_att, 1),
        stack_nt(projs[2], w_att, 2),
        stack_nt(projs[0], w_att, 0),
        half_nt(projs[3], w_att, 0, *gate_other),
    ]
    g_normed = g_prior_sum = None
    maa_rows, up_grads, hid_grads = [], [], []
    for i in range(5):
        offset = vec[3 + i] + nn(hid[i], ups[i])
        g_off = g_mixed[i] * delta
        maa_rows.append(jnp.sum(g_off, 0, keepdims=True))
        off_low = low(g_off)
        up_grads.append(tn(hid[i], off_low))
        hid_grads.append(nt(off_low, ups[i]))
        here = g_mixed[i] * (1.0 - offset)
        back = g_mixed[i] * offset
        g_normed = here if g_normed is None else g_normed + here
        g_prior_sum = back if g_prior_sum is None else g_prior_sum + back
    g_pre_mix = low(jnp.concatenate(hid_grads, 1) * (1.0 - tanh_mix * tanh_mix))
    mix_down_grad = tn(g_pre_mix, mix_low)
    g_first_mix = nn(g_pre_mix, down_t[:MIXCOLS])
    maa_first = jnp.sum(g_first_mix * delta, 0, keepdims=True)
    g_prior_sum = g_prior_sum + g_first_mix * vec[2]
    g_normed = g_normed + g_first_mix * (1.0 - vec[2]) + prior_back(g_prior_sum, seqs)
    g_normed, side_got = tie(g_normed, side_got)
    side = low(side_keep.astype(F32) + side_got.astype(F32))
    side = side.reshape(zs, -1, side.shape[1])
    moving = line_step(side, 1, None)
    g_gain = jnp.sum(g_normed * hat, 0, keepdims=True)
    g_bias = jnp.sum(g_normed, 0, keepdims=True)

    vec_rows = (
        [g_gain, g_bias, maa_first] + maa_rows
        + [wkv_sums[1:2], wkv_sums[0:1], gate_sums[0:1], gate_sums[1:2], g_gain_two, g_bias_two,
           g_maa_key, g_maa_rec]
    )
    packed = pack_columns(up_grads + [decay_up_grad, mix_down_grad, decay_down_grad] + vec_rows)
    packed, moving, value_part, key_part = tie(packed, moving, value_part, key_part)
    for t in range(2, zs - 1):
        moving = line_step(side, t, moving)
    first = y == 0
    other = swap(value_part, "y")
    value_share = jnp.concatenate(
        [jnp.where(first, value_part, other), jnp.where(first, other, value_part)], 0
    ).astype(F32)
    key_share = spread_cols(key_part[:, None])[0].reshape(-1, 2, 2, zs, 2, half)
    key_share = key_share.transpose(0, 3, 4, 2, 1, 5).reshape(-1, ff)
    packed, moving, value_share, main, g_normed = tie(packed, moving, value_share, main, g_normed)
    late = spread_cols(main.reshape(main.shape[0], 3, -1))
    moving = line_step(side, zs - 1, moving)
    back_one, _, _ = norm_backward(g_normed, hat, rstd, vec[0])
    input_grad = (grad_first + back_one).reshape(tokens.shape)
    packed = small_cross(small_core(packed))
    packed, moving, key_share, late = tie(packed, moving, key_share, late)
    side = low(line_end(side, moving))
    early = spread_cols(side.reshape(side.shape[0], 3, -1))
    packed = small_sum(packed)
    rec_share = early[0]
    att_share = jnp.stack(late + [early[2], early[1]], 0)
    return (
        block_out, input_grad, att_share, packed[cols : 2 * cols].T, packed[:cols],
        key_share, value_share, rec_share, packed[2 * cols :],
    )


def solution(mesh):
    seq, wide = mesh.devices.shape
    fine = Mesh(mesh.devices.reshape(seq, wide // 4, 2, 2), ALL)
    token = P(None, ALL, None)
    by_row, by_col, stacked = P(WIDE, None), P(None, WIDE), P(None, WIDE, None)
    return jax.shard_map(
        body,
        mesh=fine,
        in_specs=(token, stacked, by_row, by_col, by_row, by_row, by_row, by_col, token),
        out_specs=(token, token, stacked, by_row, by_col, by_row, by_row, by_row, by_col),
        check_vma=False,
    )
```
